128 devices in a mesh: dp: 8 (over x_lo, y), ctx: 16 (over x_hi, z, core).
Axes of the slice: x: 4 (x_hi: 2, x_lo: 2; x = x_hi * 2 + x_lo), y: 4, z: 4, core: 2. Of those that a mesh axis runs over, the one named last changes fastest.
Arguments:
- latent_q: bfloat16 [8, 4096, 1280], P('dp', 'ctx'), may hold values from -7 to 7
- latent_k: bfloat16 [8, 4096, 1280], P('dp', 'ctx'), may hold values from -7 to 7
- latent_v: bfloat16 [8, 4096, 1280], P('dp', 'ctx'), may hold values from -30 to 30
- caption_states: bfloat16 [8, 256, 4096], P('dp', None, 'ctx'), may hold values from -6 to 6
- caption_proj: bfloat16 [4096, 2560], P('ctx'), may hold values from -0.09375 to 0.09375
- caption_len: int32 [8], P('dp'), may hold values from 1 to 256, as said below
- timestep: int32 [8], P('dp'), may hold values from 0 to 999
- out_cot: bfloat16 [8, 4096, 2432], P('dp', 'ctx'), may hold values from -6 to 6
- out_weight: bfloat16 [1280, 2432], P('ctx'), may hold values from -0.15625 to 0.15625
- mom_val: bfloat16 [1280, 2432], P('ctx'), may hold values from -1 to 1
- mom_scale: float32 [1280, 19], P('ctx'), may hold values from 0.005 to 0.5
- var_val: bfloat16 [1280, 2432], P('ctx'), may hold values from 0.049804688 to 1
- var_scale: float32 [1280, 19], P('ctx'), may hold values from 1e-05 to 0.001
Outputs:
- attn_out: bfloat16 [8, 4096, 1280], P('dp', 'ctx')
- new_weight: bfloat16 [1280, 2432], P('ctx')
- new_mom_val: bfloat16 [1280, 2432], P('ctx')
- new_mom_scale: float32 [1280, 19], P('ctx')
- new_var_val: bfloat16 [1280, 2432], P('ctx')
- new_var_scale: float32 [1280, 19], P('ctx')
The draws below stay inside these ranges and needn't reach their ends.
Inputs may be any that keep to these rules, and one draw needn't show every extreme that they name: `caption_len`: at least one sample has a caption of all 256 tokens.
All inputs are finite; a program needn't handle non-finite values.
Results may differ from the reference program's by a relative error of at most 0.022.
Values may be sent and summed in bfloat16 or wider, within the bound.
No kernel may reach another device: no remote copies, remote signals or barrier semaphores. Data moves between devices by JAX's collectives and lax.ppermute only.
A program may use at most 128 MiB of HBM per device.

```python
import math
import jax
import jax.numpy as jnp
from jax import lax

D = 2432
HD = 64
HEADS = 20
TDIM = 4096
CAP = 256
QBLOCK = 128
INNER = 1280
SEQ = 4096
BATCH = 8


def column_ramp(top):
    columns = jnp.arange(INNER).astype(jnp.float32)
    return 1.0 + (top - 1.0) * columns / (INNER - 1)


def draw_latent_q(key, part):
    key = jax.random.fold_in(key, 1)
    return jnp.clip(jax.random.normal(key, (BATCH, SEQ, INNER), jnp.float32), -6.0, 6.0).astype(jnp.bfloat16)


def draw_latent_k(key, part):
    key = jax.random.fold_in(key, 2)
    return jnp.clip(jax.random.normal(key, (BATCH, SEQ, INNER), jnp.float32), -6.0, 6.0).astype(jnp.bfloat16)


def draw_latent_v(key, part):
    key = jax.random.fold_in(key, 4)
    base = jnp.clip(jax.random.normal(key, (BATCH, SEQ, INNER), jnp.float32), -6.0, 6.0)
    return (base * column_ramp(3.0)[None, None, :]).astype(jnp.bfloat16)


def draw_caption_len(key, part):
    key = jax.random.fold_in(key, 3)
    lengths = jax.random.randint(jax.random.fold_in(key, 1), (BATCH,), 1, CAP + 1)
    chosen = jax.random.randint(jax.random.fold_in(key, 2), (), 0, BATCH)
    return jnp.where(jnp.arange(BATCH) == chosen, CAP, lengths).astype(jnp.int32)


def with_ends(result, own_key, low, high):
    longest = result.shape.index(max(result.shape))
    spots = []
    for shift in (0, 1):
        where = [jax.random.randint(jax.random.fold_in(own_key, axis), (), 0, length) for axis, length in enumerate(result.shape)]
        where[longest] = (where[longest] + shift) % result.shape[longest]
        spots.append(tuple(where))
    return result.at[spots[0]].set(low).at[spots[1]].set(high)


def shard_levels(stream_key, extent, pieces, smallest, largest):
    def one(position, parts):
        heights = jax.random.uniform(jax.random.fold_in(jax.random.fold_in(stream_key, 6), position), (parts,), jnp.float32, smallest / len(pieces), largest / len(pieces))
        return jnp.repeat(jnp.exp(heights), extent[position] // parts).reshape((-1,) + (1,) * (len(extent) - position - 1))

    loudness = one(*pieces[0])
    for cut in pieces[1:]:
        loudness = loudness * one(*cut)
    return loudness


def gaussian(key, extent, width, most, pieces=(), kind=jnp.bfloat16):
    level = shard_levels(key, extent, pieces, -0.22, 0.18) if pieces else 1.0
    values = jax.random.normal(key, extent, jnp.float32) * width * level
    return jnp.minimum(jnp.maximum(values, -most), most).astype(kind)


def setup_inputs(seed: int = 0) -> dict:
    arg_keys = jax.random.split(jax.random.key(seed), 14)
    latent_q = draw_latent_q(jax.random.fold_in(arg_keys[13], 71), 0)
    latent_k = draw_latent_k(jax.random.fold_in(arg_keys[13], 71), 0)
    latent_v = draw_latent_v(jax.random.fold_in(arg_keys[13], 71), 0)
    caption_states = gaussian(arg_keys[3], (BATCH, CAP, TDIM), 1.0, 6.0, ((0, 8), (2, 16)))
    caption_proj = gaussian(arg_keys[4], (TDIM, 2 * INNER), TDIM ** -0.5, 0.09375, ((0, 16),))
    caption_len = draw_caption_len(jax.random.fold_in(arg_keys[13], 71), 0)
    timestep = with_ends(jax.random.randint(arg_keys[6], (BATCH,), 0, 1000), jax.random.fold_in(arg_keys[6], 1), 0, 999).astype(jnp.int32)
    out_cot = gaussian(arg_keys[7], (BATCH, SEQ, D), 1.0, 6.0, ((0, 8), (1, 16)))
    out_weight = gaussian(arg_keys[8], (INNER, D), INNER ** -0.5, 0.15625, ((0, 16),))
    mom_val = jnp.clip(jax.random.uniform(arg_keys[9], (INNER, D), jnp.float32, -1.0, 1.0) * shard_levels(arg_keys[9], (INNER, D), ((0, 16),), -0.4, 0.0), -1.0, 1.0).astype(jnp.bfloat16)
    mom_scale = jnp.clip(jnp.exp(math.log(0.5) - 4.6051702 * jax.random.uniform(arg_keys[10], (INNER, D // QBLOCK), jnp.float32) ** shard_levels(arg_keys[10], (INNER, D // QBLOCK), ((0, 16),), -0.2, 0.2)), 0.005, 0.5)
    var_val = jnp.clip(0.049804688 + 0.9501953 * jax.random.uniform(arg_keys[11], (INNER, D), jnp.float32) ** shard_levels(arg_keys[11], (INNER, D), ((0, 16),), -0.2, 0.2), 0.049804688, 1.0).astype(jnp.bfloat16)
    var_scale = jnp.clip(jnp.exp(math.log(0.001) - 4.6051703 * jax.random.uniform(arg_keys[12], (INNER, D // QBLOCK), jnp.float32) ** shard_levels(arg_keys[12], (INNER, D // QBLOCK), ((0, 16),), -0.2, 0.2)), 9.999999747378752e-06, 0.001)
    return dict(latent_q=latent_q, latent_k=latent_k, latent_v=latent_v, caption_states=caption_states, caption_proj=caption_proj, caption_len=caption_len, timestep=timestep, out_cot=out_cot, out_weight=out_weight, mom_val=mom_val, mom_scale=mom_scale, var_val=var_val, var_scale=var_scale)


def expand_blocks(scale):
    return jnp.repeat(scale, QBLOCK, axis=1)

def block_scale(values):
    rows = values.shape[0]
    return lax.optimization_barrier(jnp.max(jnp.abs(values).reshape(rows, -1, QBLOCK), axis=2)) + 1e-06

def adam_rows(grad_rows, factor, out_weight, mom_val, mom_scale, var_val, var_scale):
    step_grad = grad_rows * factor
    first = mom_val.astype(jnp.float32) * expand_blocks(mom_scale)
    second = var_val.astype(jnp.float32) * expand_blocks(var_scale)
    first = 0.9 * first + 0.1 * step_grad
    second = 0.999 * second + 0.001 * step_grad * step_grad
    update = first / (1.0 - 0.9 ** 10) / (jnp.sqrt(second / (1.0 - 0.999 ** 10)) + 1e-08)
    new_weight = (out_weight.astype(jnp.float32) - 0.02 * update).astype(jnp.bfloat16)
    first_scale = block_scale(first)
    second_scale = block_scale(second)
    first_val = (first / expand_blocks(first_scale)).astype(jnp.bfloat16)
    second_val = (second / expand_blocks(second_scale)).astype(jnp.bfloat16)
    return (new_weight, first_val, first_scale, second_val, second_scale)

def reference(latent_q, latent_k, latent_v, caption_states, caption_proj, caption_len, timestep, out_cot, out_weight, mom_val, mom_scale, var_val, var_scale):

    def project(states):
        return jnp.dot(states, caption_proj, preferred_element_type=jnp.float32).astype(jnp.bfloat16)
    caption_kv = lax.map(project, caption_states)
    qblock = math.gcd(SEQ, 512)
    scale = 1.0 / math.sqrt(HD)

    def attend(items):
        queries, keys, values, cap_kv, length = items
        all_keys = jnp.concatenate([keys, cap_kv[:, :INNER]], axis=0).astype(jnp.float32).reshape(-1, HEADS, HD)
        all_vals = jnp.concatenate([values, cap_kv[:, INNER:]], axis=0).astype(jnp.float32).reshape(-1, HEADS, HD)
        valid = jnp.concatenate([jnp.ones((SEQ,), bool), jnp.arange(CAP) < length])
        blocks = queries.astype(jnp.float32).reshape(SEQ // qblock, qblock, HEADS, HD)

        def one_block(block):
            scores = jnp.einsum('qhd,khd->hqk', block, all_keys) * scale
            scores = jnp.where(valid[None, None, :], scores, -1e+30)
            peak = lax.optimization_barrier(jnp.max(scores, axis=-1))
            probs = jnp.exp(scores - peak[..., None])
            total = lax.optimization_barrier(jnp.sum(probs, axis=-1))
            rounded = lax.optimization_barrier(probs.astype(jnp.bfloat16)).astype(jnp.float32)
            mixed = jnp.einsum('hqk,khd->hqd', rounded, all_vals) / total[..., None]
            return mixed.transpose(1, 0, 2).reshape(qblock, INNER)
        return lax.map(one_block, blocks).reshape(SEQ, INNER).astype(jnp.bfloat16)
    attn_out = lax.map(attend, (latent_q, latent_k, latent_v, caption_kv, caption_len))
    loss_weight = 1.0 + 3.0 * (timestep.astype(jnp.float32) + 0.5) / 1000.0

    def add_sample(total, items):
        outputs, cot, weight = items
        term = lax.dot_general(outputs, cot, (((0,), (0,)), ((), ())), preferred_element_type=jnp.float32)
        return (total + weight * term, None)
    grad, _ = lax.scan(add_sample, jnp.zeros((INNER, D), jnp.float32), (attn_out, out_cot, loss_weight))
    gnorm = jnp.sqrt(jnp.sum(grad * grad) + 1e-06)
    factor = 256.0 / gnorm
    new_weight, first_val, first_scale, second_val, second_scale = adam_rows(grad, factor, out_weight, mom_val, mom_scale, var_val, var_scale)
    return (attn_out, new_weight, first_val, first_scale, second_val, second_scale)
```

```python
import functools
import math

import jax
import jax.numpy as jnp
from jax import lax
from jax.experimental import pallas as pl
from jax.experimental.pallas import tpu as pltpu
from jax.sharding import Mesh, PartitionSpec as P

HD = 64
LANES = 128
ONES = 16
LOG2E = math.log2(math.e)
SAFE_BOUND = 60.0
F32 = jnp.float32
BF16 = jnp.bfloat16
NT = 4
VMEM_LIMIT = 56 * 2**20


def head_norms(x, heads):
    x = x.astype(F32)
    x = x * x
    rows = [jnp.sum(x[h * HD : (h + 1) * HD], axis=0, keepdims=True) for h in range(heads)]
    return jnp.max(jnp.concatenate(rows, axis=0), axis=1, keepdims=True)


def attention_kernel(len_ref, *refs, tiles, blocks, block_q, block_k):
    q_refs, refs = refs[:tiles], refs[tiles:]
    kv_refs, refs = refs[:blocks], refs[blocks:]
    ck_ref, cv_ref, o_ref, keys, vals = refs
    inner, tok = q_refs[0].shape
    heads = inner // HD
    cap = ck_ref.shape[1]
    total = keys.shape[1]
    length = len_ref[0]

    def place(col, k, v, kept):
        n = k.shape[1]
        for h in range(heads):
            keys[h, col : col + n, :] = k[h * HD : (h + 1) * HD].T
            vh = v[h * HD : (h + 1) * HD]
            one = jnp.ones((ONES, n), BF16)
            if kept is not None:
                vh = jnp.where(kept, vh, BF16(0))
                one = jnp.where(kept, one, BF16(0))
            vals[h, 0:HD, col : col + n] = vh
            vals[h, HD : HD + ONES, col : col + n] = one

    kmax = head_norms(ck_ref[...], heads)
    for b, ref in enumerate(kv_refs):
        k = ref[0:inner, :]
        place(b * tok, k, ref[inner : 2 * inner, :], None)
        kmax = jnp.maximum(kmax, head_norms(k, heads))
    kept = lax.broadcasted_iota(jnp.int32, (1, cap), 1) < length
    place(blocks * tok, ck_ref[...], cv_ref[...], kept)
    qmax = head_norms(q_refs[0][...], heads)
    for ref in q_refs[1:]:
        qmax = jnp.maximum(qmax, head_norms(ref[...], heads))
    small = jnp.max(qmax * kmax) < HD * SAFE_BOUND * SAFE_BOUND

    per = block_q // tok

    def block(h, first, safe):
        rows = pl.ds(pl.multiple_of(h * HD, HD), HD)
        qt = jnp.concatenate([q_refs[first + b][rows, :] for b in range(per)], axis=1)
        qt = qt * BF16(0.125)
        if safe:
            n = tok

            def score(c):
                start = pl.multiple_of(c * n, n)
                s = jnp.dot(keys[h, pl.ds(start, n), :], qt, preferred_element_type=F32)
                key = lax.broadcasted_iota(jnp.int32, (n, 1), 0) + start
                return jnp.where(key < total - cap + length, s, -1e30)

            def peak(c, m):
                return jnp.maximum(m, jnp.max(score(c), axis=0, keepdims=True))

            m = lax.fori_loop(0, total // n, peak, jnp.full((1, block_q), -1e30, F32))

            def step(c, acc):
                p = jnp.exp2((score(c) - m) * LOG2E).astype(BF16)
                v = vals[h, :, pl.ds(pl.multiple_of(c * n, n), n)]
                return acc + jnp.dot(v, p, preferred_element_type=F32)

            acc = lax.fori_loop(0, total // n, step, jnp.zeros((HD + ONES, block_q), F32))
        else:
            acc = None
            for c in range(0, total, block_k):
                n = min(block_k, total - c)
                s = jnp.dot(keys[h, c : c + n, :], qt, preferred_element_type=F32)
                p = jnp.exp2(s * LOG2E).astype(BF16)
                t = jnp.dot(vals[h, :, c : c + n], p, preferred_element_type=F32)
                acc = t if acc is None else acc + t
        out = (acc[0:HD] / acc[HD : HD + 1]).astype(BF16)
        for b in range(per):
            o_ref[first + b, rows, :] = out[:, b * tok : (b + 1) * tok]

    def run(safe):
        for first in range(0, tiles, per):
            lax.fori_loop(0, heads, lambda h, _: (block(h, first, safe), 0)[1], 0)

    @pl.when(small)
    def _():
        run(False)

    @pl.when(jnp.logical_not(small))
    def _():
        run(True)


def attention(length, queries, kvs, ck, cv, block_q=512, block_k=2176):
    inner, tok = queries[0].shape
    heads = inner // HD
    tiles = len(queries)
    blocks = len(kvs)
    total = blocks * tok + ck.shape[1]
    vm = pl.BlockSpec(memory_space=pltpu.VMEM)
    return pl.pallas_call(
        functools.partial(
            attention_kernel, tiles=tiles, blocks=blocks, block_q=block_q, block_k=block_k
        ),
        out_shape=jax.ShapeDtypeStruct((tiles, inner, tok), BF16),
        in_specs=[pl.BlockSpec(memory_space=pltpu.SMEM)] + [vm] * (tiles + blocks + 2),
        out_specs=vm,
        scratch_shapes=[
            pltpu.VMEM((heads, total, HD), BF16),
            pltpu.VMEM((heads, HD + ONES, total), BF16),
        ],
        cost_estimate=pl.CostEstimate(
            flops=16 * tiles * tok * total * inner,
            transcendentals=tiles * tok * total * heads,
            bytes_accessed=2 * inner * (2 * total + 2 * tiles * tok),
        ),
        compiler_params=pltpu.CompilerParams(vmem_limit_bytes=VMEM_LIMIT),
        name="attention",
    )(length, *queries, *kvs, ck, cv)


def grad_kernel(w_ref, o_ref, *refs, part):
    cot_refs, g_ref = refs[:-1], refs[-1]
    tiles = len(cot_refs)
    width = cot_refs[0].shape[1]
    left = jnp.concatenate([o_ref[b] for b in range(tiles)], axis=1)
    weight = w_ref[0]
    step = 2 * LANES
    for c in range(0, width, step):
        n = min(step, width - c)
        right = jnp.concatenate([ref[:, c : c + n] for ref in cot_refs], axis=0)
        g = (jnp.dot(left, right, preferred_element_type=F32) * weight).astype(BF16)
        for t in range(n // LANES):
            for j in range(left.shape[0] // part):
                g_ref[j % 2, j // 2, c // LANES + t] = g[
                    j * part : (j + 1) * part, t * LANES : (t + 1) * LANES
                ]


def local_grad(weight, attended, cots, part):
    tiles, inner, tok = attended.shape
    width = cots[0].shape[1]
    vm = pl.BlockSpec(memory_space=pltpu.VMEM)
    return pl.pallas_call(
        functools.partial(grad_kernel, part=part),
        out_shape=jax.ShapeDtypeStruct((2, inner // (2 * part), width // LANES, part, LANES), BF16),
        in_specs=[pl.BlockSpec(memory_space=pltpu.SMEM)] + [vm] * (1 + len(cots)),
        out_specs=vm,
        cost_estimate=pl.CostEstimate(
            flops=2 * tiles * tok * inner * width,
            transcendentals=0,
            bytes_accessed=2 * (tiles * tok * (inner + width) + inner * width),
        ),
        compiler_params=pltpu.CompilerParams(vmem_limit_bytes=VMEM_LIMIT),
        name="local_grad",
    )(weight, attended, *cots)


def adam_kernel(f_ref, g_ref, w_ref, mv_ref, ms_ref, vv_ref, vs_ref, nw, nmv, nms, nvv, nvs):
    rows, width = w_ref.shape
    factor = f_ref[0]
    for t in range(width // LANES):
        cols = slice(t * LANES, (t + 1) * LANES)
        one = slice(t, t + 1)
        g = g_ref[t * rows : (t + 1) * rows, :].astype(F32) * factor
        first = mv_ref[:, cols].astype(F32) * ms_ref[:, one]
        second = vv_ref[:, cols].astype(F32) * vs_ref[:, one]
        first = 0.9 * first + 0.1 * g
        second = 0.999 * second + 0.001 * g * g
        update = first / (1.0 - 0.9**10) / (jnp.sqrt(second / (1.0 - 0.999**10)) + 1e-08)
        nw[:, cols] = (w_ref[:, cols].astype(F32) - 0.02 * update).astype(BF16)
        fs = jnp.max(jnp.abs(first), axis=1, keepdims=True) + 1e-06
        ss = jnp.max(jnp.abs(second), axis=1, keepdims=True) + 1e-06
        nms[:, one] = fs
        nvs[:, one] = ss
        nmv[:, cols] = (first / fs).astype(BF16)
        nvv[:, cols] = (second / ss).astype(BF16)


def adam(factor, grad, out_weight, mom_val, mom_scale, var_val, var_scale):
    vm = pl.BlockSpec(memory_space=pltpu.VMEM)
    like = lambda a: jax.ShapeDtypeStruct(a.shape, a.dtype)
    return pl.pallas_call(
        adam_kernel,
        out_shape=(like(out_weight), like(mom_val), like(mom_scale), like(var_val), like(var_scale)),
        in_specs=[pl.BlockSpec(memory_space=pltpu.SMEM)] + [vm] * 6,
        out_specs=(vm,) * 5,
        compiler_params=pltpu.CompilerParams(vmem_limit_bytes=VMEM_LIMIT),
        name="adam",
    )(factor, grad, out_weight, mom_val, mom_scale, var_val, var_scale)


def swap(x, axis):
    return lax.ppermute(x, axis, [(0, 1), (1, 0)])


def shift(x, k):
    return lax.ppermute(x, "z", [(i, (i + k) % NT) for i in range(NT)])


def pick(x, i):
    return lax.dynamic_index_in_dim(x, i, 0, keepdims=False)


def body(
    latent_q,
    latent_k,
    latent_v,
    caption_states,
    caption_proj,
    caption_len,
    timestep,
    out_cot,
    out_weight,
    mom_val,
    mom_scale,
    var_val,
    var_scale,
):
    tok, inner = latent_q.shape[1:]
    group = inner // NT
    cap = caption_states.shape[1]
    xh, z, c = lax.axis_index("xh"), lax.axis_index("z"), lax.axis_index("c")

    kv = jnp.concatenate(
        [latent_k[0].T.reshape(NT, group, tok), latent_v[0].T.reshape(NT, group, tok)], axis=1
    )
    own = [pick(kv, (z + k) % NT) for k in range(NT)]
    own = [own[0]] + [shift(own[k], k) for k in range(1, NT)]
    qt = latent_q[0].T.reshape(NT, group, tok)
    queries = [pick(qt, (z + k) % NT) for k in range(NT)]
    queries = [queries[0]] + [shift(queries[k], k) for k in range(1, NT)]

    partial = lax.dot_general(
        caption_proj, caption_states[0], (((0,), (1,)), ((), ())), preferred_element_type=F32
    ).astype(BF16)
    pieces = partial.reshape(4 * NT, 2 * inner // (4 * NT), cap)
    pieces = lax.all_to_all(pieces, ("xh", "z", "c"), 0, 0, tiled=True)
    cap_own = jnp.sum(pieces.astype(F32), axis=0).astype(BF16)
    cap_far = swap(cap_own, "xh")

    def both(x):
        y = swap(x, "c")
        return jnp.concatenate([jnp.where(c == 0, x, y), jnp.where(c == 0, y, x)], axis=0)

    cap_own, cap_far = both(cap_own), both(cap_far)
    cap_k = jnp.where(xh == 0, cap_own, cap_far)
    cap_v = jnp.where(xh == 0, cap_far, cap_own)

    far = [swap(x, "xh") for x in own]
    kvs = own + [swap(x, "c") for x in own] + far + [swap(x, "c") for x in far]

    cot = lax.optimization_barrier((out_cot[0], own[1], own[2], own[3]))[0]
    cots = [cot] + [shift(cot, k) for k in range(1, NT)]

    attended = attention(caption_len, queries, kvs, cap_k, cap_v)

    back = jnp.stack([attended[0]] + [shift(attended[k], -k) for k in range(1, NT)])
    back = lax.dynamic_slice_in_dim(jnp.concatenate([back, back]), (NT - z) % NT, NT, 0)
    attn_out = back.reshape(inner, tok).T[None]

    loss_weight = 1.0 + 3.0 * (timestep.astype(F32) + 0.5) / 1000.0
    rows = out_weight.shape[0]
    width = out_cot.shape[2]
    grad = local_grad(loss_weight, attended, cots, rows)
    other = swap(pick(grad, 1 - c), "c")
    grad = (pick(grad, c).astype(F32) + other.astype(F32)).astype(BF16)
    parts = []
    for t in range(2):
        perm = [
            (s * NT + i, (i // 2) * NT + 2 * (i % 2) + (s ^ t)) for s in range(2) for i in range(NT)
        ]
        piece = pick(grad, xh if t == 0 else 1 - xh)
        parts.append(lax.ppermute(piece, ("xh", "z"), perm))
    grad = (parts[0].astype(F32) + parts[1].astype(F32)).astype(BF16)
    flat = rows * width // LANES
    dp = lax.axis_size("xl") * lax.axis_size("y")
    chunk = -(-flat // (dp * 16)) * 16
    grad = jnp.pad(grad.reshape(flat, LANES), ((0, dp * chunk - flat), (0, 0)))
    grad = lax.all_to_all(grad.reshape(dp, chunk, LANES), ("xl", "y"), 0, 0, tiled=True)
    grad = jnp.sum(grad.astype(F32), axis=0).astype(BF16)
    grad = jnp.broadcast_to(grad[None], (dp, chunk, LANES))
    grad = lax.all_to_all(grad, ("xl", "y"), 0, 0, tiled=True).reshape(dp * chunk, LANES)
    square = jnp.sum(jnp.square(grad.astype(F32)))
    squares = lax.all_to_all(
        jnp.broadcast_to(square, (4 * NT, 8, LANES)), ("xh", "z", "c"), 0, 0, tiled=True
    )
    factor = 256.0 / jnp.sqrt(jnp.sum(squares[:, 0, 0]) + 1e-06)
    updated = adam(factor[None], grad, out_weight, mom_val, mom_scale, var_val, var_scale)
    return (attn_out, *updated)


def solution(mesh):
    fine = Mesh(mesh.devices.reshape(2, 4, 2, NT, 2), ("xl", "y", "xh", "z", "c"))
    dp = ("xl", "y")
    ctx = ("xh", "z", "c")
    tokens = P(dp, ctx, None)
    rows = P(ctx, None)
    return jax.shard_map(
        body,
        mesh=fine,
        in_specs=(
            tokens,
            tokens,
            tokens,
            P(dp, None, ctx),
            rows,
            P(dp),
            P(dp),
            tokens,
            rows,
            rows,
            rows,
            rows,
            rows,
        ),
        out_specs=(tokens, rows, rows, rows, rows, rows),
        check_vma=False,
    )
```

```python
import functools
import math

import jax
import jax.numpy as jnp
from jax import lax
from jax.experimental import pallas as pl
from jax.experimental.pallas import tpu as pltpu
from jax.sharding import Mesh, PartitionSpec as P

HD = 64
LANES = 128
ONES = 16
LOG2E = math.log2(math.e)
SAFE_BOUND = 60.0
F32 = jnp.float32
BF16 = jnp.bfloat16
NT = 4
VMEM_LIMIT = 56 * 2**20


def head_norms(x, heads):
    x = x.astype(F32)
    x = x * x
    rows = [jnp.sum(x[h * HD : (h + 1) * HD], axis=0, keepdims=True) for h in range(heads)]
    return jnp.max(jnp.concatenate(rows, axis=0), axis=1, keepdims=True)


def stage_kernel(z_ref, *refs, count):
    x_refs, o_refs, scratch = refs[:count], refs[count : count + NT], refs[-1]
    z = z_ref[0]
    inner = scratch.shape[0]
    group = inner // NT
    for a, x_ref in enumerate(x_refs):
        for c in range(0, inner, LANES):
            scratch[c : c + LANES, :] = x_ref[:, c : c + LANES].T
        for k in range(NT):
            start = pl.multiple_of((z + k) % NT * group, group)
            o_refs[k][a * group : (a + 1) * group, :] = scratch[pl.ds(start, group), :]


def stage(z, *arrays):
    tok, inner = arrays[0].shape
    vm = pl.BlockSpec(memory_space=pltpu.VMEM)
    shape = jax.ShapeDtypeStruct((len(arrays) * inner // NT, tok), BF16)
    return pl.pallas_call(
        functools.partial(stage_kernel, count=len(arrays)),
        out_shape=(shape,) * NT,
        in_specs=[pl.BlockSpec(memory_space=pltpu.SMEM)] + [vm] * len(arrays),
        out_specs=(vm,) * NT,
        scratch_shapes=[pltpu.VMEM((inner, tok), BF16)],
        cost_estimate=pl.CostEstimate(
            flops=0, transcendentals=0, bytes_accessed=8 * len(arrays) * tok * inner
        ),
        compiler_params=pltpu.CompilerParams(vmem_limit_bytes=VMEM_LIMIT),
        name="stage",
    )(z[None], *arrays)


def unstage_kernel(z_ref, *refs):
    x_refs, o_ref, scratch = refs[:NT], refs[NT], refs[NT + 1]
    group = x_refs[0].shape[0]
    for k in range(NT):
        start = pl.multiple_of((z_ref[0] + k) % NT * group, group)
        scratch[pl.ds(start, group), :] = x_refs[k][...]
    for c in range(0, NT * group, LANES):
        o_ref[:, c : c + LANES] = scratch[c : c + LANES, :].T


def unstage(z, pieces):
    group, tok = pieces[0].shape
    vm = pl.BlockSpec(memory_space=pltpu.VMEM)
    return pl.pallas_call(
        unstage_kernel,
        out_shape=jax.ShapeDtypeStruct((tok, NT * group), BF16),
        in_specs=[pl.BlockSpec(memory_space=pltpu.SMEM)] + [vm] * NT,
        out_specs=vm,
        scratch_shapes=[pltpu.VMEM((NT * group, tok), BF16)],
        compiler_params=pltpu.CompilerParams(vmem_limit_bytes=VMEM_LIMIT),
        name="unstage",
    )(z[None], *pieces)


def attention_kernel(len_ref, *refs, tiles, blocks, first, last, block_q, block_k):
    q_refs, refs = refs[:tiles], refs[tiles:]
    kv_refs, refs = refs[:blocks], refs[blocks:]
    ck_ref = cv_ref = old_ref = None
    if not first:
        old_ref, refs = refs[0], refs[1:]
    if last:
        ck_ref, cv_ref, refs = refs[0], refs[1], refs[2:]
    o_refs, (keys, vals) = refs[:-2], refs[-2:]
    inner, tok = q_refs[0].shape
    heads = inner // HD
    total = keys.shape[1]
    cap = ck_ref.shape[1] if last else 0
    length = len_ref[0]

    def place(col, k, v, kept):
        n = k.shape[1]
        for h in range(heads):
            keys[h, col : col + n, :] = k[h * HD : (h + 1) * HD].T
            vh = v[h * HD : (h + 1) * HD]
            one = jnp.ones((ONES, n), BF16)
            if kept is not None:
                vh = jnp.where(kept, vh, BF16(0))
                one = jnp.where(kept, one, BF16(0))
            vals[h, 0:HD, col : col + n] = vh
            vals[h, HD : HD + ONES, col : col + n] = one

    kmax = None
    for b, ref in enumerate(kv_refs):
        k = ref[0:inner, :]
        place(b * tok, k, ref[inner : 2 * inner, :], None)
        norms = head_norms(k, heads)
        kmax = norms if kmax is None else jnp.maximum(kmax, norms)
    if last:
        kept = lax.broadcasted_iota(jnp.int32, (1, cap), 1) < length
        place(blocks * tok, ck_ref[...], cv_ref[...], kept)
        kmax = jnp.maximum(kmax, head_norms(ck_ref[...], heads))
    qmax = head_norms(q_refs[0][...], heads)
    for ref in q_refs[1:]:
        qmax = jnp.maximum(qmax, head_norms(ref[...], heads))
    small = jnp.max(qmax * kmax) < HD * SAFE_BOUND * SAFE_BOUND
    if not first:
        offset = jnp.max(jnp.abs(old_ref[0, HD + ONES :, :]))
        for h in range(1, heads):
            offset = jnp.maximum(offset, jnp.max(jnp.abs(old_ref[h, HD + ONES :, :])))
        small = jnp.logical_and(small, offset == 0.0)

    per = block_q // tok

    def block(h, start, safe):
        rows = pl.ds(pl.multiple_of(h * HD, HD), HD)
        cols = slice(start * tok, start * tok + block_q)
        qt = jnp.concatenate([q_refs[start + b][rows, :] for b in range(per)], axis=1)
        qt = qt * BF16(0.125)
        acc = None if first else old_ref[h, 0 : HD + ONES, cols]
        m = jnp.zeros((8, block_q), F32)
        if safe:
            n = tok

            def score(c):
                s0 = pl.multiple_of(c * n, n)
                s = jnp.dot(keys[h, pl.ds(s0, n), :], qt, preferred_element_type=F32)
                if not last:
                    return s
                key = lax.broadcasted_iota(jnp.int32, (n, 1), 0) + s0
                return jnp.where(key < total - cap + length, s, -1e30)

            def peak(c, m):
                return jnp.maximum(m, jnp.max(score(c), axis=0, keepdims=True))

            old = jnp.full((1, block_q), -1e30, F32)
            if not first:
                old = old_ref[h, HD + ONES : HD + ONES + 1, cols]
            m = lax.fori_loop(0, total // n, peak, old)
            if first:
                acc = jnp.zeros((HD + ONES, block_q), F32)
            else:
                acc = acc * jnp.exp2((old - m) * LOG2E)

            def step(c, acc):
                p = jnp.exp2((score(c) - m) * LOG2E).astype(BF16)
                v = vals[h, :, pl.ds(pl.multiple_of(c * n, n), n)]
                return acc + jnp.dot(v, p, preferred_element_type=F32)

            acc = lax.fori_loop(0, total // n, step, acc)
        else:
            for c in range(0, total, block_k):
                n = min(block_k, total - c)
                s = jnp.dot(keys[h, c : c + n, :], qt, preferred_element_type=F32)
                p = jnp.exp2(s * LOG2E).astype(BF16)
                t = jnp.dot(vals[h, :, c : c + n], p, preferred_element_type=F32)
                acc = t if acc is None else acc + t
        if last:
            out = (acc[0:HD] / acc[HD : HD + 1]).astype(BF16)
            for b in range(per):
                o_refs[start + b][rows, :] = out[:, b * tok : (b + 1) * tok]
        else:
            o_refs[0][h, 0 : HD + ONES, cols] = acc
            o_refs[0][h, HD + ONES :, cols] = jnp.broadcast_to(m, (8, block_q))

    def run(safe):
        for start in range(0, tiles, per):
            lax.fori_loop(0, heads, lambda h, _: (block(h, start, safe), 0)[1], 0)

    @pl.when(small)
    def _():
        run(False)

    @pl.when(jnp.logical_not(small))
    def _():
        run(True)


def attention(length, queries, kvs, state=None, caption=(), block_q=512):
    inner, tok = queries[0].shape
    heads = inner // HD
    tiles = len(queries)
    blocks = len(kvs)
    first, last = state is None, bool(caption)
    total = blocks * tok + (caption[0].shape[1] if last else 0)
    vm = pl.BlockSpec(memory_space=pltpu.VMEM)
    operands = (*queries, *kvs, *(() if first else (state,)), *caption)
    if last:
        out_shape = (jax.ShapeDtypeStruct((inner, tok), BF16),) * tiles
    else:
        out_shape = (jax.ShapeDtypeStruct((heads, HD + ONES + 8, tiles * tok), F32),)
    return pl.pallas_call(
        functools.partial(
            attention_kernel,
            tiles=tiles,
            blocks=blocks,
            first=first,
            last=last,
            block_q=block_q,
            block_k=total // 2,
        ),
        out_shape=out_shape,
        in_specs=[pl.BlockSpec(memory_space=pltpu.SMEM)] + [vm] * len(operands),
        out_specs=(vm,) * len(out_shape),
        scratch_shapes=[
            pltpu.VMEM((heads, total, HD), BF16),
            pltpu.VMEM((heads, HD + ONES, total), BF16),
        ],
        cost_estimate=pl.CostEstimate(
            flops=16 * tiles * tok * total * inner,
            transcendentals=tiles * tok * total * heads,
            bytes_accessed=2 * inner * (2 * total + 2 * tiles * tok),
        ),
        compiler_params=pltpu.CompilerParams(vmem_limit_bytes=VMEM_LIMIT),
        name="attention",
    )(length, *operands)


def grad_kernel(w_ref, sel_ref, *refs, tiles, part):
    o_refs, cot_refs, g_ref = refs[:tiles], refs[tiles:-1], refs[-1]
    width = cot_refs[0].shape[1]
    dp, pairs, chunk, _ = g_ref.shape
    rows = [
        pl.ds(pl.multiple_of((2 * s + sel_ref[0]) * part, 16), part) for s in range(pairs)
    ]
    left = jnp.concatenate(
        [jnp.concatenate([ref[r, :] for ref in o_refs], axis=1) for r in rows], axis=0
    )
    weight = w_ref[0]
    step = 2 * LANES
    for c in range(0, width, step):
        n = min(step, width - c)
        right = jnp.concatenate([ref[:, c : c + n] for ref in cot_refs], axis=0)
        g = (jnp.dot(left, right, preferred_element_type=F32) * weight).astype(BF16)
        for t in range(n // LANES):
            cols = slice(t * LANES, (t + 1) * LANES)
            for s in range(pairs):
                done = 0
                while done < part:
                    flat = (c // LANES + t) * part + done
                    count = min(part - done, chunk - flat % chunk)
                    g_ref[flat // chunk, s, flat % chunk : flat % chunk + count, :] = g[
                        s * part + done : s * part + done + count, cols
                    ]
                    done += count
    used = width // LANES * part - (dp - 1) * chunk
    if used < chunk:
        for s in range(pairs):
            g_ref[dp - 1, s, used:, :] = jnp.zeros((chunk - used, LANES), BF16)


def local_grad(weight, select, attended, cots, part, dp):
    inner, tok = attended[0].shape
    width = cots[0].shape[1]
    pairs = inner // (2 * part)
    chunk = -(-(width // LANES * part) // (dp * 16)) * 16
    vm = pl.BlockSpec(memory_space=pltpu.VMEM)
    smem = pl.BlockSpec(memory_space=pltpu.SMEM)
    tiles = len(attended)
    return pl.pallas_call(
        functools.partial(grad_kernel, tiles=tiles, part=part),
        out_shape=jax.ShapeDtypeStruct((dp, pairs, chunk, LANES), BF16),
        in_specs=[smem, smem] + [vm] * (tiles + len(cots)),
        out_specs=vm,
        cost_estimate=pl.CostEstimate(
            flops=tiles * tok * inner * width,
            transcendentals=0,
            bytes_accessed=2 * tiles * tok * (inner + width) + inner * width,
        ),
        compiler_params=pltpu.CompilerParams(vmem_limit_bytes=VMEM_LIMIT),
        name="local_grad",
    )(weight, select[None], *attended, *cots)


def adam_kernel(f_ref, g_ref, w_ref, mv_ref, ms_ref, vv_ref, vs_ref, nw, nmv, nms, nvv, nvs):
    rows, width = w_ref.shape
    factor = f_ref[0]
    diagonal = lax.broadcasted_iota(jnp.int32, (rows, rows), 0) == lax.broadcasted_iota(
        jnp.int32, (rows, rows), 1
    )

    def down(row):
        return jnp.sum(jnp.where(diagonal, row, 0.0), axis=1, keepdims=True)

    def across(column):
        return jnp.sum(jnp.where(diagonal, column, 0.0), axis=0, keepdims=True)

    for t in range(width // LANES):
        cols = slice(t * LANES, (t + 1) * LANES)
        one = slice(t, t + 1)
        g = g_ref[t * rows : (t + 1) * rows, :].astype(F32) * factor
        first = mv_ref[:, cols].astype(F32) * down(ms_ref[one, :])
        second = vv_ref[:, cols].astype(F32) * down(vs_ref[one, :])
        first = 0.9 * first + 0.1 * g
        second = 0.999 * second + 0.001 * g * g
        update = first / (1.0 - 0.9**10) / (jnp.sqrt(second / (1.0 - 0.999**10)) + 1e-08)
        nw[:, cols] = (w_ref[:, cols].astype(F32) - 0.02 * update).astype(BF16)
        fs = jnp.max(jnp.abs(first), axis=1, keepdims=True) + 1e-06
        ss = jnp.max(jnp.abs(second), axis=1, keepdims=True) + 1e-06
        nms[one, :] = across(fs)
        nvs[one, :] = across(ss)
        nmv[:, cols] = (first / fs).astype(BF16)
        nvv[:, cols] = (second / ss).astype(BF16)


def adam(factor, grad, out_weight, mom_val, mom_scale, var_val, var_scale):
    vm = pl.BlockSpec(memory_space=pltpu.VMEM)
    like = lambda a: jax.ShapeDtypeStruct(a.shape, a.dtype)
    mom_scale, var_scale = mom_scale.T, var_scale.T
    new_weight, first_val, first_scale, second_val, second_scale = pl.pallas_call(
        adam_kernel,
        out_shape=(like(out_weight), like(mom_val), like(mom_scale), like(var_val), like(var_scale)),
        in_specs=[pl.BlockSpec(memory_space=pltpu.SMEM)] + [vm] * 6,
        out_specs=(vm,) * 5,
        compiler_params=pltpu.CompilerParams(vmem_limit_bytes=VMEM_LIMIT),
        name="adam",
    )(factor, grad, out_weight, mom_val, mom_scale, var_val, var_scale)
    return new_weight, first_val, first_scale.T, second_val, second_scale.T


def swap(x, axis):
    return lax.ppermute(x, axis, [(0, 1), (1, 0)])


def shift(x, k):
    return lax.ppermute(x, "z", [(i, (i + k) % NT) for i in range(NT)])


def body(
    latent_q,
    latent_k,
    latent_v,
    caption_states,
    caption_proj,
    caption_len,
    timestep,
    out_cot,
    out_weight,
    mom_val,
    mom_scale,
    var_val,
    var_scale,
):
    tok, inner = latent_q.shape[1:]
    cap = caption_states.shape[1]
    xh, z, c = lax.axis_index("xh"), lax.axis_index("z"), lax.axis_index("c")

    own = stage(z, latent_k[0], latent_v[0])
    own = [own[0]] + [shift(own[k], k) for k in range(1, NT)]
    far = [swap(own[0], "xh")]

    partial = lax.dot_general(
        caption_proj, caption_states[0], (((0,), (1,)), ((), ())), preferred_element_type=F32
    ).astype(BF16)
    pieces = partial.reshape(2 * NT, 2, 2 * inner // (4 * NT), cap)
    take = lambda i: lax.dynamic_index_in_dim(pieces, i, 1, keepdims=False)
    pieces = (take(c).astype(F32) + swap(take(1 - c), "c").astype(F32)).astype(BF16)

    queries = stage(z, latent_q[0])
    held = lax.optimization_barrier((pieces, *queries[1:], *own[1:]))
    pieces, ready, own = held[0], held[1:NT], [own[0], *held[NT:]]
    queries = [queries[0]] + [shift(ready[k - 1], k) for k in range(1, NT)]
    far = far + [swap(x, "xh") for x in own[1:]]

    pieces = lax.all_to_all(pieces, ("xh", "z"), 0, 0, tiled=True)
    cap_own = jnp.sum(pieces.astype(F32), axis=0).astype(BF16)
    cap_far = swap(cap_own, "xh")

    def both(x):
        y = swap(x, "c")
        return jnp.concatenate([jnp.where(c == 0, x, y), jnp.where(c == 0, y, x)], axis=0)

    cap_own, cap_far = both(cap_own), both(cap_far)
    cap_k = jnp.where(xh == 0, cap_own, cap_far)
    cap_v = jnp.where(xh == 0, cap_far, cap_own)

    held = lax.optimization_barrier((out_cot[0], *queries[1:]))
    cot, queries = held[0], [queries[0], *held[1:]]
    half = tok // 2
    before, after = shift(cot, 1), shift(cot, -1)

    near = own + [swap(x, "c") for x in own]
    (state,) = attention(caption_len, queries, near)
    far = far + [swap(x, "c") for x in far]
    attended = attention(caption_len, queries, far, state, (cap_k, cap_v))
    cots = [cot, before, shift(before[:half], 1), shift(after[half:], -1), after]

    loss_weight = 1.0 + 3.0 * (timestep.astype(F32) + 0.5) / 1000.0
    rows = out_weight.shape[0]
    dp = lax.axis_size("xl") * lax.axis_size("y")
    other = swap(local_grad(loss_weight, 1 - c, attended, cots, rows, dp), "c")
    grad = local_grad(loss_weight, c, attended, cots, rows, dp)
    grad = (grad.astype(F32) + other.astype(F32)).astype(BF16)
    chunk = grad.shape[2]
    grad = lax.all_to_all(
        grad.reshape(2 * dp, chunk, LANES), ("xl", "y", "xh"), 0, 0, tiled=True
    )
    grad = jnp.sum(grad.astype(F32), axis=0).astype(BF16)
    square = jnp.sum(jnp.square(grad.astype(F32)))
    perm = [
        (s * NT + i, (i // 2) * NT + 2 * (i % 2) + s) for s in range(2) for i in range(NT)
    ]
    grad = lax.ppermute(grad, ("xh", "z"), perm)
    grad = jnp.broadcast_to(grad[None], (dp, chunk, LANES))
    grad = lax.all_to_all(grad, ("xl", "y"), 0, 0, tiled=True).reshape(dp * chunk, LANES)
    everyone = ("xl", "y", "xh", "z", "c")
    squares = lax.all_to_all(
        jnp.broadcast_to(square, (lax.axis_size(everyone), LANES)), everyone, 0, 0, tiled=True
    )
    factor = 256.0 / jnp.sqrt(jnp.sum(squares[:, 0]) + 1e-06)

    back = [attended[0]] + [shift(attended[k], -k) for k in range(1, NT)]
    attn_out = unstage(z, back)[None]
    updated = adam(factor[None], grad, out_weight, mom_val, mom_scale, var_val, var_scale)
    return (attn_out, *updated)


def solution(mesh):
    fine = Mesh(mesh.devices.reshape(2, 4, 2, NT, 2), ("xl", "y", "xh", "z", "c"))
    dp = ("xl", "y")
    ctx = ("xh", "z", "c")
    tokens = P(dp, ctx, None)
    rows = P(ctx, None)
    return jax.shard_map(
        body,
        mesh=fine,
        in_specs=(
            tokens,
            tokens,
            tokens,
            P(dp, None, ctx),
            rows,
            P(dp),
            P(dp),
            tokens,
            rows,
            rows,
            rows,
            rows,
            rows,
        ),
        out_specs=(tokens, rows, rows, rows, rows, rows),
        check_vma=False,
    )
```

```python
import functools
import math

import jax
import jax.numpy as jnp
from jax import lax
from jax.experimental import pallas as pl
from jax.experimental.pallas import tpu as pltpu
from jax.sharding import Mesh, PartitionSpec as P

HD = 64
LANES = 128
ONES = 16
LOG2E = math.log2(math.e)
SAFE_BOUND = 60.0
F32 = jnp.float32
BF16 = jnp.bfloat16
NT = 4
VMEM_LIMIT = 24 * 2**20


def head_norms(x, heads):
    x = x.astype(F32)
    x = x * x
    rows = [jnp.sum(x[h * HD : (h + 1) * HD], axis=0, keepdims=True) for h in range(heads)]
    return jnp.max(jnp.concatenate(rows, axis=0), axis=1, keepdims=True)


def stage_kernel(z_ref, *refs, count):
    x_refs, o_refs, own_ref, scratch = refs[:count], refs[count : count + NT], refs[-2], refs[-1]
    z = z_ref[0]
    inner = scratch.shape[0]
    group = inner // NT
    for a, x_ref in enumerate(x_refs):
        for c in range(0, inner, LANES):
            scratch[c : c + LANES, :] = x_ref[:, c : c + LANES].T
        for k in range(NT):
            start = pl.multiple_of((z + k) % NT * group, group)
            piece = scratch[pl.ds(start, group), :]
            o_refs[k][a * group : (a + 1) * group, :] = piece
            if k == 0 and a < count - 1:
                own_ref[a * group : (a + 1) * group, :] = piece


def stage(z, *arrays):
    tok, inner = arrays[0].shape
    vm = pl.BlockSpec(memory_space=pltpu.VMEM)
    shape = jax.ShapeDtypeStruct((len(arrays) * inner // NT, tok), BF16)
    own = jax.ShapeDtypeStruct(((len(arrays) - 1) * inner // NT, tok), BF16)
    return pl.pallas_call(
        functools.partial(stage_kernel, count=len(arrays)),
        out_shape=(shape,) * NT + (own,),
        in_specs=[pl.BlockSpec(memory_space=pltpu.SMEM)] + [vm] * len(arrays),
        out_specs=(vm,) * (NT + 1),
        scratch_shapes=[pltpu.VMEM((inner, tok), BF16)],
        cost_estimate=pl.CostEstimate(
            flops=0, transcendentals=0, bytes_accessed=8 * len(arrays) * tok * inner
        ),
        compiler_params=pltpu.CompilerParams(vmem_limit_bytes=VMEM_LIMIT),
        name="stage",
    )(z[None], *arrays)


def unstage_kernel(z_ref, *refs):
    x_refs, o_ref, scratch = refs[:NT], refs[NT], refs[NT + 1]
    group = x_refs[0].shape[0]
    for k in range(NT):
        start = pl.multiple_of((z_ref[0] + k) % NT * group, group)
        scratch[pl.ds(start, group), :] = x_refs[k][...]
    for c in range(0, NT * group, LANES):
        o_ref[:, c : c + LANES] = scratch[c : c + LANES, :].T


def unstage(z, pieces):
    group, tok = pieces[0].shape
    vm = pl.BlockSpec(memory_space=pltpu.VMEM)
    return pl.pallas_call(
        unstage_kernel,
        out_shape=jax.ShapeDtypeStruct((tok, NT * group), BF16),
        in_specs=[pl.BlockSpec(memory_space=pltpu.SMEM)] + [vm] * NT,
        out_specs=vm,
        scratch_shapes=[pltpu.VMEM((NT * group, tok), BF16)],
        compiler_params=pltpu.CompilerParams(vmem_limit_bytes=VMEM_LIMIT),
        name="unstage",
    )(z[None], *pieces)


def attention_kernel(len_ref, *refs, tiles, sources, first, last, block_q, block_k):
    q_refs, refs = refs[:tiles], refs[tiles:]
    kv_refs, refs = refs[:sources], refs[sources:]
    ck_ref = cv_ref = old_ref = None
    if not first:
        old_ref, refs = refs[0], refs[1:]
    if last:
        ck_ref, cv_ref, refs = refs[0], refs[1], refs[2:]
    o_refs, (keys, vals) = refs[:-2], refs[-2:]
    inner, tok = q_refs[0].shape[0] // 3, q_refs[0].shape[1]
    heads = inner // HD
    total = keys.shape[1]
    cap = ck_ref.shape[1] if last else 0
    length = len_ref[0]
    pairs = []
    for ref in (*(q_refs if first else ()), *kv_refs):
        views = [ref] if len(ref.shape) == 2 else [ref.at[i] for i in range(ref.shape[0])]
        pairs += [(v[0:inner, :], v[inner : 2 * inner, :]) for v in views]

    def place(col, k, v, kept):
        n = k.shape[1]
        for h in range(heads):
            keys[h, col : col + n, :] = k[h * HD : (h + 1) * HD].T
            vh = v[h * HD : (h + 1) * HD]
            one = jnp.ones((ONES, n), BF16)
            if kept is not None:
                vh = jnp.where(kept, vh, BF16(0))
                one = jnp.where(kept, one, BF16(0))
            vals[h, 0:HD, col : col + n] = vh
            vals[h, HD : HD + ONES, col : col + n] = one

    kmax = None
    for b, (k, v) in enumerate(pairs):
        place(b * tok, k, v, None)
        norms = head_norms(k, heads)
        kmax = norms if kmax is None else jnp.maximum(kmax, norms)
    if last:
        kept = lax.broadcasted_iota(jnp.int32, (1, cap), 1) < length
        place(len(pairs) * tok, ck_ref[...], cv_ref[...], kept)
        kmax = jnp.maximum(kmax, head_norms(ck_ref[...], heads))
    qmax = None
    for ref in q_refs:
        norms = head_norms(ref[2 * inner :, :], heads)
        qmax = norms if qmax is None else jnp.maximum(qmax, norms)
    small = jnp.max(qmax * kmax) < HD * SAFE_BOUND * SAFE_BOUND
    if not first:
        offset = jnp.max(jnp.abs(old_ref[0, HD + ONES :, :]))
        for h in range(1, heads):
            offset = jnp.maximum(offset, jnp.max(jnp.abs(old_ref[h, HD + ONES :, :])))
        small = jnp.logical_and(small, offset == 0.0)

    per = block_q // tok

    def block(h, start, safe):
        rows = pl.ds(pl.multiple_of(h * HD, HD), HD)
        cols = slice(start * tok, start * tok + block_q)
        queries = pl.ds(pl.multiple_of(2 * inner + h * HD, HD), HD)
        qt = jnp.concatenate([q_refs[start + b][queries, :] for b in range(per)], axis=1)
        qt = qt * BF16(0.125)
        acc = None if first else old_ref[h, 0 : HD + ONES, cols]
        m = jnp.zeros((8, block_q), F32)
        if safe:
            n = tok

            def score(c):
                s0 = pl.multiple_of(c * n, n)
                s = jnp.dot(keys[h, pl.ds(s0, n), :], qt, preferred_element_type=F32)
                if not last:
                    return s
                key = lax.broadcasted_iota(jnp.int32, (n, 1), 0) + s0
                return jnp.where(key < total - cap + length, s, -1e30)

            def peak(c, m):
                return jnp.maximum(m, jnp.max(score(c), axis=0, keepdims=True))

            old = jnp.full((1, block_q), -1e30, F32)
            if not first:
                old = old_ref[h, HD + ONES : HD + ONES + 1, cols]
            m = lax.fori_loop(0, total // n, peak, old)
            if first:
                acc = jnp.zeros((HD + ONES, block_q), F32)
            else:
                acc = acc * jnp.exp2((old - m) * LOG2E)

            def step(c, acc):
                p = jnp.exp2((score(c) - m) * LOG2E).astype(BF16)
                v = vals[h, :, pl.ds(pl.multiple_of(c * n, n), n)]
                return acc + jnp.dot(v, p, preferred_element_type=F32)

            acc = lax.fori_loop(0, total // n, step, acc)
        else:
            for c in range(0, total, block_k):
                n = min(block_k, total - c)
                s = jnp.dot(keys[h, c : c + n, :], qt, preferred_element_type=F32)
                p = jnp.exp2(s * LOG2E).astype(BF16)
                t = jnp.dot(vals[h, :, c : c + n], p, preferred_element_type=F32)
                acc = t if acc is None else acc + t
        if last:
            out = (acc[0:HD] / acc[HD : HD + 1]).astype(BF16)
            for b in range(per):
                o_refs[start + b][rows, :] = out[:, b * tok : (b + 1) * tok]
        else:
            o_refs[0][h, 0 : HD + ONES, cols] = acc
            o_refs[0][h, HD + ONES :, cols] = jnp.broadcast_to(m, (8, block_q))

    def run(safe):
        for start in range(0, tiles, per):
            lax.fori_loop(0, heads, lambda h, _: (block(h, start, safe), 0)[1], 0)

    @pl.when(small)
    def _():
        run(False)

    @pl.when(jnp.logical_not(small))
    def _():
        run(True)


def attention(length, chunks, kvs, state=None, caption=(), block_q=512):
    inner, tok = chunks[0].shape[0] // 3, chunks[0].shape[1]
    heads = inner // HD
    tiles = len(chunks)
    first, last = state is None, bool(caption)
    blocks = sum(x.size for x in kvs) // (2 * inner * tok) + (tiles if first else 0)
    total = blocks * tok + (caption[0].shape[1] if last else 0)
    vm = pl.BlockSpec(memory_space=pltpu.VMEM)
    operands = (*chunks, *kvs, *(() if first else (state,)), *caption)
    if last:
        out_shape = (jax.ShapeDtypeStruct((inner, tok), BF16),) * tiles
    else:
        out_shape = (jax.ShapeDtypeStruct((heads, HD + ONES + 8, tiles * tok), F32),)
    return pl.pallas_call(
        functools.partial(
            attention_kernel,
            tiles=tiles,
            sources=len(kvs),
            first=first,
            last=last,
            block_q=block_q,
            block_k=total // 2,
        ),
        out_shape=out_shape,
        in_specs=[pl.BlockSpec(memory_space=pltpu.SMEM)] + [vm] * len(operands),
        out_specs=(vm,) * len(out_shape),
        scratch_shapes=[
            pltpu.VMEM((heads, total, HD), BF16),
            pltpu.VMEM((heads, HD + ONES, total), BF16),
        ],
        cost_estimate=pl.CostEstimate(
            flops=16 * tiles * tok * total * inner,
            transcendentals=tiles * tok * total * heads,
            bytes_accessed=2 * inner * (2 * total + 2 * tiles * tok),
        ),
        compiler_params=pltpu.CompilerParams(vmem_limit_bytes=VMEM_LIMIT),
        name="attention",
    )(length, *operands)


def grad_kernel(w_ref, sel_ref, *refs, tiles, part):
    o_refs, cot_refs, g_ref = refs[:tiles], refs[tiles:-1], refs[-1]
    width = cot_refs[0].shape[1]
    dp, pairs, chunk, _ = g_ref.shape
    rows = [
        pl.ds(pl.multiple_of((2 * s + sel_ref[0]) * part, 16), part) for s in range(pairs)
    ]
    left = jnp.concatenate(
        [jnp.concatenate([ref[r, :] for ref in o_refs], axis=1) for r in rows], axis=0
    )
    weight = w_ref[0]
    step = 2 * LANES
    for c in range(0, width, step):
        n = min(step, width - c)
        right = jnp.concatenate([ref[:, c : c + n] for ref in cot_refs], axis=0)
        g = (jnp.dot(left, right, preferred_element_type=F32) * weight).astype(BF16)
        for t in range(n // LANES):
            cols = slice(t * LANES, (t + 1) * LANES)
            for s in range(pairs):
                done = 0
                while done < part:
                    flat = (c // LANES + t) * part + done
                    count = min(part - done, chunk - flat % chunk)
                    g_ref[flat // chunk, s, flat % chunk : flat % chunk + count, :] = g[
                        s * part + done : s * part + done + count, cols
                    ]
                    done += count
    used = width // LANES * part - (dp - 1) * chunk
    if used < chunk:
        for s in range(pairs):
            g_ref[dp - 1, s, used:, :] = jnp.zeros((chunk - used, LANES), BF16)


def local_grad(weight, select, attended, cots, part, dp):
    inner, tok = attended[0].shape
    width = cots[0].shape[1]
    pairs = inner // (2 * part)
    chunk = -(-(width // LANES * part) // (dp * 16)) * 16
    vm = pl.BlockSpec(memory_space=pltpu.VMEM)
    smem = pl.BlockSpec(memory_space=pltpu.SMEM)
    tiles = len(attended)
    return pl.pallas_call(
        functools.partial(grad_kernel, tiles=tiles, part=part),
        out_shape=jax.ShapeDtypeStruct((dp, pairs, chunk, LANES), BF16),
        in_specs=[smem, smem] + [vm] * (tiles + len(cots)),
        out_specs=vm,
        cost_estimate=pl.CostEstimate(
            flops=tiles * tok * inner * width,
            transcendentals=0,
            bytes_accessed=2 * tiles * tok * (inner + width) + inner * width,
        ),
        compiler_params=pltpu.CompilerParams(vmem_limit_bytes=VMEM_LIMIT),
        name="local_grad",
    )(weight, select[None], *attended, *cots)


def adam_kernel(f_ref, g_ref, w_ref, mv_ref, ms_ref, vv_ref, vs_ref, nw, nmv, nms, nvv, nvs):
    rows, width = w_ref.shape
    factor = f_ref[0]
    diagonal = lax.broadcasted_iota(jnp.int32, (rows, rows), 0) == lax.broadcasted_iota(
        jnp.int32, (rows, rows), 1
    )

    def down(row):
        return jnp.sum(jnp.where(diagonal, row, 0.0), axis=1, keepdims=True)

    def across(column):
        return jnp.sum(jnp.where(diagonal, column, 0.0), axis=0, keepdims=True)

    for t in range(width // LANES):
        cols = slice(t * LANES, (t + 1) * LANES)
        one = slice(t, t + 1)
        g = g_ref[t * rows : (t + 1) * rows, :].astype(F32) * factor
        first = mv_ref[:, cols].astype(F32) * down(ms_ref[one, :])
        second = vv_ref[:, cols].astype(F32) * down(vs_ref[one, :])
        first = 0.9 * first + 0.1 * g
        second = 0.999 * second + 0.001 * g * g
        update = first / (1.0 - 0.9**10) / (jnp.sqrt(second / (1.0 - 0.999**10)) + 1e-08)
        nw[:, cols] = (w_ref[:, cols].astype(F32) - 0.02 * update).astype(BF16)
        fs = jnp.max(jnp.abs(first), axis=1, keepdims=True) + 1e-06
        ss = jnp.max(jnp.abs(second), axis=1, keepdims=True) + 1e-06
        nms[one, :] = across(fs)
        nvs[one, :] = across(ss)
        nmv[:, cols] = (first / fs).astype(BF16)
        nvv[:, cols] = (second / ss).astype(BF16)


def adam(factor, grad, out_weight, mom_val, mom_scale, var_val, var_scale):
    vm = pl.BlockSpec(memory_space=pltpu.VMEM)
    like = lambda a: jax.ShapeDtypeStruct(a.shape, a.dtype)
    mom_scale, var_scale = mom_scale.T, var_scale.T
    new_weight, first_val, first_scale, second_val, second_scale = pl.pallas_call(
        adam_kernel,
        out_shape=(like(out_weight), like(mom_val), like(mom_scale), like(var_val), like(var_scale)),
        in_specs=[pl.BlockSpec(memory_space=pltpu.SMEM)] + [vm] * 6,
        out_specs=(vm,) * 5,
        compiler_params=pltpu.CompilerParams(vmem_limit_bytes=VMEM_LIMIT),
        name="adam",
    )(factor, grad, out_weight, mom_val, mom_scale, var_val, var_scale)
    return new_weight, first_val, first_scale.T, second_val, second_scale.T


def swap(x, axis):
    return lax.ppermute(x, axis, [(0, 1), (1, 0)])


def shift(x, k):
    return lax.ppermute(x, "z", [(i, (i + k) % NT) for i in range(NT)])


def body(
    latent_q,
    latent_k,
    latent_v,
    caption_states,
    caption_proj,
    caption_len,
    timestep,
    out_cot,
    out_weight,
    mom_val,
    mom_scale,
    var_val,
    var_scale,
):
    tok, inner = latent_q.shape[1:]
    cap = caption_states.shape[1]
    xh, z, c = lax.axis_index("xh"), lax.axis_index("z"), lax.axis_index("c")

    *chunks, own = stage(z, latent_k[0], latent_v[0], latent_q[0])
    chunks = [chunks[0]] + [shift(chunks[k], k) for k in range(1, NT)]
    near = [swap(own, "c")]
    far = [swap(own, "xh")]

    states = lax.optimization_barrier((caption_states[0], own))[0]
    partial = lax.dot_general(
        caption_proj, states, (((0,), (1,)), ((), ())), preferred_element_type=F32
    ).astype(BF16)
    pieces = partial.reshape(2 * NT, 2, 2 * inner // (4 * NT), cap)
    take = lambda i: lax.dynamic_index_in_dim(pieces, i, 1, keepdims=False)
    pieces = (take(c).astype(F32) + swap(take(1 - c), "c").astype(F32)).astype(BF16)

    others = jnp.stack([x[: 2 * inner // NT] for x in chunks[1:]])
    far = far + [swap(others, "xh")]
    near = near + [swap(others, "c")]
    pieces, others = lax.optimization_barrier((pieces, others))

    pieces = lax.all_to_all(pieces, ("xh", "z"), 0, 0, tiled=True)
    cap_own = jnp.sum(pieces.astype(F32), axis=0).astype(BF16)
    cap_far = swap(cap_own, "xh")

    def both(x):
        y = swap(x, "c")
        return jnp.concatenate([jnp.where(c == 0, x, y), jnp.where(c == 0, y, x)], axis=0)

    cap_own, cap_far = both(cap_own), both(cap_far)
    cap_k = jnp.where(xh == 0, cap_own, cap_far)
    cap_v = jnp.where(xh == 0, cap_far, cap_own)

    cot, *near = lax.optimization_barrier((out_cot[0], *near))
    half = tok // 2
    before, after = shift(cot, 1), shift(cot, -1)

    (state,) = attention(caption_len, chunks, near)
    (state,) = attention(caption_len, chunks, far, state)
    before, after, state = lax.optimization_barrier((before, after, state))
    far = [swap(x, "c") for x in far]
    attended = attention(caption_len, chunks, far, state, (cap_k, cap_v))
    cots = [cot, before, shift(before[:half], 1), shift(after[half:], -1), after]
    back = [attended[0]] + [shift(attended[k], -k) for k in range(1, NT)]

    loss_weight = 1.0 + 3.0 * (timestep.astype(F32) + 0.5) / 1000.0
    rows = out_weight.shape[0]
    dp = lax.axis_size("xl") * lax.axis_size("y")
    other = swap(local_grad(loss_weight, 1 - c, attended, cots, rows, dp), "c")
    grad = local_grad(loss_weight, c, attended, cots, rows, dp)
    grad = (grad.astype(F32) + other.astype(F32)).astype(BF16)
    grad, *back = lax.optimization_barrier((grad, *back))
    chunk = grad.shape[2]
    grad = lax.all_to_all(
        grad.reshape(2 * dp, chunk, LANES), ("xl", "y", "xh"), 0, 0, tiled=True
    )
    grad = jnp.sum(grad.astype(F32), axis=0).astype(BF16)
    square = jnp.sum(jnp.square(grad.astype(F32)))
    perm = [
        (s * NT + i, (i // 2) * NT + 2 * (i % 2) + s) for s in range(2) for i in range(NT)
    ]
    grad = lax.ppermute(grad, ("xh", "z"), perm)
    grad, square = lax.optimization_barrier((grad, square))
    grad = jnp.broadcast_to(grad[None], (dp, chunk, LANES))
    grad = lax.all_to_all(grad, ("xl", "y"), 0, 0, tiled=True).reshape(dp * chunk, LANES)
    everyone = ("xl", "y", "xh", "z", "c")
    squares = lax.all_to_all(
        jnp.broadcast_to(square, (lax.axis_size(everyone), LANES)), everyone, 0, 0, tiled=True
    )
    factor = 256.0 / jnp.sqrt(jnp.sum(squares[:, 0]) + 1e-06)

    attn_out = unstage(z, back)[None]
    updated = adam(factor[None], grad, out_weight, mom_val, mom_scale, var_val, var_scale)
    return (attn_out, *updated)


def solution(mesh):
    fine = Mesh(mesh.devices.reshape(2, 4, 2, NT, 2), ("xl", "y", "xh", "z", "c"))
    dp = ("xl", "y")
    ctx = ("xh", "z", "c")
    tokens = P(dp, ctx, None)
    rows = P(ctx, None)
    return jax.shard_map(
        body,
        mesh=fine,
        in_specs=(
            tokens,
            tokens,
            tokens,
            P(dp, None, ctx),
            rows,
            P(dp),
            P(dp),
            tokens,
            rows,
            rows,
            rows,
            rows,
            rows,
        ),
        out_specs=(tokens, rows, rows, rows, rows, rows),
        check_vma=False,
    )
```

```python
import functools
import math

import jax
import jax.numpy as jnp
from jax import lax
from jax.experimental import pallas as pl
from jax.experimental.pallas import tpu as pltpu
from jax.sharding import Mesh, PartitionSpec as P

HD = 64
LANES = 128
ONES = 16
LOG2E = math.log2(math.e)
SAFE_BOUND = 60.0
F32 = jnp.float32
BF16 = jnp.bfloat16
NT = 4
VMEM_LIMIT = 24 * 2**20


def head_norms(x, heads):
    x = x.astype(F32)
    x = x * x
    rows = [jnp.sum(x[h * HD : (h + 1) * HD], axis=0, keepdims=True) for h in range(heads)]
    return jnp.max(jnp.concatenate(rows, axis=0), axis=1, keepdims=True)


def stage_kernel(z_ref, *refs, count):
    x_refs, o_refs, own_ref, scratch = refs[:count], refs[count : count + NT], refs[-2], refs[-1]
    z = z_ref[0]
    inner = scratch.shape[0]
    group = inner // NT
    for a, x_ref in enumerate(x_refs):
        for c in range(0, inner, LANES):
            scratch[c : c + LANES, :] = x_ref[:, c : c + LANES].T
        for k in range(NT):
            start = pl.multiple_of((z + k) % NT * group, group)
            piece = scratch[pl.ds(start, group), :]
            o_refs[k][a * group : (a + 1) * group, :] = piece
            if k == 0 and a < count - 1:
                own_ref[a * group : (a + 1) * group, :] = piece


def stage(z, *arrays):
    tok, inner = arrays[0].shape
    vm = pl.BlockSpec(memory_space=pltpu.VMEM)
    shape = jax.ShapeDtypeStruct((len(arrays) * inner // NT, tok), BF16)
    own = jax.ShapeDtypeStruct(((len(arrays) - 1) * inner // NT, tok), BF16)
    return pl.pallas_call(
        functools.partial(stage_kernel, count=len(arrays)),
        out_shape=(shape,) * NT + (own,),
        in_specs=[pl.BlockSpec(memory_space=pltpu.SMEM)] + [vm] * len(arrays),
        out_specs=(vm,) * (NT + 1),
        scratch_shapes=[pltpu.VMEM((inner, tok), BF16)],
        cost_estimate=pl.CostEstimate(
            flops=0, transcendentals=0, bytes_accessed=8 * len(arrays) * tok * inner
        ),
        compiler_params=pltpu.CompilerParams(vmem_limit_bytes=VMEM_LIMIT),
        name="stage",
    )(z[None], *arrays)


def unstage_kernel(z_ref, *refs):
    x_refs, o_ref, scratch = refs[:NT], refs[NT], refs[NT + 1]
    group = x_refs[0].shape[0]
    for k in range(NT):
        start = pl.multiple_of((z_ref[0] + k) % NT * group, group)
        scratch[pl.ds(start, group), :] = x_refs[k][...]
    for c in range(0, NT * group, LANES):
        o_ref[:, c : c + LANES] = scratch[c : c + LANES, :].T


def unstage(z, pieces):
    group, tok = pieces[0].shape
    vm = pl.BlockSpec(memory_space=pltpu.VMEM)
    return pl.pallas_call(
        unstage_kernel,
        out_shape=jax.ShapeDtypeStruct((tok, NT * group), BF16),
        in_specs=[pl.BlockSpec(memory_space=pltpu.SMEM)] + [vm] * NT,
        out_specs=vm,
        scratch_shapes=[pltpu.VMEM((NT * group, tok), BF16)],
        compiler_params=pltpu.CompilerParams(vmem_limit_bytes=VMEM_LIMIT),
        name="unstage",
    )(z[None], *pieces)


def attention_kernel(len_ref, where_ref, *refs, tiles, sources, first, last, block_q, block_k):
    q_refs, refs = refs[:tiles], refs[tiles:]
    kv_refs, refs = refs[:sources], refs[sources:]
    old_ref = None
    if not first:
        old_ref, refs = refs[0], refs[1:]
    if last:
        piece_refs, refs = refs[:4], refs[4:]
        refs, cap_ref = refs[:-1], refs[-1]
        part = cap_ref.shape[0] // 4
        for flip, ref in enumerate(piece_refs):
            at = (where_ref[0] ^ (flip // 2)) * 2 + (where_ref[1] ^ (flip % 2))
            cap_ref[pl.ds(pl.multiple_of(at * part, part), part), :] = ref[ref.shape[0] - part :, :]
    o_refs, (keys, vals) = refs[:-2], refs[-2:]
    inner, tok = q_refs[0].shape[0] // 3, q_refs[0].shape[1]
    heads = inner // HD
    total = keys.shape[1]
    cap = cap_ref.shape[1] if last else 0
    length = len_ref[0]
    pairs = []
    for ref in (*(q_refs if first else ()), *kv_refs):
        for r in range(0, max(1, ref.shape[0] // (2 * inner)) * 2 * inner, 2 * inner):
            pairs.append((ref[r : r + inner, :], ref[r + inner : r + 2 * inner, :]))

    def place(col, k, v, kept):
        n = k.shape[1]
        for h in range(heads):
            keys[h, col : col + n, :] = k[h * HD : (h + 1) * HD].T
            vh = v[h * HD : (h + 1) * HD]
            one = jnp.ones((ONES, n), BF16)
            if kept is not None:
                vh = jnp.where(kept, vh, BF16(0))
                one = jnp.where(kept, one, BF16(0))
            vals[h, 0:HD, col : col + n] = vh
            vals[h, HD : HD + ONES, col : col + n] = one

    kmax = None
    for b, (k, v) in enumerate(pairs):
        place(b * tok, k, v, None)
        norms = head_norms(k, heads)
        kmax = norms if kmax is None else jnp.maximum(kmax, norms)
    if last:
        kept = lax.broadcasted_iota(jnp.int32, (1, cap), 1) < length
        ck = cap_ref[0:inner, :]
        place(len(pairs) * tok, ck, cap_ref[inner : 2 * inner, :], kept)
        kmax = jnp.maximum(kmax, head_norms(ck, heads))
    qmax = None
    for ref in q_refs:
        norms = head_norms(ref[2 * inner :, :], heads)
        qmax = norms if qmax is None else jnp.maximum(qmax, norms)
    small = jnp.max(qmax * kmax) < HD * SAFE_BOUND * SAFE_BOUND
    if not first:
        offset = jnp.max(jnp.abs(old_ref[0, HD + ONES :, :]))
        for h in range(1, heads):
            offset = jnp.maximum(offset, jnp.max(jnp.abs(old_ref[h, HD + ONES :, :])))
        small = jnp.logical_and(small, offset == 0.0)

    per = block_q // tok

    def block(h, start, safe):
        rows = pl.ds(pl.multiple_of(h * HD, HD), HD)
        cols = slice(start * tok, start * tok + block_q)
        queries = pl.ds(pl.multiple_of(2 * inner + h * HD, HD), HD)
        qt = jnp.concatenate([q_refs[start + b][queries, :] for b in range(per)], axis=1)
        qt = qt * BF16(0.125)
        acc = None if first else old_ref[h, 0 : HD + ONES, cols]
        m = jnp.zeros((8, block_q), F32)
        if safe:
            n = tok

            def score(c):
                s0 = pl.multiple_of(c * n, n)
                s = jnp.dot(keys[h, pl.ds(s0, n), :], qt, preferred_element_type=F32)
                if not last:
                    return s
                key = lax.broadcasted_iota(jnp.int32, (n, 1), 0) + s0
                return jnp.where(key < total - cap + length, s, -1e30)

            def peak(c, m):
                return jnp.maximum(m, jnp.max(score(c), axis=0, keepdims=True))

            old = jnp.full((1, block_q), -1e30, F32)
            if not first:
                old = old_ref[h, HD + ONES : HD + ONES + 1, cols]
            m = lax.fori_loop(0, total // n, peak, old)
            if first:
                acc = jnp.zeros((HD + ONES, block_q), F32)
            else:
                acc = acc * jnp.exp2((old - m) * LOG2E)

            def step(c, acc):
                p = jnp.exp2((score(c) - m) * LOG2E).astype(BF16)
                v = vals[h, :, pl.ds(pl.multiple_of(c * n, n), n)]
                return acc + jnp.dot(v, p, preferred_element_type=F32)

            acc = lax.fori_loop(0, total // n, step, acc)
        else:
            for c in range(0, total, block_k):
                n = min(block_k, total - c)
                s = jnp.dot(keys[h, c : c + n, :], qt, preferred_element_type=F32)
                p = jnp.exp2(s * LOG2E).astype(BF16)
                t = jnp.dot(vals[h, :, c : c + n], p, preferred_element_type=F32)
                acc = t if acc is None else acc + t
        if last:
            out = (acc[0:HD] / acc[HD : HD + 1]).astype(BF16)
            for b in range(per):
                o_refs[start + b][rows, :] = out[:, b * tok : (b + 1) * tok]
        else:
            o_refs[0][h, 0 : HD + ONES, cols] = acc
            o_refs[0][h, HD + ONES :, cols] = jnp.broadcast_to(m, (8, block_q))

    def run(safe):
        for start in range(0, tiles, per):
            lax.fori_loop(0, heads, lambda h, _: (block(h, start, safe), 0)[1], 0)

    @pl.when(small)
    def _():
        run(False)

    @pl.when(jnp.logical_not(small))
    def _():
        run(True)


def attention(length, where, chunks, kvs, state=None, caption=(), block_q=512):
    inner, tok = chunks[0].shape[0] // 3, chunks[0].shape[1]
    heads = inner // HD
    tiles = len(chunks)
    first, last = state is None, bool(caption)
    blocks = sum(x.shape[0] // (2 * inner) for x in kvs) + (tiles if first else 0)
    total = blocks * tok + (caption[0].shape[1] if last else 0)
    smem = pl.BlockSpec(memory_space=pltpu.SMEM)
    vm = pl.BlockSpec(memory_space=pltpu.VMEM)
    operands = (*chunks, *kvs, *(() if first else (state,)), *caption)
    if last:
        out_shape = (jax.ShapeDtypeStruct((inner, tok), BF16),) * tiles
    else:
        out_shape = (jax.ShapeDtypeStruct((heads, HD + ONES + 8, tiles * tok), F32),)
    return pl.pallas_call(
        functools.partial(
            attention_kernel,
            tiles=tiles,
            sources=len(kvs),
            first=first,
            last=last,
            block_q=block_q,
            block_k=total // 2,
        ),
        out_shape=out_shape,
        in_specs=[smem, smem] + [vm] * len(operands),
        out_specs=(vm,) * len(out_shape),
        scratch_shapes=[
            pltpu.VMEM((heads, total, HD), BF16),
            pltpu.VMEM((heads, HD + ONES, total), BF16),
        ]
        + ([pltpu.VMEM((2 * inner, tok), BF16)] if last else []),
        cost_estimate=pl.CostEstimate(
            flops=16 * tiles * tok * total * inner,
            transcendentals=tiles * tok * total * heads,
            bytes_accessed=2 * inner * (2 * total + 2 * tiles * tok),
        ),
        compiler_params=pltpu.CompilerParams(vmem_limit_bytes=VMEM_LIMIT),
        name="attention",
    )(length, where, *operands)


def grad_kernel(w_ref, sel_ref, *refs, tiles, part):
    o_refs, cot_refs, g_ref = refs[:tiles], refs[tiles:-1], refs[-1]
    width = cot_refs[0].shape[1]
    dp, pairs, chunk, _ = g_ref.shape
    rows = [
        pl.ds(pl.multiple_of((2 * s + sel_ref[0]) * part, 16), part) for s in range(pairs)
    ]
    left = jnp.concatenate(
        [jnp.concatenate([ref[r, :] for ref in o_refs], axis=1) for r in rows], axis=0
    )
    weight = w_ref[0]
    step = 2 * LANES
    for c in range(0, width, step):
        n = min(step, width - c)
        right = jnp.concatenate([ref[:, c : c + n] for ref in cot_refs], axis=0)
        g = (jnp.dot(left, right, preferred_element_type=F32) * weight).astype(BF16)
        for t in range(n // LANES):
            cols = slice(t * LANES, (t + 1) * LANES)
            for s in range(pairs):
                done = 0
                while done < part:
                    flat = (c // LANES + t) * part + done
                    count = min(part - done, chunk - flat % chunk)
                    g_ref[flat // chunk, s, flat % chunk : flat % chunk + count, :] = g[
                        s * part + done : s * part + done + count, cols
                    ]
                    done += count
    used = width // LANES * part - (dp - 1) * chunk
    if used < chunk:
        for s in range(pairs):
            g_ref[dp - 1, s, used:, :] = jnp.zeros((chunk - used, LANES), BF16)


def local_grad(weight, select, attended, cots, part, dp):
    inner, tok = attended[0].shape
    width = cots[0].shape[1]
    pairs = inner // (2 * part)
    chunk = -(-(width // LANES * part) // (dp * 16)) * 16
    vm = pl.BlockSpec(memory_space=pltpu.VMEM)
    smem = pl.BlockSpec(memory_space=pltpu.SMEM)
    tiles = len(attended)
    return pl.pallas_call(
        functools.partial(grad_kernel, tiles=tiles, part=part),
        out_shape=jax.ShapeDtypeStruct((dp, pairs, chunk, LANES), BF16),
        in_specs=[smem, smem] + [vm] * (tiles + len(cots)),
        out_specs=vm,
        cost_estimate=pl.CostEstimate(
            flops=tiles * tok * inner * width,
            transcendentals=0,
            bytes_accessed=2 * tiles * tok * (inner + width) + inner * width,
        ),
        compiler_params=pltpu.CompilerParams(vmem_limit_bytes=VMEM_LIMIT),
        name="local_grad",
    )(weight, select[None], *attended, *cots)


def adam_kernel(f_ref, at_ref, *refs):
    g_refs, refs, g_ref = refs[:4], refs[4:-1], refs[-1]
    chunk = g_refs[0].shape[1]
    for k, ref in enumerate(g_refs):
        for i in range(2):
            at = (at_ref[0] ^ i) * 4 + (at_ref[1] + 4 - k) % 4
            g_ref[pl.ds(pl.multiple_of(at * chunk, chunk), chunk), :] = ref[i]
    adam_rows(f_ref, g_ref, *refs)


def adam_rows(f_ref, g_ref, w_ref, mv_ref, ms_ref, vv_ref, vs_ref, nw, nmv, nms, nvv, nvs):
    rows, width = w_ref.shape
    factor = f_ref[0]
    diagonal = lax.broadcasted_iota(jnp.int32, (rows, rows), 0) == lax.broadcasted_iota(
        jnp.int32, (rows, rows), 1
    )

    def down(row):
        return jnp.sum(jnp.where(diagonal, row, 0.0), axis=1, keepdims=True)

    def across(column):
        return jnp.sum(jnp.where(diagonal, column, 0.0), axis=0, keepdims=True)

    for t in range(width // LANES):
        cols = slice(t * LANES, (t + 1) * LANES)
        one = slice(t, t + 1)
        g = g_ref[t * rows : (t + 1) * rows, :].astype(F32) * factor
        first = mv_ref[:, cols].astype(F32) * down(ms_ref[one, :])
        second = vv_ref[:, cols].astype(F32) * down(vs_ref[one, :])
        first = 0.9 * first + 0.1 * g
        second = 0.999 * second + 0.001 * g * g
        update = first / (1.0 - 0.9**10) / (jnp.sqrt(second / (1.0 - 0.999**10)) + 1e-08)
        nw[:, cols] = (w_ref[:, cols].astype(F32) - 0.02 * update).astype(BF16)
        fs = jnp.max(jnp.abs(first), axis=1, keepdims=True) + 1e-06
        ss = jnp.max(jnp.abs(second), axis=1, keepdims=True) + 1e-06
        nms[one, :] = across(fs)
        nvs[one, :] = across(ss)
        nmv[:, cols] = (first / fs).astype(BF16)
        nvv[:, cols] = (second / ss).astype(BF16)


def adam(factor, at, grads, out_weight, mom_val, mom_scale, var_val, var_scale):
    vm = pl.BlockSpec(memory_space=pltpu.VMEM)
    like = lambda a: jax.ShapeDtypeStruct(a.shape, a.dtype)
    mom_scale, var_scale = mom_scale.T, var_scale.T
    new_weight, first_val, first_scale, second_val, second_scale = pl.pallas_call(
        adam_kernel,
        out_shape=(like(out_weight), like(mom_val), like(mom_scale), like(var_val), like(var_scale)),
        in_specs=[pl.BlockSpec(memory_space=pltpu.SMEM)] * 2 + [vm] * 9,
        out_specs=(vm,) * 5,
        scratch_shapes=[pltpu.VMEM((8 * grads[0].shape[1], LANES), BF16)],
        compiler_params=pltpu.CompilerParams(vmem_limit_bytes=VMEM_LIMIT),
        name="adam",
    )(factor, at, *grads, out_weight, mom_val, mom_scale, var_val, var_scale)
    return new_weight, first_val, first_scale.T, second_val, second_scale.T


def swap(x, axis):
    return lax.ppermute(x, axis, [(0, 1), (1, 0)])


def shift(x, k):
    return lax.ppermute(x, "z", [(i, (i + k) % NT) for i in range(NT)])


def body(
    latent_q,
    latent_k,
    latent_v,
    caption_states,
    caption_proj,
    caption_len,
    timestep,
    out_cot,
    out_weight,
    mom_val,
    mom_scale,
    var_val,
    var_scale,
):
    tok, inner = latent_q.shape[1:]
    cap = caption_states.shape[1]
    xh, z, c = lax.axis_index("xh"), lax.axis_index("z"), lax.axis_index("c")

    *chunks, own = stage(z, latent_k[0], latent_v[0], latent_q[0])
    chunks = [chunks[0]] + [shift(chunks[k], k) for k in range(1, NT)]
    near = [swap(own, "c")]
    far = [swap(own, "xh")]

    states = lax.optimization_barrier((caption_states[0], own))[0]
    partial = lax.dot_general(
        caption_proj, states, (((0,), (1,)), ((), ())), preferred_element_type=F32
    ).astype(BF16)
    pieces = partial.reshape(2 * NT, 2, 2 * inner // (4 * NT), cap)
    take = lambda i: lax.dynamic_index_in_dim(pieces, i, 1, keepdims=False)
    pieces = (take(c).astype(F32) + swap(take(1 - c), "c").astype(F32)).astype(BF16)

    pieces = lax.all_to_all(pieces, ("xh", "z"), 0, 0, tiled=True)
    cap_own = jnp.sum(pieces.astype(F32), axis=0).astype(BF16)
    held = lax.optimization_barrier((cap_own, *near, *far, out_cot[0], *chunks[1:]))
    cap_own, near, far, cot = held[0], [held[1]], [held[2]], held[3]
    chunks = [chunks[0], *held[4:]]

    others = jnp.concatenate([x[: 2 * inner // NT] for x in chunks[1:]] + [cap_own], axis=0)
    near = near + [swap(others, "c")]
    far = far + [swap(others, "xh")]

    half = tok // 2
    before, after = shift(cot, 1), shift(cot, -1)

    where = jnp.stack([xh, c])
    (state,) = attention(caption_len, where, chunks, near)
    state, *far = lax.optimization_barrier((state, *far))
    last = [swap(x, "c") for x in far]
    (state,) = attention(caption_len, where, chunks, far, state)
    before, after, state = lax.optimization_barrier((before, after, state))
    caption = (cap_own, near[1], far[1], last[1])
    attended = attention(caption_len, where, chunks, last, state, caption)
    cots = [cot, before, shift(before[:half], 1), shift(after[half:], -1), after]
    back = [attended[0]] + [shift(attended[k], -k) for k in range(1, NT)]

    loss_weight = 1.0 + 3.0 * (timestep.astype(F32) + 0.5) / 1000.0
    rows = out_weight.shape[0]
    dp = lax.axis_size("xl") * lax.axis_size("y")
    other = swap(local_grad(loss_weight, 1 - c, attended, cots, rows, dp), "c")
    grad = local_grad(loss_weight, c, attended, cots, rows, dp)
    grad = (grad.astype(F32) + other.astype(F32)).astype(BF16)
    chunk = grad.shape[2]
    grad = lax.all_to_all(
        grad.reshape(2 * dp, chunk, LANES), ("xl", "y", "xh"), 0, 0, tiled=True
    )
    grad, *back = lax.optimization_barrier((grad, *back))
    grad = jnp.sum(grad.astype(F32), axis=0).astype(BF16)
    square = jnp.sum(jnp.square(grad.astype(F32)))
    perm = [
        (s * NT + i, (i // 2) * NT + 2 * (i % 2) + s) for s in range(2) for i in range(NT)
    ]
    grad = lax.ppermute(grad, ("xh", "z"), perm)
    everyone = ("xl", "y", "xh", "z", "c")
    squares = lax.all_to_all(
        jnp.broadcast_to(square, (lax.axis_size(everyone), LANES)), everyone, 0, 0, tiled=True
    )
    factor = 256.0 / jnp.sqrt(jnp.sum(squares[:, 0]) + 1e-06)
    grad = jnp.stack([grad, swap(grad, "xl")])
    grads = [grad] + [
        lax.ppermute(grad, "y", [(i, (i + k) % 4) for i in range(4)]) for k in range(1, 4)
    ]
    at = jnp.stack([lax.axis_index("xl"), lax.axis_index("y")])
    attn_out = unstage(z, back)[None]
    updated = adam(factor[None], at, grads, out_weight, mom_val, mom_scale, var_val, var_scale)
    return (attn_out, *updated)


def solution(mesh):
    fine = Mesh(mesh.devices.reshape(2, 4, 2, NT, 2), ("xl", "y", "xh", "z", "c"))
    dp = ("xl", "y")
    ctx = ("xh", "z", "c")
    tokens = P(dp, ctx, None)
    rows = P(ctx, None)
    return jax.shard_map(
        body,
        mesh=fine,
        in_specs=(
            tokens,
            tokens,
            tokens,
            P(dp, None, ctx),
            rows,
            P(dp),
            P(dp),
            tokens,
            rows,
            rows,
            rows,
            rows,
            rows,
        ),
        out_specs=(tokens, rows, rows, rows, rows, rows),
        check_vma=False,
    )
```

```python
import functools
import math

import jax
import jax.numpy as jnp
from jax import lax
from jax.experimental import pallas as pl
from jax.experimental.pallas import tpu as pltpu
from jax.sharding import Mesh, PartitionSpec as P

HD = 64
LANES = 128
ONES = 16
LOG2E = math.log2(math.e)
SAFE_BOUND = 60.0
F32 = jnp.float32
BF16 = jnp.bfloat16
NT = 4
VMEM_LIMIT = 20 * 2**20
SMALL_LIMIT = 10 * 2**20


def head_norms(x, heads):
    x = x.astype(F32)
    x = x * x
    rows = [jnp.sum(x[h * HD : (h + 1) * HD], axis=0, keepdims=True) for h in range(heads)]
    return jnp.max(jnp.concatenate(rows, axis=0), axis=1, keepdims=True)


def rel_rows(z_ref, k, group):
    return pl.ds(pl.multiple_of((z_ref[0] + k) % NT * group, group), group)


def stage_kv_kernel(z_ref, k_ref, v_ref, *refs):
    o_refs, scratch = refs[:NT], refs[NT]
    inner = scratch.shape[0]
    group = inner // NT
    for a, x_ref in enumerate((k_ref, v_ref)):
        for c in range(0, inner, LANES):
            scratch[c : c + LANES, :] = x_ref[:, c : c + LANES].T
        for k in range(NT):
            o_refs[k][a * group : (a + 1) * group, :] = scratch[rel_rows(z_ref, k, group), :]


def stage_kv(z, keys, values):
    tok, inner = keys.shape
    vm = pl.BlockSpec(memory_space=pltpu.VMEM)
    shape = jax.ShapeDtypeStruct((2 * inner // NT, tok), BF16)
    return pl.pallas_call(
        stage_kv_kernel,
        out_shape=(shape,) * NT,
        in_specs=[pl.BlockSpec(memory_space=pltpu.SMEM), vm, vm],
        out_specs=(vm,) * NT,
        scratch_shapes=[pltpu.VMEM((inner, tok), BF16)],
        cost_estimate=pl.CostEstimate(flops=0, transcendentals=0, bytes_accessed=8 * tok * inner),
        compiler_params=pltpu.CompilerParams(vmem_limit_bytes=SMALL_LIMIT),
        name="stage_kv",
    )(z[None], keys, values)


def caption_kernel(z_ref, c_ref, proj_ref, states_ref, keep_ref, send_ref, scratch):
    scratch[...] = lax.dot_general(
        proj_ref[...], states_ref[...], (((0,), (1,)), ((), ())), preferred_element_type=F32
    ).astype(BF16)
    inner = scratch.shape[0] // 2
    half = inner // (2 * NT)
    for o_ref, core in ((keep_ref, c_ref[0]), (send_ref, 1 - c_ref[0])):
        for k in range(NT):
            for a in range(2):
                start = a * inner + ((z_ref[0] + k) % NT * 2 + core) * half
                at = (2 * k + a) * half
                o_ref[at : at + half, :] = scratch[pl.ds(pl.multiple_of(start, half), half), :]


def caption_partial(z, c, proj, states):
    features, width = proj.shape
    cap = states.shape[0]
    vm = pl.BlockSpec(memory_space=pltpu.VMEM)
    smem = pl.BlockSpec(memory_space=pltpu.SMEM)
    shape = jax.ShapeDtypeStruct((width // 2, cap), BF16)
    return pl.pallas_call(
        caption_kernel,
        out_shape=(shape, shape),
        in_specs=[smem, smem, vm, vm],
        out_specs=(vm, vm),
        scratch_shapes=[pltpu.VMEM((width, cap), BF16)],
        cost_estimate=pl.CostEstimate(
            flops=2 * width * cap * features, transcendentals=0, bytes_accessed=4 * width * cap
        ),
        compiler_params=pltpu.CompilerParams(vmem_limit_bytes=SMALL_LIMIT),
        name="caption_partial",
    )(z[None], c[None], proj, states)


def stage_q_kernel(z_ref, q_ref, keep_ref, other_ref, *refs):
    o_refs, scratch = refs[:NT], refs[NT]
    inner = scratch.shape[0]
    group = inner // NT
    for c in range(0, inner, LANES):
        scratch[c : c + LANES, :] = q_ref[:, c : c + LANES].T
    for k in range(NT):
        rows = slice(k * group, (k + 1) * group)
        o_refs[k][0:group, :] = scratch[rel_rows(z_ref, k, group), :]
        both = keep_ref[rows, :].astype(F32) + other_ref[rows, :].astype(F32)
        o_refs[k][group:, :] = both.astype(BF16)


def stage_q(z, queries, keep, other):
    tok, inner = queries.shape
    vm = pl.BlockSpec(memory_space=pltpu.VMEM)
    shape = jax.ShapeDtypeStruct((2 * inner // NT, tok), BF16)
    return pl.pallas_call(
        stage_q_kernel,
        out_shape=(shape,) * NT,
        in_specs=[pl.BlockSpec(memory_space=pltpu.SMEM), vm, vm, vm],
        out_specs=(vm,) * NT,
        scratch_shapes=[pltpu.VMEM((inner, tok), BF16)],
        cost_estimate=pl.CostEstimate(flops=0, transcendentals=0, bytes_accessed=8 * tok * inner),
        compiler_params=pltpu.CompilerParams(vmem_limit_bytes=SMALL_LIMIT),
        name="stage_q",
    )(z[None], queries, keep, other)


def caption_sum_kernel(*refs):
    group = refs[-1].shape[0]
    total = refs[0][group:, :].astype(F32)
    for ref in refs[1:-1]:
        total = total + ref[group:, :].astype(F32)
    refs[-1][...] = total.astype(BF16)


def caption_sum(chunks):
    rows, cap = chunks[0].shape
    vm = pl.BlockSpec(memory_space=pltpu.VMEM)
    return pl.pallas_call(
        caption_sum_kernel,
        out_shape=jax.ShapeDtypeStruct((rows // 2, cap), BF16),
        in_specs=[vm] * len(chunks),
        out_specs=vm,
        compiler_params=pltpu.CompilerParams(vmem_limit_bytes=SMALL_LIMIT),
        name="caption_sum",
    )(*chunks)


def unstage_kernel(z_ref, *refs):
    x_refs, o_ref, scratch = refs[:NT], refs[NT], refs[NT + 1]
    group = x_refs[0].shape[0]
    for k in range(NT):
        start = pl.multiple_of((z_ref[0] + k) % NT * group, group)
        scratch[pl.ds(start, group), :] = x_refs[k][...]
    for c in range(0, NT * group, LANES):
        o_ref[:, c : c + LANES] = scratch[c : c + LANES, :].T


def unstage(z, pieces):
    group, tok = pieces[0].shape
    vm = pl.BlockSpec(memory_space=pltpu.VMEM)
    return pl.pallas_call(
        unstage_kernel,
        out_shape=jax.ShapeDtypeStruct((tok, NT * group), BF16),
        in_specs=[pl.BlockSpec(memory_space=pltpu.SMEM)] + [vm] * NT,
        out_specs=vm,
        scratch_shapes=[pltpu.VMEM((NT * group, tok), BF16)],
        compiler_params=pltpu.CompilerParams(vmem_limit_bytes=VMEM_LIMIT),
        name="unstage",
    )(z[None], *pieces)


def attention_kernel(len_ref, core_ref, *refs, tiles, sources, first, last, block_q, block_k):
    q_refs, refs = refs[:tiles], refs[tiles:]
    kv_refs, refs = refs[:sources], refs[sources:]
    old_ref = None
    if not first:
        old_ref, refs = refs[0], refs[1:]
    if last:
        piece_refs, refs = refs[:4], refs[4:]
        refs, cap_ref = refs[:-1], refs[-1]
        half = cap_ref.shape[0] // 4
        for flip in range(2):
            rows = piece_refs[flip][...].astype(F32) + piece_refs[2 + flip][...].astype(F32)
            rows = rows.astype(BF16)
            for a in range(2):
                start = pl.multiple_of((2 * a + (core_ref[0] ^ flip)) * half, half)
                cap_ref[pl.ds(start, half), :] = rows[a * half : (a + 1) * half]
    o_refs, (keys, vals) = refs[:-2], refs[-2:]
    inner, tok = q_refs[0].shape[0] // 2, q_refs[0].shape[1]
    heads = inner // HD
    total = keys.shape[1]
    cap = cap_ref.shape[1] if last else 0
    length = len_ref[0]
    pairs = [(ref[0:inner, :], ref[inner:, :]) for ref in kv_refs]

    def place(col, k, v, kept):
        n = k.shape[1]
        for h in range(heads):
            keys[h, col : col + n, :] = k[h * HD : (h + 1) * HD].T
            vh = v[h * HD : (h + 1) * HD]
            one = jnp.ones((ONES, n), BF16)
            if kept is not None:
                vh = jnp.where(kept, vh, BF16(0))
                one = jnp.where(kept, one, BF16(0))
            vals[h, 0:HD, col : col + n] = vh
            vals[h, HD : HD + ONES, col : col + n] = one

    kmax = None
    for b, (k, v) in enumerate(pairs):
        place(b * tok, k, v, None)
        norms = head_norms(k, heads)
        kmax = norms if kmax is None else jnp.maximum(kmax, norms)
    if last:
        kept = lax.broadcasted_iota(jnp.int32, (1, cap), 1) < length
        ck = cap_ref[0:inner, :]
        place(len(pairs) * tok, ck, cap_ref[inner : 2 * inner, :], kept)
        kmax = jnp.maximum(kmax, head_norms(ck, heads))
    qmax = None
    for ref in q_refs:
        norms = head_norms(ref[0:inner, :], heads)
        qmax = norms if qmax is None else jnp.maximum(qmax, norms)
    small = jnp.max(qmax * kmax) < HD * SAFE_BOUND * SAFE_BOUND
    if not first:
        offset = jnp.max(jnp.abs(old_ref[0, HD + ONES :, :]))
        for h in range(1, heads):
            offset = jnp.maximum(offset, jnp.max(jnp.abs(old_ref[h, HD + ONES :, :])))
        small = jnp.logical_and(small, offset == 0.0)

    per = block_q // tok

    def block(h, start, safe):
        rows = pl.ds(pl.multiple_of(h * HD, HD), HD)
        cols = slice(start * tok, start * tok + block_q)
        qt = jnp.concatenate([q_refs[start + b][rows, :] for b in range(per)], axis=1)
        qt = qt * BF16(0.125)
        acc = None if first else old_ref[h, 0 : HD + ONES, cols]
        m = jnp.zeros((8, block_q), F32)
        if safe:
            n = tok

            def score(c):
                s0 = pl.multiple_of(c * n, n)
                s = jnp.dot(keys[h, pl.ds(s0, n), :], qt, preferred_element_type=F32)
                if not last:
                    return s
                key = lax.broadcasted_iota(jnp.int32, (n, 1), 0) + s0
                return jnp.where(key < total - cap + length, s, -1e30)

            def peak(c, m):
                return jnp.maximum(m, jnp.max(score(c), axis=0, keepdims=True))

            old = jnp.full((1, block_q), -1e30, F32)
            if not first:
                old = old_ref[h, HD + ONES : HD + ONES + 1, cols]
            m = lax.fori_loop(0, total // n, peak, old)
            if first:
                acc = jnp.zeros((HD + ONES, block_q), F32)
            else:
                acc = acc * jnp.exp2((old - m) * LOG2E)

            def step(c, acc):
                p = jnp.exp2((score(c) - m) * LOG2E).astype(BF16)
                v = vals[h, :, pl.ds(pl.multiple_of(c * n, n), n)]
                return acc + jnp.dot(v, p, preferred_element_type=F32)

            acc = lax.fori_loop(0, total // n, step, acc)
        else:
            for c in range(0, total, block_k):
                n = min(block_k, total - c)
                s = jnp.dot(keys[h, c : c + n, :], qt, preferred_element_type=F32)
                p = jnp.exp2(s * LOG2E).astype(BF16)
                t = jnp.dot(vals[h, :, c : c + n], p, preferred_element_type=F32)
                acc = t if acc is None else acc + t
        if last:
            out = (acc[0:HD] / acc[HD : HD + 1]).astype(BF16)
            for b in range(per):
                o_refs[start + b][rows, :] = out[:, b * tok : (b + 1) * tok]
        else:
            o_refs[0][h, 0 : HD + ONES, cols] = acc
            o_refs[0][h, HD + ONES :, cols] = jnp.broadcast_to(m, (8, block_q))

    def run(safe):
        for start in range(0, tiles, per):
            lax.fori_loop(0, heads, lambda h, _: (block(h, start, safe), 0)[1], 0)

    @pl.when(small)
    def _():
        run(False)

    @pl.when(jnp.logical_not(small))
    def _():
        run(True)


def attention(length, core, queries, kvs, state=None, caption=(), block_q=512):
    inner, tok = queries[0].shape[0] // 2, queries[0].shape[1]
    heads = inner // HD
    tiles = len(queries)
    first, last = state is None, bool(caption)
    blocks = len(kvs)
    total = blocks * tok + (caption[0].shape[1] if last else 0)
    smem = pl.BlockSpec(memory_space=pltpu.SMEM)
    vm = pl.BlockSpec(memory_space=pltpu.VMEM)
    operands = (*queries, *kvs, *(() if first else (state,)), *caption)
    if last:
        out_shape = (jax.ShapeDtypeStruct((inner, tok), BF16),) * tiles
    else:
        out_shape = (jax.ShapeDtypeStruct((heads, HD + ONES + 8, tiles * tok), F32),)
    return pl.pallas_call(
        functools.partial(
            attention_kernel,
            tiles=tiles,
            sources=len(kvs),
            first=first,
            last=last,
            block_q=block_q,
            block_k=total // 2,
        ),
        out_shape=out_shape,
        in_specs=[smem, smem] + [vm] * len(operands),
        out_specs=(vm,) * len(out_shape),
        scratch_shapes=[
            pltpu.VMEM((heads, total, HD), BF16),
            pltpu.VMEM((heads, HD + ONES, total), BF16),
        ]
        + ([pltpu.VMEM((2 * inner, tok), BF16)] if last else []),
        cost_estimate=pl.CostEstimate(
            flops=16 * tiles * tok * total * inner,
            transcendentals=tiles * tok * total * heads,
            bytes_accessed=2 * inner * (2 * total + 2 * tiles * tok),
        ),
        compiler_params=pltpu.CompilerParams(vmem_limit_bytes=VMEM_LIMIT),
        name="attention",
    )(length, core[None], *operands)


def grad_kernel(w_ref, sel_ref, *refs, tiles, part):
    o_refs, cot_refs, g_ref = refs[:tiles], refs[tiles:-1], refs[-1]
    width = cot_refs[0].shape[1]
    dp, pairs, chunk, _ = g_ref.shape
    rows = [
        pl.ds(pl.multiple_of((2 * s + sel_ref[0]) * part, 16), part) for s in range(pairs)
    ]
    left = jnp.concatenate(
        [jnp.concatenate([ref[r, :] for ref in o_refs], axis=1) for r in rows], axis=0
    )
    weight = w_ref[0]
    step = 2 * LANES
    for c in range(0, width, step):
        n = min(step, width - c)
        right = jnp.concatenate([ref[:, c : c + n] for ref in cot_refs], axis=0)
        g = (jnp.dot(left, right, preferred_element_type=F32) * weight).astype(BF16)
        for t in range(n // LANES):
            cols = slice(t * LANES, (t + 1) * LANES)
            for s in range(pairs):
                done = 0
                while done < part:
                    flat = (c // LANES + t) * part + done
                    count = min(part - done, chunk - flat % chunk)
                    g_ref[flat // chunk, s, flat % chunk : flat % chunk + count, :] = g[
                        s * part + done : s * part + done + count, cols
                    ]
                    done += count
    used = width // LANES * part - (dp - 1) * chunk
    if used < chunk:
        for s in range(pairs):
            g_ref[dp - 1, s, used:, :] = jnp.zeros((chunk - used, LANES), BF16)


def local_grad(weight, select, attended, cots, part, dp):
    inner, tok = attended[0].shape
    width = cots[0].shape[1]
    pairs = inner // (2 * part)
    chunk = -(-(width // LANES * part) // (dp * 16)) * 16
    vm = pl.BlockSpec(memory_space=pltpu.VMEM)
    smem = pl.BlockSpec(memory_space=pltpu.SMEM)
    tiles = len(attended)
    return pl.pallas_call(
        functools.partial(grad_kernel, tiles=tiles, part=part),
        out_shape=jax.ShapeDtypeStruct((dp, pairs, chunk, LANES), BF16),
        in_specs=[smem, smem] + [vm] * (tiles + len(cots)),
        out_specs=vm,
        cost_estimate=pl.CostEstimate(
            flops=tiles * tok * inner * width,
            transcendentals=0,
            bytes_accessed=2 * tiles * tok * (inner + width) + inner * width,
        ),
        compiler_params=pltpu.CompilerParams(vmem_limit_bytes=VMEM_LIMIT),
        name="local_grad",
    )(weight, select[None], *attended, *cots)


def adam_kernel(f_ref, at_ref, *refs):
    g_refs, refs, g_ref = refs[:8], refs[8:-1], refs[-1]
    chunk = g_refs[0].shape[0]
    for k, ref in enumerate(g_refs):
        at = (at_ref[0] ^ (k // 4)) * 4 + (at_ref[1] + 4 - k % 4) % 4
        g_ref[pl.ds(pl.multiple_of(at * chunk, chunk), chunk), :] = ref[...]
    adam_rows(f_ref, g_ref, *refs)


def adam_rows(f_ref, g_ref, w_ref, mv_ref, ms_ref, vv_ref, vs_ref, nw, nmv, nms, nvv, nvs):
    rows, width = w_ref.shape
    factor = f_ref[0]
    diagonal = lax.broadcasted_iota(jnp.int32, (rows, rows), 0) == lax.broadcasted_iota(
        jnp.int32, (rows, rows), 1
    )

    def down(row):
        return jnp.sum(jnp.where(diagonal, row, 0.0), axis=1, keepdims=True)

    def across(column):
        return jnp.sum(jnp.where(diagonal, column, 0.0), axis=0, keepdims=True)

    for t in range(width // LANES):
        cols = slice(t * LANES, (t + 1) * LANES)
        one = slice(t, t + 1)
        g = g_ref[t * rows : (t + 1) * rows, :].astype(F32) * factor
        first = mv_ref[:, cols].astype(F32) * down(ms_ref[one, :])
        second = vv_ref[:, cols].astype(F32) * down(vs_ref[one, :])
        first = 0.9 * first + 0.1 * g
        second = 0.999 * second + 0.001 * g * g
        update = first / (1.0 - 0.9**10) / (jnp.sqrt(second / (1.0 - 0.999**10)) + 1e-08)
        nw[:, cols] = (w_ref[:, cols].astype(F32) - 0.02 * update).astype(BF16)
        fs = jnp.max(jnp.abs(first), axis=1, keepdims=True) + 1e-06
        ss = jnp.max(jnp.abs(second), axis=1, keepdims=True) + 1e-06
        nms[one, :] = across(fs)
        nvs[one, :] = across(ss)
        nmv[:, cols] = (first / fs).astype(BF16)
        nvv[:, cols] = (second / ss).astype(BF16)


def adam(factor, at, grads, out_weight, mom_val, mom_scale, var_val, var_scale):
    vm = pl.BlockSpec(memory_space=pltpu.VMEM)
    like = lambda a: jax.ShapeDtypeStruct(a.shape, a.dtype)
    mom_scale, var_scale = mom_scale.T, var_scale.T
    new_weight, first_val, first_scale, second_val, second_scale = pl.pallas_call(
        adam_kernel,
        out_shape=(like(out_weight), like(mom_val), like(mom_scale), like(var_val), like(var_scale)),
        in_specs=[pl.BlockSpec(memory_space=pltpu.SMEM)] * 2 + [vm] * 13,
        out_specs=(vm,) * 5,
        scratch_shapes=[pltpu.VMEM((8 * grads[0].shape[0], LANES), BF16)],
        compiler_params=pltpu.CompilerParams(vmem_limit_bytes=VMEM_LIMIT),
        name="adam",
    )(factor, at, *grads, out_weight, mom_val, mom_scale, var_val, var_scale)
    return new_weight, first_val, first_scale.T, second_val, second_scale.T


def swap(x, axis):
    return lax.ppermute(x, axis, [(0, 1), (1, 0)])


def shift(x, k):
    return lax.ppermute(x, "z", [(i, (i + k) % NT) for i in range(NT)])


def body(
    latent_q,
    latent_k,
    latent_v,
    caption_states,
    caption_proj,
    caption_len,
    timestep,
    out_cot,
    out_weight,
    mom_val,
    mom_scale,
    var_val,
    var_scale,
):
    tok, inner = latent_q.shape[1:]
    cap = caption_states.shape[1]
    xh, z, c = lax.axis_index("xh"), lax.axis_index("z"), lax.axis_index("c")

    own = stage_kv(z, latent_k[0], latent_v[0])
    kvs = [own[0]] + [shift(own[k], k) for k in range(1, NT)]
    near, far = [swap(own[0], "c")], [swap(own[0], "xh")]

    states = lax.optimization_barrier((caption_states[0], own[0]))[0]
    keep, send = caption_partial(z, c, caption_proj, states)
    other = swap(send, "c")
    staged = stage_q(z, latent_q[0], keep, other)
    queries = [staged[0]] + [shift(staged[k], k) for k in range(1, NT)]

    near0, far0, *rest = lax.optimization_barrier((near[0], far[0], *kvs[1:], *staged[1:]))
    kvs = [kvs[0], *rest[: NT - 1]]
    near = [near0] + [swap(x, "c") for x in kvs[1:]]
    far = [far0] + [swap(x, "xh") for x in kvs[1:]]

    cot, *rest = lax.optimization_barrier((out_cot[0], *queries[1:]))
    queries = [queries[0], *rest]
    half = tok // 2
    before, after = shift(cot, 1), shift(cot, -1)
    caption = [caption_sum(queries)]
    caption = caption + [swap(caption[0], "c"), swap(caption[0], "xh")]

    (state,) = attention(caption_len, c, queries, kvs + near)
    state, caption[2], *far = lax.optimization_barrier((state, caption[2], *far))
    last = [swap(x, "c") for x in far]
    caption = caption + [swap(caption[2], "c")]
    (state,) = attention(caption_len, c, queries, far, state)
    before, after, state = lax.optimization_barrier((before, after, state))
    attended = attention(caption_len, c, queries, last, state, caption)
    cots = [cot, before, shift(before[:half], 1), shift(after[half:], -1), after]
    back = [attended[0]] + [shift(attended[k], -k) for k in range(1, NT)]

    loss_weight = 1.0 + 3.0 * (timestep.astype(F32) + 0.5) / 1000.0
    rows = out_weight.shape[0]
    dp = lax.axis_size("xl") * lax.axis_size("y")
    other = swap(local_grad(loss_weight, 1 - c, attended, cots, rows, dp), "c")
    grad = local_grad(loss_weight, c, attended, cots, rows, dp)
    grad = (grad.astype(F32) + other.astype(F32)).astype(BF16)
    chunk = grad.shape[2]
    grad = lax.all_to_all(
        grad.reshape(2 * dp, chunk, LANES), ("xl", "y", "xh"), 0, 0, tiled=True
    )
    grad = jnp.sum(grad.astype(F32), axis=0).astype(BF16)
    square = jnp.sum(jnp.square(grad.astype(F32)))
    grads = []
    for k in range(dp):
        perm = []
        for i in range(dp * 2 * NT):
            xl, y, s, t = i // (8 * NT), i // (2 * NT) % 4, i // NT % 2, i % NT
            peer = (xl ^ (k // 4)) * 4 + (y + k) % 4
            perm.append((i, peer * 2 * NT + t // 2 * NT + t % 2 * 2 + s))
        grads.append(lax.ppermute(grad, ("xl", "y", "xh", "z"), perm))
    everyone = ("xl", "y", "xh", "z", "c")
    squares = lax.all_to_all(
        jnp.broadcast_to(square, (lax.axis_size(everyone), LANES)), everyone, 0, 0, tiled=True
    )
    squares, *back = lax.optimization_barrier((squares, *back))
    factor = 256.0 / jnp.sqrt(jnp.sum(squares[:, 0]) + 1e-06)
    at = jnp.stack([lax.axis_index("xl"), lax.axis_index("y")])
    attn_out = unstage(z, back)[None]
    updated = adam(factor[None], at, grads, out_weight, mom_val, mom_scale, var_val, var_scale)
    return (attn_out, *updated)


def solution(mesh):
    fine = Mesh(mesh.devices.reshape(2, 4, 2, NT, 2), ("xl", "y", "xh", "z", "c"))
    dp = ("xl", "y")
    ctx = ("xh", "z", "c")
    tokens = P(dp, ctx, None)
    rows = P(ctx, None)
    return jax.shard_map(
        body,
        mesh=fine,
        in_specs=(
            tokens,
            tokens,
            tokens,
            P(dp, None, ctx),
            rows,
            P(dp),
            P(dp),
            tokens,
            rows,
            rows,
            rows,
            rows,
            rows,
        ),
        out_specs=(tokens, rows, rows, rows, rows, rows),
        check_vma=False,
    )
```

```python
import functools
import math

import jax
import jax.numpy as jnp
from jax import lax
from jax.experimental import pallas as pl
from jax.experimental.pallas import tpu as pltpu
from jax.sharding import Mesh, PartitionSpec as P

HD = 64
LANES = 128
ONES = 16
LOG2E = math.log2(math.e)
SAFE_BOUND = 60.0
F32 = jnp.float32
BF16 = jnp.bfloat16
NT = 4
VMEM_LIMIT = 20 * 2**20
SMALL_LIMIT = 10 * 2**20


def head_norms(x, heads):
    x = x.astype(F32)
    x = x * x
    rows = [jnp.sum(x[h * HD : (h + 1) * HD], axis=0, keepdims=True) for h in range(heads)]
    return jnp.max(jnp.concatenate(rows, axis=0), axis=1, keepdims=True)


def rel_rows(z_ref, k, group):
    return pl.ds(pl.multiple_of((z_ref[0] + k) % NT * group, group), group)


def stage_kv_kernel(z_ref, k_ref, v_ref, *refs):
    o_refs, scratch = refs[:NT], refs[NT]
    inner = scratch.shape[0]
    group = inner // NT
    for a, x_ref in enumerate((k_ref, v_ref)):
        for c in range(0, inner, LANES):
            scratch[c : c + LANES, :] = x_ref[:, c : c + LANES].T
        for k in range(NT):
            o_refs[k][a * group : (a + 1) * group, :] = scratch[rel_rows(z_ref, k, group), :]


def stage_kv(z, keys, values):
    tok, inner = keys.shape
    vm = pl.BlockSpec(memory_space=pltpu.VMEM)
    shape = jax.ShapeDtypeStruct((2 * inner // NT, tok), BF16)
    return pl.pallas_call(
        stage_kv_kernel,
        out_shape=(shape,) * NT,
        in_specs=[pl.BlockSpec(memory_space=pltpu.SMEM), vm, vm],
        out_specs=(vm,) * NT,
        scratch_shapes=[pltpu.VMEM((inner, tok), BF16)],
        cost_estimate=pl.CostEstimate(flops=0, transcendentals=0, bytes_accessed=8 * tok * inner),
        compiler_params=pltpu.CompilerParams(vmem_limit_bytes=SMALL_LIMIT),
        name="stage_kv",
    )(z[None], keys, values)


def caption_kernel(z_ref, c_ref, proj_ref, states_ref, keep_ref, send_ref, scratch):
    scratch[...] = lax.dot_general(
        proj_ref[...], states_ref[...], (((0,), (1,)), ((), ())), preferred_element_type=F32
    ).astype(BF16)
    inner = scratch.shape[0] // 2
    half = inner // (2 * NT)
    for o_ref, core in ((keep_ref, c_ref[0]), (send_ref, 1 - c_ref[0])):
        for k in range(NT):
            for a in range(2):
                start = a * inner + ((z_ref[0] + k) % NT * 2 + core) * half
                at = (2 * k + a) * half
                o_ref[at : at + half, :] = scratch[pl.ds(pl.multiple_of(start, half), half), :]


def caption_partial(z, c, proj, states):
    features, width = proj.shape
    cap = states.shape[0]
    vm = pl.BlockSpec(memory_space=pltpu.VMEM)
    smem = pl.BlockSpec(memory_space=pltpu.SMEM)
    shape = jax.ShapeDtypeStruct((width // 2, cap), BF16)
    return pl.pallas_call(
        caption_kernel,
        out_shape=(shape, shape),
        in_specs=[smem, smem, vm, vm],
        out_specs=(vm, vm),
        scratch_shapes=[pltpu.VMEM((width, cap), BF16)],
        cost_estimate=pl.CostEstimate(
            flops=2 * width * cap * features, transcendentals=0, bytes_accessed=4 * width * cap
        ),
        compiler_params=pltpu.CompilerParams(vmem_limit_bytes=SMALL_LIMIT),
        name="caption_partial",
    )(z[None], c[None], proj, states)


def stage_q_kernel(z_ref, q_ref, keep_ref, other_ref, *refs):
    o_refs, scratch = refs[:NT], refs[NT]
    inner = scratch.shape[0]
    group = inner // NT
    for c in range(0, inner, LANES):
        scratch[c : c + LANES, :] = q_ref[:, c : c + LANES].T
    for k in range(NT):
        rows = slice(k * group, (k + 1) * group)
        o_refs[k][0:group, :] = scratch[rel_rows(z_ref, k, group), :]
        both = keep_ref[rows, :].astype(F32) + other_ref[rows, :].astype(F32)
        o_refs[k][group:, :] = both.astype(BF16)


def stage_q(z, queries, keep, other):
    tok, inner = queries.shape
    vm = pl.BlockSpec(memory_space=pltpu.VMEM)
    shape = jax.ShapeDtypeStruct((2 * inner // NT, tok), BF16)
    return pl.pallas_call(
        stage_q_kernel,
        out_shape=(shape,) * NT,
        in_specs=[pl.BlockSpec(memory_space=pltpu.SMEM), vm, vm, vm],
        out_specs=(vm,) * NT,
        scratch_shapes=[pltpu.VMEM((inner, tok), BF16)],
        cost_estimate=pl.CostEstimate(flops=0, transcendentals=0, bytes_accessed=8 * tok * inner),
        compiler_params=pltpu.CompilerParams(vmem_limit_bytes=SMALL_LIMIT),
        name="stage_q",
    )(z[None], queries, keep, other)


def caption_sum_kernel(*refs):
    group = refs[-1].shape[0]
    total = refs[0][group:, :].astype(F32)
    for ref in refs[1:-1]:
        total = total + ref[group:, :].astype(F32)
    refs[-1][...] = total.astype(BF16)


def caption_sum(chunks):
    rows, cap = chunks[0].shape
    vm = pl.BlockSpec(memory_space=pltpu.VMEM)
    return pl.pallas_call(
        caption_sum_kernel,
        out_shape=jax.ShapeDtypeStruct((rows // 2, cap), BF16),
        in_specs=[vm] * len(chunks),
        out_specs=vm,
        compiler_params=pltpu.CompilerParams(vmem_limit_bytes=SMALL_LIMIT),
        name="caption_sum",
    )(*chunks)


def unstage_kernel(z_ref, *refs):
    x_refs, o_ref, scratch = refs[:NT], refs[NT], refs[NT + 1]
    group = x_refs[0].shape[0]
    for k in range(NT):
        start = pl.multiple_of((z_ref[0] + k) % NT * group, group)
        scratch[pl.ds(start, group), :] = x_refs[k][...]
    for c in range(0, NT * group, LANES):
        o_ref[:, c : c + LANES] = scratch[c : c + LANES, :].T


def unstage(z, pieces):
    group, tok = pieces[0].shape
    vm = pl.BlockSpec(memory_space=pltpu.VMEM)
    return pl.pallas_call(
        unstage_kernel,
        out_shape=jax.ShapeDtypeStruct((tok, NT * group), BF16),
        in_specs=[pl.BlockSpec(memory_space=pltpu.SMEM)] + [vm] * NT,
        out_specs=vm,
        scratch_shapes=[pltpu.VMEM((NT * group, tok), BF16)],
        compiler_params=pltpu.CompilerParams(vmem_limit_bytes=VMEM_LIMIT),
        name="unstage",
    )(z[None], *pieces)


def attention_kernel(len_ref, core_ref, *refs, tiles, sources, first, last, block_q, block_k):
    q_refs, refs = refs[:tiles], refs[tiles:]
    kv_refs, refs = refs[:sources], refs[sources:]
    old_ref = None
    if not first:
        old_ref, refs = refs[0], refs[1:]
    if last:
        piece_refs, cap_ref, refs = refs[:4], refs[-6], refs[4:-6] + refs[-5:]
        half = cap_ref.shape[0] // 4
        for flip in range(2):
            rows = piece_refs[flip][...].astype(F32) + piece_refs[2 + flip][...].astype(F32)
            rows = rows.astype(BF16)
            for a in range(2):
                start = pl.multiple_of((2 * a + (core_ref[0] ^ flip)) * half, half)
                cap_ref[pl.ds(start, half), :] = rows[a * half : (a + 1) * half]
    o_refs, (keys, vals, held_q, held_kv, sems) = refs[:-5], refs[-5:]
    inner, tok = q_refs[0].shape[0] // 2, q_refs[0].shape[1]
    copies = [
        pltpu.make_async_copy(ref, held_kv.at[i], sems.at[i]) for i, ref in enumerate(kv_refs)
    ] + [
        pltpu.make_async_copy(ref.at[pl.ds(0, inner), :], held_q.at[i], sems.at[sources + i])
        for i, ref in enumerate(q_refs)
    ]
    for copy in copies:
        copy.start()
    heads = inner // HD
    total = keys.shape[1]
    cap = cap_ref.shape[1] if last else 0
    length = len_ref[0]
    def place(col, k, v, kept):
        n = k.shape[1]
        for h in range(heads):
            keys[h, col : col + n, :] = k[h * HD : (h + 1) * HD].T
            vh = v[h * HD : (h + 1) * HD]
            one = jnp.ones((ONES, n), BF16)
            if kept is not None:
                vh = jnp.where(kept, vh, BF16(0))
                one = jnp.where(kept, one, BF16(0))
            vals[h, 0:HD, col : col + n] = vh
            vals[h, HD : HD + ONES, col : col + n] = one

    kmax = None
    for b in range(sources):
        copies[b].wait()
        k = held_kv[b, 0:inner, :]
        place(b * tok, k, held_kv[b, inner:, :], None)
        norms = head_norms(k, heads)
        kmax = norms if kmax is None else jnp.maximum(kmax, norms)
    if last:
        kept = lax.broadcasted_iota(jnp.int32, (1, cap), 1) < length
        ck = cap_ref[0:inner, :]
        place(sources * tok, ck, cap_ref[inner : 2 * inner, :], kept)
        kmax = jnp.maximum(kmax, head_norms(ck, heads))
    qmax = None
    for i in range(tiles):
        copies[sources + i].wait()
        norms = head_norms(held_q[i], heads)
        qmax = norms if qmax is None else jnp.maximum(qmax, norms)
    small = jnp.max(qmax * kmax) < HD * SAFE_BOUND * SAFE_BOUND
    if not first:
        offset = jnp.max(jnp.abs(old_ref[0, HD + ONES :, :]))
        for h in range(1, heads):
            offset = jnp.maximum(offset, jnp.max(jnp.abs(old_ref[h, HD + ONES :, :])))
        small = jnp.logical_and(small, offset == 0.0)

    per = block_q // tok

    def block(h, start, safe):
        rows = pl.ds(pl.multiple_of(h * HD, HD), HD)
        cols = slice(start * tok, start * tok + block_q)
        qt = jnp.concatenate([held_q[start + b, rows, :] for b in range(per)], axis=1)
        qt = qt * BF16(0.125)
        acc = None if first else old_ref[h, 0 : HD + ONES, cols]
        m = jnp.zeros((8, block_q), F32)
        if safe:
            n = tok

            def score(c):
                s0 = pl.multiple_of(c * n, n)
                s = jnp.dot(keys[h, pl.ds(s0, n), :], qt, preferred_element_type=F32)
                if not last:
                    return s
                key = lax.broadcasted_iota(jnp.int32, (n, 1), 0) + s0
                return jnp.where(key < total - cap + length, s, -1e30)

            def peak(c, m):
                return jnp.maximum(m, jnp.max(score(c), axis=0, keepdims=True))

            old = jnp.full((1, block_q), -1e30, F32)
            if not first:
                old = old_ref[h, HD + ONES : HD + ONES + 1, cols]
            m = lax.fori_loop(0, total // n, peak, old)
            if first:
                acc = jnp.zeros((HD + ONES, block_q), F32)
            else:
                acc = acc * jnp.exp2((old - m) * LOG2E)

            def step(c, acc):
                p = jnp.exp2((score(c) - m) * LOG2E).astype(BF16)
                v = vals[h, :, pl.ds(pl.multiple_of(c * n, n), n)]
                return acc + jnp.dot(v, p, preferred_element_type=F32)

            acc = lax.fori_loop(0, total // n, step, acc)
        else:
            for c in range(0, total, block_k):
                n = min(block_k, total - c)
                s = jnp.dot(keys[h, c : c + n, :], qt, preferred_element_type=F32)
                p = jnp.exp2(s * LOG2E).astype(BF16)
                t = jnp.dot(vals[h, :, c : c + n], p, preferred_element_type=F32)
                acc = t if acc is None else acc + t
        if last:
            out = (acc[0:HD] / acc[HD : HD + 1]).astype(BF16)
            for b in range(per):
                o_refs[start + b][rows, :] = out[:, b * tok : (b + 1) * tok]
        else:
            o_refs[0][h, 0 : HD + ONES, cols] = acc
            o_refs[0][h, HD + ONES :, cols] = jnp.broadcast_to(m, (8, block_q))

    def run(safe):
        for start in range(0, tiles, per):
            lax.fori_loop(0, heads, lambda h, _: (block(h, start, safe), 0)[1], 0)

    @pl.when(small)
    def _():
        run(False)

    @pl.when(jnp.logical_not(small))
    def _():
        run(True)


def attention(length, core, queries, kvs, state=None, caption=(), block_q=512):
    inner, tok = queries[0].shape[0] // 2, queries[0].shape[1]
    heads = inner // HD
    tiles = len(queries)
    first, last = state is None, bool(caption)
    blocks = len(kvs)
    total = blocks * tok + (caption[0].shape[1] if last else 0)
    smem = pl.BlockSpec(memory_space=pltpu.SMEM)
    vm = pl.BlockSpec(memory_space=pltpu.VMEM)
    operands = (*queries, *kvs, *(() if first else (state,)), *caption)
    if last:
        out_shape = (jax.ShapeDtypeStruct((inner, tok), BF16),) * tiles
    else:
        out_shape = (jax.ShapeDtypeStruct((heads, HD + ONES + 8, tiles * tok), F32),)
    return pl.pallas_call(
        functools.partial(
            attention_kernel,
            tiles=tiles,
            sources=len(kvs),
            first=first,
            last=last,
            block_q=block_q,
            block_k=total // 2,
        ),
        out_shape=out_shape,
        in_specs=[smem, smem]
        + [pl.BlockSpec(memory_space=pltpu.HBM)] * (tiles + blocks)
        + [vm] * (len(operands) - tiles - blocks),
        out_specs=(vm,) * len(out_shape),
        scratch_shapes=([pltpu.VMEM((2 * inner, tok), BF16)] if last else [])
        + [
            pltpu.VMEM((heads, total, HD), BF16),
            pltpu.VMEM((heads, HD + ONES, total), BF16),
            pltpu.VMEM((tiles, inner, tok), BF16),
            pltpu.VMEM((blocks, 2 * inner, tok), BF16),
            pltpu.SemaphoreType.DMA((tiles + blocks,)),
        ],
        cost_estimate=pl.CostEstimate(
            flops=16 * tiles * tok * total * inner,
            transcendentals=tiles * tok * total * heads,
            bytes_accessed=2 * inner * (2 * total + 2 * tiles * tok),
        ),
        compiler_params=pltpu.CompilerParams(vmem_limit_bytes=VMEM_LIMIT),
        name="attention",
    )(length, core[None], *operands)


def grad_kernel(w_ref, sel_ref, *refs, tiles, part):
    o_refs, cot_refs, g_ref = refs[:tiles], refs[tiles:-1], refs[-1]
    width = cot_refs[0].shape[1]
    dp, pairs, chunk, _ = g_ref.shape
    rows = [
        pl.ds(pl.multiple_of((2 * s + sel_ref[0]) * part, 16), part) for s in range(pairs)
    ]
    left = jnp.concatenate(
        [jnp.concatenate([ref[r, :] for ref in o_refs], axis=1) for r in rows], axis=0
    )
    weight = w_ref[0]
    step = 2 * LANES
    for c in range(0, width, step):
        n = min(step, width - c)
        right = jnp.concatenate([ref[:, c : c + n] for ref in cot_refs], axis=0)
        g = (jnp.dot(left, right, preferred_element_type=F32) * weight).astype(BF16)
        for t in range(n // LANES):
            cols = slice(t * LANES, (t + 1) * LANES)
            for s in range(pairs):
                done = 0
                while done < part:
                    flat = (c // LANES + t) * part + done
                    count = min(part - done, chunk - flat % chunk)
                    g_ref[flat // chunk, s, flat % chunk : flat % chunk + count, :] = g[
                        s * part + done : s * part + done + count, cols
                    ]
                    done += count
    used = width // LANES * part - (dp - 1) * chunk
    if used < chunk:
        for s in range(pairs):
            g_ref[dp - 1, s, used:, :] = jnp.zeros((chunk - used, LANES), BF16)


def local_grad(weight, select, attended, cots, part, dp):
    inner, tok = attended[0].shape
    width = cots[0].shape[1]
    pairs = inner // (2 * part)
    chunk = -(-(width // LANES * part) // (dp * 16)) * 16
    vm = pl.BlockSpec(memory_space=pltpu.VMEM)
    smem = pl.BlockSpec(memory_space=pltpu.SMEM)
    tiles = len(attended)
    return pl.pallas_call(
        functools.partial(grad_kernel, tiles=tiles, part=part),
        out_shape=jax.ShapeDtypeStruct((dp, pairs, chunk, LANES), BF16),
        in_specs=[smem, smem] + [vm] * (tiles + len(cots)),
        out_specs=vm,
        cost_estimate=pl.CostEstimate(
            flops=tiles * tok * inner * width,
            transcendentals=0,
            bytes_accessed=2 * tiles * tok * (inner + width) + inner * width,
        ),
        compiler_params=pltpu.CompilerParams(vmem_limit_bytes=VMEM_LIMIT),
        name="local_grad",
    )(weight, select[None], *attended, *cots)


def add_pieces_kernel(x_ref, o_ref):
    total = x_ref[0].astype(F32)
    for i in range(1, x_ref.shape[0]):
        total = total + x_ref[i].astype(F32)
    total = total.astype(BF16)
    for i in range(o_ref.shape[0]):
        o_ref[i] = total


def add_pieces(x, copies):
    vm = pl.BlockSpec(memory_space=pltpu.VMEM)
    return pl.pallas_call(
        add_pieces_kernel,
        out_shape=jax.ShapeDtypeStruct((copies, *x.shape[1:]), BF16),
        in_specs=[vm],
        out_specs=vm,
        compiler_params=pltpu.CompilerParams(vmem_limit_bytes=SMALL_LIMIT),
        name="add_pieces",
    )(x)


def add_squares_kernel(x_ref, o_ref):
    x = x_ref[...].astype(F32)
    rows = jnp.sum(x * x, axis=0, keepdims=True)
    total = jnp.sum(rows, axis=1, keepdims=True)
    o_ref[...] = jnp.broadcast_to(total, o_ref.shape)


def add_squares(x, copies):
    vm = pl.BlockSpec(memory_space=pltpu.VMEM)
    return pl.pallas_call(
        add_squares_kernel,
        out_shape=jax.ShapeDtypeStruct((copies, LANES), F32),
        in_specs=[vm],
        out_specs=vm,
        compiler_params=pltpu.CompilerParams(vmem_limit_bytes=SMALL_LIMIT),
        name="add_squares",
    )(x)


def adam_kernel(s_ref, g_ref, w_ref, mv_ref, ms_ref, vv_ref, vs_ref, nw, nmv, nms, nvv, nvs):
    rows, width = w_ref.shape
    squares = jnp.sum(s_ref[...], axis=0, keepdims=True)
    factor = 256.0 / jnp.sqrt(squares + 1e-06)
    diagonal = lax.broadcasted_iota(jnp.int32, (rows, rows), 0) == lax.broadcasted_iota(
        jnp.int32, (rows, rows), 1
    )

    def down(row):
        return jnp.sum(jnp.where(diagonal, row, 0.0), axis=1, keepdims=True)

    def across(column):
        return jnp.sum(jnp.where(diagonal, column, 0.0), axis=0, keepdims=True)

    for t in range(width // LANES):
        cols = slice(t * LANES, (t + 1) * LANES)
        one = slice(t, t + 1)
        g = g_ref[t * rows : (t + 1) * rows, :].astype(F32) * factor
        first = mv_ref[:, cols].astype(F32) * down(ms_ref[one, :])
        second = vv_ref[:, cols].astype(F32) * down(vs_ref[one, :])
        first = 0.9 * first + 0.1 * g
        second = 0.999 * second + 0.001 * g * g
        update = first / (1.0 - 0.9**10) / (jnp.sqrt(second / (1.0 - 0.999**10)) + 1e-08)
        nw[:, cols] = (w_ref[:, cols].astype(F32) - 0.02 * update).astype(BF16)
        fs = jnp.max(jnp.abs(first), axis=1, keepdims=True) + 1e-06
        ss = jnp.max(jnp.abs(second), axis=1, keepdims=True) + 1e-06
        nms[one, :] = across(fs)
        nvs[one, :] = across(ss)
        nmv[:, cols] = (first / fs).astype(BF16)
        nvv[:, cols] = (second / ss).astype(BF16)


def adam(squares, grad, out_weight, mom_val, mom_scale, var_val, var_scale):
    vm = pl.BlockSpec(memory_space=pltpu.VMEM)
    like = lambda a: jax.ShapeDtypeStruct(a.shape, a.dtype)
    mom_scale, var_scale = mom_scale.T, var_scale.T
    new_weight, first_val, first_scale, second_val, second_scale = pl.pallas_call(
        adam_kernel,
        out_shape=(like(out_weight), like(mom_val), like(mom_scale), like(var_val), like(var_scale)),
        in_specs=[vm] * 7,
        out_specs=(vm,) * 5,
        compiler_params=pltpu.CompilerParams(vmem_limit_bytes=SMALL_LIMIT),
        name="adam",
    )(squares, grad, out_weight, mom_val, mom_scale, var_val, var_scale)
    return new_weight, first_val, first_scale.T, second_val, second_scale.T


def swap(x, axis):
    return lax.ppermute(x, axis, [(0, 1), (1, 0)])


def shift(x, k):
    return lax.ppermute(x, "z", [(i, (i + k) % NT) for i in range(NT)])


def body(
    latent_q,
    latent_k,
    latent_v,
    caption_states,
    caption_proj,
    caption_len,
    timestep,
    out_cot,
    out_weight,
    mom_val,
    mom_scale,
    var_val,
    var_scale,
):
    tok, inner = latent_q.shape[1:]
    cap = caption_states.shape[1]
    xh, z, c = lax.axis_index("xh"), lax.axis_index("z"), lax.axis_index("c")

    own = stage_kv(z, latent_k[0], latent_v[0])
    kvs = [own[0]] + [shift(own[k], k) for k in range(1, NT)]
    near, far = [swap(own[0], "c")], [swap(own[0], "xh")]

    states = lax.optimization_barrier((caption_states[0], own[0]))[0]
    keep, send = caption_partial(z, c, caption_proj, states)
    other = swap(send, "c")
    staged = stage_q(z, latent_q[0], keep, other)
    queries = [staged[0]] + [shift(staged[k], k) for k in range(1, NT)]

    near0, far0, *rest = lax.optimization_barrier((near[0], far[0], *kvs[1:], *staged[1:]))
    kvs = [kvs[0], *rest[: NT - 1]]
    near = [near0] + [swap(x, "c") for x in kvs[1:]]
    far = [far0] + [swap(x, "xh") for x in kvs[1:]]

    cot = lax.optimization_barrier((out_cot[0], *kvs[1:]))[0]
    half = tok // 2
    before, after = shift(cot, 1), shift(cot, -1)
    caption = [caption_sum(queries)]
    caption = caption + [swap(caption[0], "c"), swap(caption[0], "xh")]

    (state,) = attention(caption_len, c, queries, kvs + near)
    held = lax.optimization_barrier((state, caption[2], before, after, *far))
    state, caption[2], before, after, *far = held
    cots = [cot, before, shift(before[:half], 1), shift(after[half:], -1), after]
    last = [swap(x, "c") for x in far]
    caption = caption + [swap(caption[2], "c")]
    (state,) = attention(caption_len, c, queries, far, state)
    attended = attention(caption_len, c, queries, last, state, caption)
    back = [attended[0]] + [shift(attended[k], -k) for k in range(1, NT)]

    loss_weight = 1.0 + 3.0 * (timestep.astype(F32) + 0.5) / 1000.0
    rows = out_weight.shape[0]
    dp = lax.axis_size("xl") * lax.axis_size("y")
    other = swap(local_grad(loss_weight, 1 - c, attended, cots, rows, dp), "c")
    grad = local_grad(loss_weight, c, attended, cots, rows, dp)
    grad = (grad.astype(F32) + other.astype(F32)).astype(BF16)
    chunk = grad.shape[2]
    grad = lax.all_to_all(
        grad.reshape(2 * dp, chunk, LANES), ("xl", "y", "xh"), 0, 0, tiled=True
    )
    grad = lax.all_to_all(add_pieces(grad, dp), ("xl", "y"), 0, 0, tiled=True)
    grad = grad.reshape(dp * chunk, LANES)
    perm = [
        (s * NT + i, (i // 2) * NT + 2 * (i % 2) + s) for s in range(2) for i in range(NT)
    ]
    ctx = ("xh", "z", "c")
    squares = lax.all_to_all(add_squares(grad, lax.axis_size(ctx)), ctx, 0, 0, tiled=True)
    grad = lax.ppermute(grad, ("xh", "z"), perm)
    squares, *back = lax.optimization_barrier((squares, *back))
    attn_out = unstage(z, back)[None]
    updated = adam(squares, grad, out_weight, mom_val, mom_scale, var_val, var_scale)
    return (attn_out, *updated)


def solution(mesh):
    fine = Mesh(mesh.devices.reshape(2, 4, 2, NT, 2), ("xl", "y", "xh", "z", "c"))
    dp = ("xl", "y")
    ctx = ("xh", "z", "c")
    tokens = P(dp, ctx, None)
    rows = P(ctx, None)
    return jax.shard_map(
        body,
        mesh=fine,
        in_specs=(
            tokens,
            tokens,
            tokens,
            P(dp, None, ctx),
            rows,
            P(dp),
            P(dp),
            tokens,
            rows,
            rows,
            rows,
            rows,
            rows,
        ),
        out_specs=(tokens, rows, rows, rows, rows, rows),
        check_vma=False,
    )
```

```python
import functools
import math

import jax
import jax.numpy as jnp
from jax import lax
from jax.experimental import pallas as pl
from jax.experimental.pallas import tpu as pltpu
from jax.sharding import Mesh, PartitionSpec as P

HD = 64
LANES = 128
ONES = 16
LOG2E = math.log2(math.e)
SAFE_BOUND = 60.0
F32 = jnp.float32
BF16 = jnp.bfloat16
NT = 4
VMEM_LIMIT = 16 * 2**20
SMALL_LIMIT = 10 * 2**20


def head_norms(x, heads):
    x = x.astype(F32)
    x = x * x
    rows = [jnp.sum(x[h * HD : (h + 1) * HD], axis=0, keepdims=True) for h in range(heads)]
    return jnp.max(jnp.concatenate(rows, axis=0), axis=1, keepdims=True)


def rel_rows(z_ref, k, group):
    return pl.ds(pl.multiple_of((z_ref[0] + k) % NT * group, group), group)


def stage_kernel(z_ref, *refs, count):
    x_refs, refs = refs[:count], refs[count:]
    add_refs, o_refs, scratch = refs[: -NT - 1], refs[-NT - 1 : -1], refs[-1]
    inner = scratch.shape[0]
    group = inner // NT
    for a, x_ref in enumerate(x_refs):
        for c in range(0, inner, LANES):
            scratch[c : c + LANES, :] = x_ref[:, c : c + LANES].T
        for k in range(NT):
            o_refs[k][a * group : (a + 1) * group, :] = scratch[rel_rows(z_ref, k, group), :]
    if add_refs:
        for k in range(NT):
            rows = slice(k * group, (k + 1) * group)
            both = add_refs[0][rows, :].astype(F32) + add_refs[1][rows, :].astype(F32)
            o_refs[k][count * group :, :] = both.astype(BF16)


def stage(z, arrays, addends=()):
    tok, inner = arrays[0].shape
    parts = len(arrays) + len(addends) // 2
    vm = pl.BlockSpec(memory_space=pltpu.VMEM)
    shape = jax.ShapeDtypeStruct((parts * inner // NT, tok), BF16)
    return pl.pallas_call(
        functools.partial(stage_kernel, count=len(arrays)),
        out_shape=(shape,) * NT,
        in_specs=[pl.BlockSpec(memory_space=pltpu.SMEM)] + [vm] * (len(arrays) + len(addends)),
        out_specs=(vm,) * NT,
        scratch_shapes=[pltpu.VMEM((inner, tok), BF16)],
        cost_estimate=pl.CostEstimate(
            flops=0, transcendentals=0, bytes_accessed=4 * parts * tok * inner
        ),
        compiler_params=pltpu.CompilerParams(vmem_limit_bytes=SMALL_LIMIT),
        name="stage",
    )(z[None], *arrays, *addends)


def caption_kernel(z_ref, c_ref, proj_ref, states_ref, keep_ref, send_ref, scratch):
    scratch[...] = lax.dot_general(
        proj_ref[...], states_ref[...], (((0,), (1,)), ((), ())), preferred_element_type=F32
    ).astype(BF16)
    inner = scratch.shape[0] // 2
    half = inner // (2 * NT)
    for o_ref, core in ((keep_ref, c_ref[0]), (send_ref, 1 - c_ref[0])):
        for k in range(NT):
            for a in range(2):
                start = a * inner + ((z_ref[0] + k) % NT * 2 + core) * half
                at = (2 * k + a) * half
                o_ref[at : at + half, :] = scratch[pl.ds(pl.multiple_of(start, half), half), :]


def caption_partial(z, c, proj, states):
    features, width = proj.shape
    cap = states.shape[0]
    vm = pl.BlockSpec(memory_space=pltpu.VMEM)
    smem = pl.BlockSpec(memory_space=pltpu.SMEM)
    shape = jax.ShapeDtypeStruct((width // 2, cap), BF16)
    return pl.pallas_call(
        caption_kernel,
        out_shape=(shape, shape),
        in_specs=[smem, smem, vm, vm],
        out_specs=(vm, vm),
        scratch_shapes=[pltpu.VMEM((width, cap), BF16)],
        cost_estimate=pl.CostEstimate(
            flops=2 * width * cap * features, transcendentals=0, bytes_accessed=4 * width * cap
        ),
        compiler_params=pltpu.CompilerParams(vmem_limit_bytes=SMALL_LIMIT),
        name="caption_partial",
    )(z[None], c[None], proj, states)


def pack_kernel(*refs, rows, count):
    o_ref, total = refs[count], None
    for i, ref in enumerate(refs[:count]):
        o_ref[i * rows : (i + 1) * rows, :] = ref[0:rows, :]
        if ref.shape[0] > rows:
            more = ref[rows:, :].astype(F32)
            total = more if total is None else total + more
    if total is not None:
        refs[count + 1][...] = total.astype(BF16)


def pack(chunks, rows):
    tok = chunks[0].shape[1]
    added = chunks[0].shape[0] - rows
    vm = pl.BlockSpec(memory_space=pltpu.VMEM)
    shapes = [jax.ShapeDtypeStruct((len(chunks) * rows, tok), BF16)]
    if added:
        shapes.append(jax.ShapeDtypeStruct((added, tok), BF16))
    return pl.pallas_call(
        functools.partial(pack_kernel, rows=rows, count=len(chunks)),
        out_shape=tuple(shapes),
        in_specs=[vm] * len(chunks),
        out_specs=(vm,) * len(shapes),
        compiler_params=pltpu.CompilerParams(vmem_limit_bytes=SMALL_LIMIT),
        name="pack",
    )(*chunks)


def halves_kernel(x_ref, y_ref, upper_ref, lower_ref):
    half = upper_ref.shape[0]
    upper_ref[...] = x_ref[0:half, :]
    lower_ref[...] = y_ref[half:, :]


def halves(x, y):
    rows, cols = x.shape
    vm = pl.BlockSpec(memory_space=pltpu.VMEM)
    shape = jax.ShapeDtypeStruct((rows // 2, cols), x.dtype)
    return pl.pallas_call(
        halves_kernel,
        out_shape=(shape, shape),
        in_specs=[vm, vm],
        out_specs=(vm, vm),
        compiler_params=pltpu.CompilerParams(vmem_limit_bytes=SMALL_LIMIT),
        name="halves",
    )(x, y)


def unstage_kernel(z_ref, *refs):
    x_refs, o_ref, scratch = refs[:NT], refs[NT], refs[NT + 1]
    group = x_refs[0].shape[0]
    for k in range(NT):
        start = pl.multiple_of((z_ref[0] + k) % NT * group, group)
        scratch[pl.ds(start, group), :] = x_refs[k][...]
    for c in range(0, NT * group, LANES):
        o_ref[:, c : c + LANES] = scratch[c : c + LANES, :].T


def unstage(z, pieces):
    group, tok = pieces[0].shape
    vm = pl.BlockSpec(memory_space=pltpu.VMEM)
    return pl.pallas_call(
        unstage_kernel,
        out_shape=jax.ShapeDtypeStruct((tok, NT * group), BF16),
        in_specs=[pl.BlockSpec(memory_space=pltpu.SMEM)] + [vm] * NT,
        out_specs=vm,
        scratch_shapes=[pltpu.VMEM((NT * group, tok), BF16)],
        compiler_params=pltpu.CompilerParams(vmem_limit_bytes=VMEM_LIMIT),
        name="unstage",
    )(z[None], *pieces)


def attention_kernel(len_ref, core_ref, q_ref, *refs, tiles, sources, first, last, block_q, block_k):
    kv_refs, refs = refs[:sources], refs[sources:]
    old_ref = None
    if not first:
        old_ref, refs = refs[0], refs[1:]
    if last:
        piece_refs, cap_ref, refs = refs[:4], refs[-3], refs[4:-3] + refs[-2:]
        half = cap_ref.shape[0] // 4
        for flip in range(2):
            rows = 0.0
            for ref in (piece_refs[flip], piece_refs[2 + flip]):
                rows = rows + ref[ref.shape[0] - 2 * half :, :].astype(F32)
            rows = rows.astype(BF16)
            for a in range(2):
                start = pl.multiple_of((2 * a + (core_ref[0] ^ flip)) * half, half)
                cap_ref[pl.ds(start, half), :] = rows[a * half : (a + 1) * half]
    o_refs, (keys, vals) = refs[:-2], refs[-2:]
    inner, tok = q_ref.shape[0] // tiles, q_ref.shape[1]
    heads = inner // HD
    total = keys.shape[1]
    cap = cap_ref.shape[1] if last else 0
    length = len_ref[0]
    pairs = [
        (ref[r : r + inner, :], ref[r + inner : r + 2 * inner, :])
        for ref in kv_refs
        for r in range(0, ref.shape[0] // (2 * inner) * 2 * inner, 2 * inner)
    ]

    def place(col, k, v, kept):
        n = k.shape[1]
        for h in range(heads):
            keys[h, col : col + n, :] = k[h * HD : (h + 1) * HD].T
            vh = v[h * HD : (h + 1) * HD]
            one = jnp.ones((ONES, n), BF16)
            if kept is not None:
                vh = jnp.where(kept, vh, BF16(0))
                one = jnp.where(kept, one, BF16(0))
            vals[h, 0:HD, col : col + n] = vh
            vals[h, HD : HD + ONES, col : col + n] = one

    kmax = None
    for b, (k, v) in enumerate(pairs):
        place(b * tok, k, v, None)
        norms = head_norms(k, heads)
        kmax = norms if kmax is None else jnp.maximum(kmax, norms)
    if last:
        kept = lax.broadcasted_iota(jnp.int32, (1, cap), 1) < length
        ck = cap_ref[0:inner, :]
        place(len(pairs) * tok, ck, cap_ref[inner : 2 * inner, :], kept)
        kmax = jnp.maximum(kmax, head_norms(ck, heads))
    qmax = None
    for i in range(tiles):
        norms = head_norms(q_ref[i * inner : (i + 1) * inner, :], heads)
        qmax = norms if qmax is None else jnp.maximum(qmax, norms)
    small = jnp.max(qmax * kmax) < HD * SAFE_BOUND * SAFE_BOUND
    if not first:
        offset = jnp.max(jnp.abs(old_ref[0, HD + ONES :, :]))
        for h in range(1, heads):
            offset = jnp.maximum(offset, jnp.max(jnp.abs(old_ref[h, HD + ONES :, :])))
        small = jnp.logical_and(small, offset == 0.0)

    per = block_q // tok

    def block(h, start, safe):
        rows = pl.ds(pl.multiple_of(h * HD, HD), HD)
        cols = slice(start * tok, start * tok + block_q)
        at = [pl.multiple_of((start + b) * inner + h * HD, HD) for b in range(per)]
        qt = jnp.concatenate([q_ref[pl.ds(i, HD), :] for i in at], axis=1)
        qt = qt * BF16(0.125)
        acc = None if first else old_ref[h, 0 : HD + ONES, cols]
        m = jnp.zeros((8, block_q), F32)
        if safe:
            n = tok

            def score(c):
                s0 = pl.multiple_of(c * n, n)
                s = jnp.dot(keys[h, pl.ds(s0, n), :], qt, preferred_element_type=F32)
                if not last:
                    return s
                key = lax.broadcasted_iota(jnp.int32, (n, 1), 0) + s0
                return jnp.where(key < total - cap + length, s, -1e30)

            def peak(c, m):
                return jnp.maximum(m, jnp.max(score(c), axis=0, keepdims=True))

            old = jnp.full((1, block_q), -1e30, F32)
            if not first:
                old = old_ref[h, HD + ONES : HD + ONES + 1, cols]
            m = lax.fori_loop(0, total // n, peak, old)
            if first:
                acc = jnp.zeros((HD + ONES, block_q), F32)
            else:
                acc = acc * jnp.exp2((old - m) * LOG2E)

            def step(c, acc):
                p = jnp.exp2((score(c) - m) * LOG2E).astype(BF16)
                v = vals[h, :, pl.ds(pl.multiple_of(c * n, n), n)]
                return acc + jnp.dot(v, p, preferred_element_type=F32)

            acc = lax.fori_loop(0, total // n, step, acc)
        else:
            for c in range(0, total, block_k):
                n = min(block_k, total - c)
                s = jnp.dot(keys[h, c : c + n, :], qt, preferred_element_type=F32)
                p = jnp.exp2(s * LOG2E).astype(BF16)
                t = jnp.dot(vals[h, :, c : c + n], p, preferred_element_type=F32)
                acc = t if acc is None else acc + t
        if last:
            out = (acc[0:HD] / acc[HD : HD + 1]).astype(BF16)
            for b in range(per):
                o_refs[start + b][rows, :] = out[:, b * tok : (b + 1) * tok]
        else:
            o_refs[0][h, 0 : HD + ONES, cols] = acc
            o_refs[0][h, HD + ONES :, cols] = jnp.broadcast_to(m, (8, block_q))

    def run(safe):
        for start in range(0, tiles, per):
            lax.fori_loop(0, heads, lambda h, _: (block(h, start, safe), 0)[1], 0)

    @pl.when(small)
    def _():
        run(False)

    @pl.when(jnp.logical_not(small))
    def _():
        run(True)


def attention(length, core, queries, kvs, state=None, caption=(), block_q=512):
    inner, tok = queries.shape[0] // NT, queries.shape[1]
    heads = inner // HD
    tiles = NT
    first, last = state is None, bool(caption)
    blocks = sum(x.shape[0] // (2 * inner) for x in kvs)
    total = blocks * tok + (caption[0].shape[1] if last else 0)
    smem = pl.BlockSpec(memory_space=pltpu.SMEM)
    vm = pl.BlockSpec(memory_space=pltpu.VMEM)
    operands = (queries, *kvs, *(() if first else (state,)), *caption)
    if last:
        out_shape = (jax.ShapeDtypeStruct((inner, tok), BF16),) * tiles
    else:
        out_shape = (jax.ShapeDtypeStruct((heads, HD + ONES + 8, tiles * tok), F32),)
    return pl.pallas_call(
        functools.partial(
            attention_kernel,
            tiles=tiles,
            sources=len(kvs),
            first=first,
            last=last,
            block_q=block_q,
            block_k=total // 2,
        ),
        out_shape=out_shape,
        in_specs=[smem, smem]
        + [vm] * len(operands),
        out_specs=(vm,) * len(out_shape),
        scratch_shapes=([pltpu.VMEM((2 * inner, tok), BF16)] if last else [])
        + [
            pltpu.VMEM((heads, total, HD), BF16),
            pltpu.VMEM((heads, HD + ONES, total), BF16),
        ],
        cost_estimate=pl.CostEstimate(flops=0, transcendentals=0, bytes_accessed=0),
        compiler_params=pltpu.CompilerParams(vmem_limit_bytes=VMEM_LIMIT),
        name="attention",
    )(length, core[None], *operands)


def grad_kernel(w_ref, sel_ref, *refs, tiles, part, step):
    o_refs, cot_refs, g_ref = refs[:tiles], refs[tiles:-1], refs[-1]
    width = cot_refs[0].shape[1]
    dp, pairs, chunk, _ = g_ref.shape
    rows = [
        pl.ds(pl.multiple_of((2 * s + sel_ref[0]) * part, 16), part) for s in range(pairs)
    ]
    left = jnp.concatenate(
        [jnp.concatenate([ref[r, :] for ref in o_refs], axis=1) for r in rows], axis=0
    )
    weight = w_ref[0]
    for c in range(0, width, step):
        n = min(step, width - c)
        right = jnp.concatenate([ref[:, c : c + n] for ref in cot_refs], axis=0)
        g = (jnp.dot(left, right, preferred_element_type=F32) * weight).astype(BF16)
        for t in range(n // LANES):
            cols = slice(t * LANES, (t + 1) * LANES)
            for s in range(pairs):
                done = 0
                while done < part:
                    flat = (c // LANES + t) * part + done
                    count = min(part - done, chunk - flat % chunk)
                    g_ref[flat // chunk, s, flat % chunk : flat % chunk + count, :] = g[
                        s * part + done : s * part + done + count, cols
                    ]
                    done += count
    used = width // LANES * part - (dp - 1) * chunk
    if used < chunk:
        for s in range(pairs):
            g_ref[dp - 1, s, used:, :] = jnp.zeros((chunk - used, LANES), BF16)


def local_grad(weight, select, attended, cots, part, dp):
    inner, tok = attended[0].shape
    width = cots[0].shape[1]
    pairs = inner // (2 * part)
    chunk = -(-(width // LANES * part) // (dp * 16)) * 16
    vm = pl.BlockSpec(memory_space=pltpu.VMEM)
    smem = pl.BlockSpec(memory_space=pltpu.SMEM)
    tiles = len(attended)
    step = 2 * LANES
    return pl.pallas_call(
        functools.partial(grad_kernel, tiles=tiles, part=part, step=step),
        out_shape=jax.ShapeDtypeStruct((dp, pairs, chunk, LANES), BF16),
        in_specs=[smem, smem] + [vm] * (tiles + len(cots)),
        out_specs=vm,
        cost_estimate=pl.CostEstimate(
            flops=tiles * tok * inner * width,
            transcendentals=0,
            bytes_accessed=2 * tiles * tok * (inner + width) + inner * width,
        ),
        compiler_params=pltpu.CompilerParams(vmem_limit_bytes=16 * 2**20),
        name="local_grad",
    )(weight, select[None], *attended, *cots)


def add_pieces_kernel(x_ref, o_ref, s_ref):
    total = x_ref[0].astype(F32)
    for i in range(1, x_ref.shape[0]):
        total = total + x_ref[i].astype(F32)
    total = total.astype(BF16)
    o_ref[...] = total
    x = total.astype(F32)
    rows = jnp.sum(x * x, axis=0, keepdims=True)
    s_ref[...] = jnp.broadcast_to(jnp.sum(rows, axis=1, keepdims=True), s_ref.shape)


def add_pieces(x, peers):
    vm = pl.BlockSpec(memory_space=pltpu.VMEM)
    return pl.pallas_call(
        add_pieces_kernel,
        out_shape=(
            jax.ShapeDtypeStruct(x.shape[1:], BF16),
            jax.ShapeDtypeStruct((peers, LANES), F32),
        ),
        in_specs=[vm],
        out_specs=(vm, vm),
        compiler_params=pltpu.CompilerParams(vmem_limit_bytes=SMALL_LIMIT),
        name="add_pieces",
    )(x)


def adam_kernel(at_ref, s_ref, *refs):
    g_refs, refs, g_ref = refs[:4], refs[4:-1], refs[-1]
    chunk = g_refs[0].shape[1]
    for k, ref in enumerate(g_refs):
        for i in range(2):
            at = (at_ref[0] ^ i) * 4 + (at_ref[1] + 4 - k) % 4
            g_ref[pl.ds(pl.multiple_of(at * chunk, chunk), chunk), :] = ref[i]
    adam_rows(s_ref, g_ref, *refs)


def adam_rows(s_ref, g_ref, w_ref, mv_ref, ms_ref, vv_ref, vs_ref, nw, nmv, nms, nvv, nvs):
    rows, width = w_ref.shape
    squares = jnp.sum(s_ref[...], axis=0, keepdims=True)
    factor = 256.0 / jnp.sqrt(squares + 1e-06)
    diagonal = lax.broadcasted_iota(jnp.int32, (rows, rows), 0) == lax.broadcasted_iota(
        jnp.int32, (rows, rows), 1
    )

    def down(row):
        return jnp.sum(jnp.where(diagonal, row, 0.0), axis=1, keepdims=True)

    def across(column):
        return jnp.sum(jnp.where(diagonal, column, 0.0), axis=0, keepdims=True)

    for t in range(width // LANES):
        cols = slice(t * LANES, (t + 1) * LANES)
        one = slice(t, t + 1)
        g = g_ref[t * rows : (t + 1) * rows, :].astype(F32) * factor
        first = mv_ref[:, cols].astype(F32) * down(ms_ref[one, :])
        second = vv_ref[:, cols].astype(F32) * down(vs_ref[one, :])
        first = 0.9 * first + 0.1 * g
        second = 0.999 * second + 0.001 * g * g
        update = first / (1.0 - 0.9**10) / (jnp.sqrt(second / (1.0 - 0.999**10)) + 1e-08)
        nw[:, cols] = (w_ref[:, cols].astype(F32) - 0.02 * update).astype(BF16)
        fs = jnp.max(jnp.abs(first), axis=1, keepdims=True) + 1e-06
        ss = jnp.max(jnp.abs(second), axis=1, keepdims=True) + 1e-06
        nms[one, :] = across(fs)
        nvs[one, :] = across(ss)
        nmv[:, cols] = (first / fs).astype(BF16)
        nvv[:, cols] = (second / ss).astype(BF16)


def adam(at, squares, grads, out_weight, mom_val, mom_scale, var_val, var_scale):
    vm = pl.BlockSpec(memory_space=pltpu.VMEM)
    like = lambda a: jax.ShapeDtypeStruct(a.shape, a.dtype)
    mom_scale, var_scale = mom_scale.T, var_scale.T
    new_weight, first_val, first_scale, second_val, second_scale = pl.pallas_call(
        adam_kernel,
        out_shape=(like(out_weight), like(mom_val), like(mom_scale), like(var_val), like(var_scale)),
        in_specs=[pl.BlockSpec(memory_space=pltpu.SMEM)] + [vm] * 10,
        out_specs=(vm,) * 5,
        scratch_shapes=[pltpu.VMEM((8 * grads[0].shape[1], LANES), BF16)],
        compiler_params=pltpu.CompilerParams(vmem_limit_bytes=SMALL_LIMIT),
        name="adam",
    )(at, squares, *grads, out_weight, mom_val, mom_scale, var_val, var_scale)
    return new_weight, first_val, first_scale.T, second_val, second_scale.T


def swap(x, axis):
    return lax.ppermute(x, axis, [(0, 1), (1, 0)])


def shift(x, k):
    return lax.ppermute(x, "z", [(i, (i + k) % NT) for i in range(NT)])


def body(
    latent_q,
    latent_k,
    latent_v,
    caption_states,
    caption_proj,
    caption_len,
    timestep,
    out_cot,
    out_weight,
    mom_val,
    mom_scale,
    var_val,
    var_scale,
):
    tok, inner = latent_q.shape[1:]
    cap = caption_states.shape[1]
    xh, z, c = lax.axis_index("xh"), lax.axis_index("z"), lax.axis_index("c")

    keep, send = caption_partial(z, c, caption_proj, caption_states[0])
    other = swap(send, "c")

    group = inner // NT
    staged = stage(z, (latent_k[0], latent_v[0]))
    kvs = [staged[0]] + [shift(staged[k], k) for k in range(1, NT)]
    staged = stage(z, (latent_q[0],), (keep, other))
    held = lax.optimization_barrier((*kvs, *staged))
    kvs, staged = held[:NT], held[NT:]

    (ring,) = pack(kvs, 2 * group)
    near, far = swap(ring, "c"), swap(ring, "xh")
    queries, here = pack([staged[0]] + [shift(staged[k], k) for k in range(1, NT)], group)

    cot, queries, near = lax.optimization_barrier((out_cot[0], queries, near))
    before, after = shift(cot, 1), shift(cot, -1)
    there = swap(here, "xh")

    (state,) = attention(caption_len, c, queries, [ring, near])
    state, far, there = lax.optimization_barrier((state, far, there))
    last = swap(far, "c")
    caption = (here, swap(here, "c"), there, swap(there, "c"))
    (state,) = attention(caption_len, c, queries, [far], state)
    state, before, after = lax.optimization_barrier((state, before, after))
    upper, lower = halves(before, after)
    cots = [cot, before, shift(upper, 1), shift(lower, -1), after]
    attended = attention(caption_len, c, queries, [last], state, caption)
    back = [attended[0]] + [shift(attended[k], -k) for k in range(1, NT)]

    loss_weight = 1.0 + 3.0 * (timestep.astype(F32) + 0.5) / 1000.0
    rows = out_weight.shape[0]
    dp = lax.axis_size("xl") * lax.axis_size("y")
    other = swap(local_grad(loss_weight, 1 - c, attended, cots, rows, dp), "c")
    grad = local_grad(loss_weight, c, attended, cots, rows, dp)
    grad = (grad.astype(F32) + other.astype(F32)).astype(BF16)
    chunk = grad.shape[2]
    grad = lax.all_to_all(
        grad.reshape(2 * dp, chunk, LANES), ("xl", "y", "xh"), 0, 0, tiled=True
    )
    grad, *back = lax.optimization_barrier((grad, *back))
    everyone = ("xl", "y", "xh", "z", "c")
    grad, squares = add_pieces(grad, lax.axis_size(everyone))
    pair = []
    for flip in range(2):
        perm = []
        for i in range(4 * NT):
            xl, s, t = i // (2 * NT), i // NT % 2, i % NT
            perm.append((i, (xl ^ flip) * 2 * NT + t // 2 * NT + t % 2 * 2 + s))
        pair.append(lax.ppermute(grad, ("xl", "xh", "z"), perm))
    pair = jnp.stack(pair)
    squares = lax.all_to_all(squares, everyone, 0, 0, tiled=True)
    grads = [pair] + [
        lax.ppermute(pair, "y", [(i, (i + k) % 4) for i in range(4)]) for k in range(1, 4)
    ]
    at = jnp.stack([lax.axis_index("xl"), lax.axis_index("y")])
    attn_out = unstage(z, back)[None]
    updated = adam(at, squares, grads, out_weight, mom_val, mom_scale, var_val, var_scale)
    return (attn_out, *updated)


def solution(mesh):
    fine = Mesh(mesh.devices.reshape(2, 4, 2, NT, 2), ("xl", "y", "xh", "z", "c"))
    dp = ("xl", "y")
    ctx = ("xh", "z", "c")
    tokens = P(dp, ctx, None)
    rows = P(ctx, None)
    return jax.shard_map(
        body,
        mesh=fine,
        in_specs=(
            tokens,
            tokens,
            tokens,
            P(dp, None, ctx),
            rows,
            P(dp),
            P(dp),
            tokens,
            rows,
            rows,
            rows,
            rows,
            rows,
        ),
        out_specs=(tokens, rows, rows, rows, rows, rows),
        check_vma=False,
    )
```

```python
import functools
import math

import jax
import jax.numpy as jnp
from jax import lax
from jax.experimental import pallas as pl
from jax.experimental.pallas import tpu as pltpu
from jax.sharding import Mesh, PartitionSpec as P

HD = 64
LANES = 128
ONES = 16
LOG2E = math.log2(math.e)
SAFE_BOUND = 60.0
F32 = jnp.float32
BF16 = jnp.bfloat16
NT = 4
VMEM_LIMIT = 16 * 2**20
SMALL_LIMIT = 10 * 2**20


def head_norms(x, heads):
    x = x.astype(F32)
    x = x * x
    rows = [jnp.sum(x[h * HD : (h + 1) * HD], axis=0, keepdims=True) for h in range(heads)]
    return jnp.max(jnp.concatenate(rows, axis=0), axis=1, keepdims=True)


def rel_rows(z_ref, k, group):
    return pl.ds(pl.multiple_of((z_ref[0] + k) % NT * group, group), group)


def stage_kernel(z_ref, *refs, count):
    x_refs, refs = refs[:count], refs[count:]
    add_refs, o_refs, scratch = refs[: -NT - 1], refs[-NT - 1 : -1], refs[-1]
    inner = scratch.shape[0]
    group = inner // NT
    for a, x_ref in enumerate(x_refs):
        for c in range(0, inner, LANES):
            scratch[c : c + LANES, :] = x_ref[:, c : c + LANES].T
        for k in range(NT):
            o_refs[k][a * group : (a + 1) * group, :] = scratch[rel_rows(z_ref, k, group), :]
    if add_refs:
        for k in range(NT):
            rows = slice(k * group, (k + 1) * group)
            both = add_refs[0][rows, :].astype(F32) + add_refs[1][rows, :].astype(F32)
            o_refs[k][count * group :, :] = both.astype(BF16)


def stage(z, arrays, addends=()):
    tok, inner = arrays[0].shape
    parts = len(arrays) + len(addends) // 2
    vm = pl.BlockSpec(memory_space=pltpu.VMEM)
    shape = jax.ShapeDtypeStruct((parts * inner // NT, tok), BF16)
    return pl.pallas_call(
        functools.partial(stage_kernel, count=len(arrays)),
        out_shape=(shape,) * NT,
        in_specs=[pl.BlockSpec(memory_space=pltpu.SMEM)] + [vm] * (len(arrays) + len(addends)),
        out_specs=(vm,) * NT,
        scratch_shapes=[pltpu.VMEM((inner, tok), BF16)],
        cost_estimate=pl.CostEstimate(
            flops=0, transcendentals=0, bytes_accessed=4 * parts * tok * inner
        ),
        compiler_params=pltpu.CompilerParams(vmem_limit_bytes=SMALL_LIMIT),
        name="stage",
    )(z[None], *arrays, *addends)


def caption_kernel(z_ref, c_ref, proj_ref, states_ref, keep_ref, send_ref, scratch):
    scratch[...] = lax.dot_general(
        proj_ref[...], states_ref[...], (((0,), (1,)), ((), ())), preferred_element_type=F32
    ).astype(BF16)
    inner = scratch.shape[0] // 2
    half = inner // (2 * NT)
    for o_ref, core in ((keep_ref, c_ref[0]), (send_ref, 1 - c_ref[0])):
        for k in range(NT):
            for a in range(2):
                start = a * inner + ((z_ref[0] + k) % NT * 2 + core) * half
                at = (2 * k + a) * half
                o_ref[at : at + half, :] = scratch[pl.ds(pl.multiple_of(start, half), half), :]


def caption_partial(z, c, proj, states):
    features, width = proj.shape
    cap = states.shape[0]
    vm = pl.BlockSpec(memory_space=pltpu.VMEM)
    smem = pl.BlockSpec(memory_space=pltpu.SMEM)
    shape = jax.ShapeDtypeStruct((width // 2, cap), BF16)
    return pl.pallas_call(
        caption_kernel,
        out_shape=(shape, shape),
        in_specs=[smem, smem, vm, vm],
        out_specs=(vm, vm),
        scratch_shapes=[pltpu.VMEM((width, cap), BF16)],
        cost_estimate=pl.CostEstimate(
            flops=2 * width * cap * features, transcendentals=0, bytes_accessed=4 * width * cap
        ),
        compiler_params=pltpu.CompilerParams(vmem_limit_bytes=SMALL_LIMIT),
        name="caption_partial",
    )(z[None], c[None], proj, states)


def pack_kernel(*refs, rows, count):
    o_ref, total = refs[count], None
    for i, ref in enumerate(refs[:count]):
        o_ref[i * rows : (i + 1) * rows, :] = ref[0:rows, :]
        if ref.shape[0] > rows:
            more = ref[rows:, :].astype(F32)
            total = more if total is None else total + more
    if total is not None:
        refs[count + 1][...] = total.astype(BF16)


def pack(chunks, rows):
    tok = chunks[0].shape[1]
    added = chunks[0].shape[0] - rows
    vm = pl.BlockSpec(memory_space=pltpu.VMEM)
    shapes = [jax.ShapeDtypeStruct((len(chunks) * rows, tok), BF16)]
    if added:
        shapes.append(jax.ShapeDtypeStruct((added, tok), BF16))
    return pl.pallas_call(
        functools.partial(pack_kernel, rows=rows, count=len(chunks)),
        out_shape=tuple(shapes),
        in_specs=[vm] * len(chunks),
        out_specs=(vm,) * len(shapes),
        compiler_params=pltpu.CompilerParams(vmem_limit_bytes=SMALL_LIMIT),
        name="pack",
    )(*chunks)


def halves_kernel(x_ref, y_ref, upper_ref, lower_ref):
    half = upper_ref.shape[0]
    upper_ref[...] = x_ref[0:half, :]
    lower_ref[...] = y_ref[half:, :]


def halves(x, y):
    rows, cols = x.shape
    vm = pl.BlockSpec(memory_space=pltpu.VMEM)
    shape = jax.ShapeDtypeStruct((rows // 2, cols), x.dtype)
    return pl.pallas_call(
        halves_kernel,
        out_shape=(shape, shape),
        in_specs=[vm, vm],
        out_specs=(vm, vm),
        compiler_params=pltpu.CompilerParams(vmem_limit_bytes=6 * 2**20),
        name="halves",
    )(x, y)


def unstage_kernel(z_ref, *refs):
    x_refs, o_ref, scratch = refs[:NT], refs[NT], refs[NT + 1]
    group = x_refs[0].shape[0]
    for k in range(NT):
        start = pl.multiple_of((z_ref[0] + k) % NT * group, group)
        scratch[pl.ds(start, group), :] = x_refs[k][...]
    for c in range(0, NT * group, LANES):
        o_ref[:, c : c + LANES] = scratch[c : c + LANES, :].T


def unstage(z, pieces):
    group, tok = pieces[0].shape
    vm = pl.BlockSpec(memory_space=pltpu.VMEM)
    return pl.pallas_call(
        unstage_kernel,
        out_shape=jax.ShapeDtypeStruct((tok, NT * group), BF16),
        in_specs=[pl.BlockSpec(memory_space=pltpu.SMEM)] + [vm] * NT,
        out_specs=vm,
        scratch_shapes=[pltpu.VMEM((NT * group, tok), BF16)],
        compiler_params=pltpu.CompilerParams(vmem_limit_bytes=VMEM_LIMIT),
        name="unstage",
    )(z[None], *pieces)


def attention_kernel(len_ref, core_ref, q_ref, *refs, tiles, sources, first, last, block_q, block_k):
    kv_refs, refs = refs[:sources], refs[sources:]
    old_ref = None
    if not first:
        old_ref, refs = refs[0], refs[1:]
    if last:
        piece_refs, cap_ref, refs = refs[:2], refs[-3], refs[2:-3] + refs[-2:]
        half = cap_ref.shape[0] // 4
        for flip in range(2):
            one = slice(2 * flip * half, 2 * (flip + 1) * half)
            rows = piece_refs[0][one, :].astype(F32) + piece_refs[1][one, :].astype(F32)
            rows = rows.astype(BF16)
            for a in range(2):
                start = pl.multiple_of((2 * a + (core_ref[0] ^ flip)) * half, half)
                cap_ref[pl.ds(start, half), :] = rows[a * half : (a + 1) * half]
    o_refs, (keys, vals) = refs[:-2], refs[-2:]
    inner, tok = q_ref.shape[0] // tiles, q_ref.shape[1]
    heads = inner // HD
    total = keys.shape[1]
    cap = cap_ref.shape[1] if last else 0
    length = len_ref[0]
    pairs = [
        (ref[r : r + inner, :], ref[r + inner : r + 2 * inner, :])
        for ref in kv_refs
        for r in range(0, ref.shape[0] // (2 * inner) * 2 * inner, 2 * inner)
    ]

    def place(col, k, v, kept):
        n = k.shape[1]
        for h in range(heads):
            keys[h, col : col + n, :] = k[h * HD : (h + 1) * HD].T
            vh = v[h * HD : (h + 1) * HD]
            one = jnp.ones((ONES, n), BF16)
            if kept is not None:
                vh = jnp.where(kept, vh, BF16(0))
                one = jnp.where(kept, one, BF16(0))
            vals[h, 0:HD, col : col + n] = vh
            vals[h, HD : HD + ONES, col : col + n] = one

    kmax = None
    for b, (k, v) in enumerate(pairs):
        place(b * tok, k, v, None)
        norms = head_norms(k, heads)
        kmax = norms if kmax is None else jnp.maximum(kmax, norms)
    if last:
        kept = lax.broadcasted_iota(jnp.int32, (1, cap), 1) < length
        ck = cap_ref[0:inner, :]
        place(len(pairs) * tok, ck, cap_ref[inner : 2 * inner, :], kept)
        kmax = jnp.maximum(kmax, head_norms(ck, heads))
    qmax = None
    for i in range(tiles):
        norms = head_norms(q_ref[i * inner : (i + 1) * inner, :], heads)
        qmax = norms if qmax is None else jnp.maximum(qmax, norms)
    small = jnp.max(qmax * kmax) < HD * SAFE_BOUND * SAFE_BOUND
    if not first:
        offset = jnp.max(jnp.abs(old_ref[0, HD + ONES :, :]))
        for h in range(1, heads):
            offset = jnp.maximum(offset, jnp.max(jnp.abs(old_ref[h, HD + ONES :, :])))
        small = jnp.logical_and(small, offset == 0.0)

    per = block_q // tok

    def block(h, start, safe):
        rows = pl.ds(pl.multiple_of(h * HD, HD), HD)
        cols = slice(start * tok, start * tok + block_q)
        at = [pl.multiple_of((start + b) * inner + h * HD, HD) for b in range(per)]
        qt = jnp.concatenate([q_ref[pl.ds(i, HD), :] for i in at], axis=1)
        qt = qt * BF16(0.125)
        acc = None if first else old_ref[h, 0 : HD + ONES, cols]
        m = jnp.zeros((8, block_q), F32)
        if safe:
            n = tok

            def score(c):
                s0 = pl.multiple_of(c * n, n)
                s = jnp.dot(keys[h, pl.ds(s0, n), :], qt, preferred_element_type=F32)
                if not last:
                    return s
                key = lax.broadcasted_iota(jnp.int32, (n, 1), 0) + s0
                return jnp.where(key < total - cap + length, s, -1e30)

            def peak(c, m):
                return jnp.maximum(m, jnp.max(score(c), axis=0, keepdims=True))

            old = jnp.full((1, block_q), -1e30, F32)
            if not first:
                old = old_ref[h, HD + ONES : HD + ONES + 1, cols]
            m = lax.fori_loop(0, total // n, peak, old)
            if first:
                acc = jnp.zeros((HD + ONES, block_q), F32)
            else:
                acc = acc * jnp.exp2((old - m) * LOG2E)

            def step(c, acc):
                p = jnp.exp2((score(c) - m) * LOG2E).astype(BF16)
                v = vals[h, :, pl.ds(pl.multiple_of(c * n, n), n)]
                return acc + jnp.dot(v, p, preferred_element_type=F32)

            acc = lax.fori_loop(0, total // n, step, acc)
        else:
            for c in range(0, total, block_k):
                n = min(block_k, total - c)
                s = jnp.dot(keys[h, c : c + n, :], qt, preferred_element_type=F32)
                p = jnp.exp2(s * LOG2E).astype(BF16)
                t = jnp.dot(vals[h, :, c : c + n], p, preferred_element_type=F32)
                acc = t if acc is None else acc + t
        if last:
            out = (acc[0:HD] / acc[HD : HD + 1]).astype(BF16)
            for b in range(per):
                o_refs[start + b][rows, :] = out[:, b * tok : (b + 1) * tok]
        else:
            o_refs[0][h, 0 : HD + ONES, cols] = acc
            o_refs[0][h, HD + ONES :, cols] = jnp.broadcast_to(m, (8, block_q))

    def run(safe):
        for start in range(0, tiles, per):
            lax.fori_loop(0, heads, lambda h, _: (block(h, start, safe), 0)[1], 0)

    @pl.when(small)
    def _():
        run(False)

    @pl.when(jnp.logical_not(small))
    def _():
        run(True)


def attention(length, core, queries, kvs, state=None, caption=(), block_q=512):
    inner, tok = queries.shape[0] // NT, queries.shape[1]
    heads = inner // HD
    tiles = NT
    first, last = state is None, bool(caption)
    blocks = sum(x.shape[0] // (2 * inner) for x in kvs)
    total = blocks * tok + (caption[0].shape[1] if last else 0)
    smem = pl.BlockSpec(memory_space=pltpu.SMEM)
    vm = pl.BlockSpec(memory_space=pltpu.VMEM)
    operands = (queries, *kvs, *(() if first else (state,)), *caption)
    if last:
        out_shape = (jax.ShapeDtypeStruct((inner, tok), BF16),) * tiles
    else:
        out_shape = (jax.ShapeDtypeStruct((heads, HD + ONES + 8, tiles * tok), F32),)
    return pl.pallas_call(
        functools.partial(
            attention_kernel,
            tiles=tiles,
            sources=len(kvs),
            first=first,
            last=last,
            block_q=block_q,
            block_k=total // 2,
        ),
        out_shape=out_shape,
        in_specs=[smem, smem]
        + [vm] * len(operands),
        out_specs=(vm,) * len(out_shape),
        scratch_shapes=([pltpu.VMEM((2 * inner, tok), BF16)] if last else [])
        + [
            pltpu.VMEM((heads, total, HD), BF16),
            pltpu.VMEM((heads, HD + ONES, total), BF16),
        ],
        cost_estimate=pl.CostEstimate(flops=0, transcendentals=0, bytes_accessed=0),
        compiler_params=pltpu.CompilerParams(vmem_limit_bytes=VMEM_LIMIT),
        name="attention",
    )(length, core[None], *operands)


def grad_kernel(t_ref, core_ref, *refs, tiles, part, step, flip):
    o_refs, cot_refs, g_ref = refs[:tiles], refs[tiles:-1], refs[-1]
    width = cot_refs[0].shape[1]
    dp, pairs, chunk, _ = g_ref.shape
    rows = [
        pl.ds(pl.multiple_of((2 * s + (core_ref[0] ^ flip)) * part, 16), part) for s in range(pairs)
    ]
    left = jnp.concatenate(
        [jnp.concatenate([ref[r, :] for ref in o_refs], axis=1) for r in rows], axis=0
    )
    time = jnp.full((1, step), t_ref[0], jnp.int32).astype(F32)
    weight = 1.0 + 3.0 * (time + 0.5) / 1000.0
    for c in range(0, width, step):
        n = min(step, width - c)
        right = jnp.concatenate([ref[:, c : c + n] for ref in cot_refs], axis=0)
        g = (jnp.dot(left, right, preferred_element_type=F32) * weight[:, :n]).astype(BF16)
        for t in range(n // LANES):
            cols = slice(t * LANES, (t + 1) * LANES)
            for s in range(pairs):
                done = 0
                while done < part:
                    flat = (c // LANES + t) * part + done
                    count = min(part - done, chunk - flat % chunk)
                    g_ref[flat // chunk, s, flat % chunk : flat % chunk + count, :] = g[
                        s * part + done : s * part + done + count, cols
                    ]
                    done += count
    used = width // LANES * part - (dp - 1) * chunk
    if used < chunk:
        for s in range(pairs):
            g_ref[dp - 1, s, used:, :] = jnp.zeros((chunk - used, LANES), BF16)


def local_grad(timestep, core, flip, attended, cots, part, dp):
    inner, tok = attended[0].shape
    width = cots[0].shape[1]
    pairs = inner // (2 * part)
    chunk = -(-(width // LANES * part) // (dp * 16)) * 16
    vm = pl.BlockSpec(memory_space=pltpu.VMEM)
    smem = pl.BlockSpec(memory_space=pltpu.SMEM)
    tiles = len(attended)
    step = 2 * LANES
    return pl.pallas_call(
        functools.partial(grad_kernel, tiles=tiles, part=part, step=step, flip=flip),
        out_shape=jax.ShapeDtypeStruct((dp, pairs, chunk, LANES), BF16),
        in_specs=[smem, smem] + [vm] * (tiles + len(cots)),
        out_specs=vm,
        cost_estimate=pl.CostEstimate(
            flops=tiles * tok * inner * width,
            transcendentals=0,
            bytes_accessed=2 * tiles * tok * (inner + width) + inner * width,
        ),
        compiler_params=pltpu.CompilerParams(vmem_limit_bytes=16 * 2**20),
        name="local_grad",
    )(timestep, core[None], *attended, *cots)


def add_two_kernel(x_ref, y_ref, o_ref):
    o_ref[...] = (x_ref[...].astype(F32) + y_ref[...].astype(F32)).astype(BF16)


def add_two(x, y):
    vm = pl.BlockSpec(memory_space=pltpu.VMEM)
    return pl.pallas_call(
        add_two_kernel,
        out_shape=jax.ShapeDtypeStruct(x.shape, BF16),
        in_specs=[vm, vm],
        out_specs=vm,
        compiler_params=pltpu.CompilerParams(vmem_limit_bytes=SMALL_LIMIT),
        name="add_two",
    )(x, y)


def add_pieces_kernel(x_ref, o_ref, s_ref):
    total = x_ref[0].astype(F32)
    for i in range(1, x_ref.shape[0]):
        total = total + x_ref[i].astype(F32)
    total = total.astype(BF16)
    o_ref[...] = total
    x = total.astype(F32)
    rows = jnp.sum(x * x, axis=0, keepdims=True)
    s_ref[...] = jnp.broadcast_to(jnp.sum(rows, axis=1, keepdims=True), s_ref.shape)


def add_pieces(x, peers):
    vm = pl.BlockSpec(memory_space=pltpu.VMEM)
    return pl.pallas_call(
        add_pieces_kernel,
        out_shape=(
            jax.ShapeDtypeStruct(x.shape[1:], BF16),
            jax.ShapeDtypeStruct((peers, LANES), F32),
        ),
        in_specs=[vm],
        out_specs=(vm, vm),
        compiler_params=pltpu.CompilerParams(vmem_limit_bytes=SMALL_LIMIT),
        name="add_pieces",
    )(x)


def adam_kernel(at_ref, s_ref, *refs):
    g_refs, refs, g_ref = refs[:4], refs[4:-1], refs[-1]
    chunk = g_refs[0].shape[1]
    for k, ref in enumerate(g_refs):
        for i in range(2):
            at = (at_ref[0] ^ i) * 4 + (at_ref[1] + 4 - k) % 4
            rows = pl.ds(pl.multiple_of(at * chunk, chunk), chunk)
            g_ref[rows, :] = ref[i]
    adam_rows(s_ref, g_ref, *refs)


def adam_rows(s_ref, g_ref, w_ref, mv_ref, ms_ref, vv_ref, vs_ref, nw, nmv, nms, nvv, nvs):
    rows, width = w_ref.shape
    squares = jnp.sum(s_ref[...], axis=0, keepdims=True)
    factor = 256.0 / jnp.sqrt(squares + 1e-06)
    diagonal = lax.broadcasted_iota(jnp.int32, (rows, rows), 0) == lax.broadcasted_iota(
        jnp.int32, (rows, rows), 1
    )

    def down(row):
        return jnp.sum(jnp.where(diagonal, row, 0.0), axis=1, keepdims=True)

    def across(column):
        return jnp.sum(jnp.where(diagonal, column, 0.0), axis=0, keepdims=True)

    for t in range(width // LANES):
        cols = slice(t * LANES, (t + 1) * LANES)
        one = slice(t, t + 1)
        g = g_ref[t * rows : (t + 1) * rows, :].astype(F32) * factor
        first = mv_ref[:, cols].astype(F32) * down(ms_ref[one, :])
        second = vv_ref[:, cols].astype(F32) * down(vs_ref[one, :])
        first = 0.9 * first + 0.1 * g
        second = 0.999 * second + 0.001 * g * g
        update = first / (1.0 - 0.9**10) / (jnp.sqrt(second / (1.0 - 0.999**10)) + 1e-08)
        nw[:, cols] = (w_ref[:, cols].astype(F32) - 0.02 * update).astype(BF16)
        fs = jnp.max(jnp.abs(first), axis=1, keepdims=True) + 1e-06
        ss = jnp.max(jnp.abs(second), axis=1, keepdims=True) + 1e-06
        nms[one, :] = across(fs)
        nvs[one, :] = across(ss)
        nmv[:, cols] = (first / fs).astype(BF16)
        nvv[:, cols] = (second / ss).astype(BF16)


def adam(at, squares, grads, out_weight, mom_val, mom_scale, var_val, var_scale):
    vm = pl.BlockSpec(memory_space=pltpu.VMEM)
    like = lambda a: jax.ShapeDtypeStruct(a.shape, a.dtype)
    mom_scale, var_scale = mom_scale.T, var_scale.T
    new_weight, first_val, first_scale, second_val, second_scale = pl.pallas_call(
        adam_kernel,
        out_shape=(like(out_weight), like(mom_val), like(mom_scale), like(var_val), like(var_scale)),
        in_specs=[pl.BlockSpec(memory_space=pltpu.SMEM)] + [vm] * 10,
        out_specs=(vm,) * 5,
        scratch_shapes=[pltpu.VMEM((8 * grads[0].shape[1], LANES), BF16)],
        compiler_params=pltpu.CompilerParams(vmem_limit_bytes=SMALL_LIMIT),
        name="adam",
    )(at, squares, *grads, out_weight, mom_val, mom_scale, var_val, var_scale)
    return new_weight, first_val, first_scale.T, second_val, second_scale.T


def swap(x, axis):
    return lax.ppermute(x, axis, [(0, 1), (1, 0)])


def shift(x, k):
    return lax.ppermute(x, "z", [(i, (i + k) % NT) for i in range(NT)])


def body(
    latent_q,
    latent_k,
    latent_v,
    caption_states,
    caption_proj,
    caption_len,
    timestep,
    out_cot,
    out_weight,
    mom_val,
    mom_scale,
    var_val,
    var_scale,
):
    tok, inner = latent_q.shape[1:]
    cap = caption_states.shape[1]
    xh, z, c = lax.axis_index("xh"), lax.axis_index("z"), lax.axis_index("c")

    keep, send = caption_partial(z, c, caption_proj, caption_states[0])
    other = swap(send, "c")

    group = inner // NT
    staged = stage(z, (latent_k[0], latent_v[0]))
    kvs = [staged[0]] + [shift(staged[k], k) for k in range(1, NT)]
    staged = stage(z, (latent_q[0],), (keep, other))
    queries = [staged[0]] + [shift(staged[k], k) for k in range(1, NT)]
    far_own = swap(kvs[0], "xh")
    held = lax.optimization_barrier((*kvs, *queries, far_own))
    kvs, queries, far_own = held[:NT], held[NT : 2 * NT], held[-1]

    (ring,), (rest,) = pack(kvs, 2 * group), pack(kvs[1:], 2 * group)
    near, far = swap(ring, "c"), swap(rest, "xh")
    queries, here = pack(queries, group)
    (here,) = pack((here, swap(here, "c")), group)

    cot, queries, near, here = lax.optimization_barrier((out_cot[0], queries, near, here))
    before, after = shift(cot, 1), shift(cot, -1)
    there, last_own = swap(here, "xh"), swap(far_own, "c")

    (state,) = attention(caption_len, c, queries, [ring, near])
    state, far, last_own = lax.optimization_barrier((state, far, last_own))
    last = swap(far, "c")
    (state,) = attention(caption_len, c, queries, [far_own, far], state, block_q=NT * tok)
    state, before, after, there = lax.optimization_barrier((state, before, after, there))
    upper, lower = halves(before, after)
    cots = [cot, before, shift(upper, 1), shift(lower, -1), after]
    attended = attention(caption_len, c, queries, [last_own, last], state, (here, there), NT * tok)
    back = [attended[0]] + [shift(attended[k], -k) for k in range(1, NT)]

    rows = out_weight.shape[0]
    dp = lax.axis_size("xl") * lax.axis_size("y")
    other = swap(local_grad(timestep, c, 1, attended, cots, rows, dp), "c")
    grad = local_grad(timestep, c, 0, attended, cots, rows, dp)
    chunk = grad.shape[2]
    grad = add_two(grad, other)
    grad = lax.all_to_all(
        grad.reshape(2 * dp, chunk, LANES), ("xl", "y", "xh"), 0, 0, tiled=True
    )
    grad, *back = lax.optimization_barrier((grad, *back))
    everyone = ("xl", "y", "xh", "z", "c")
    grad, squares = add_pieces(grad, lax.axis_size(everyone))
    pair = []
    for flip in range(2):
        perm = []
        for i in range(4 * NT):
            xl, s, t = i // (2 * NT), i // NT % 2, i % NT
            perm.append((i, (xl ^ flip) * 2 * NT + t // 2 * NT + t % 2 * 2 + s))
        pair.append(lax.ppermute(grad, ("xl", "xh", "z"), perm))
    pair = jnp.stack(pair)
    squares = lax.all_to_all(squares, everyone, 0, 0, tiled=True)
    grads = [pair] + [
        lax.ppermute(pair, "y", [(i, (i + k) % 4) for i in range(4)]) for k in range(1, 4)
    ]
    at = jnp.stack([lax.axis_index("xl"), lax.axis_index("y")])
    attn_out = unstage(z, back)[None]
    updated = adam(at, squares, grads, out_weight, mom_val, mom_scale, var_val, var_scale)
    return (attn_out, *updated)


def solution(mesh):
    fine = Mesh(mesh.devices.reshape(2, 4, 2, NT, 2), ("xl", "y", "xh", "z", "c"))
    dp = ("xl", "y")
    ctx = ("xh", "z", "c")
    tokens = P(dp, ctx, None)
    rows = P(ctx, None)
    return jax.shard_map(
        body,
        mesh=fine,
        in_specs=(
            tokens,
            tokens,
            tokens,
            P(dp, None, ctx),
            rows,
            P(dp),
            P(dp),
            tokens,
            rows,
            rows,
            rows,
            rows,
            rows,
        ),
        out_specs=(tokens, rows, rows, rows, rows, rows),
        check_vma=False,
    )
```

```python
import functools
import math

import jax
import jax.numpy as jnp
from jax import lax
from jax.experimental import pallas as pl
from jax.experimental.pallas import tpu as pltpu
from jax.sharding import Mesh, PartitionSpec as P

HD = 64
LANES = 128
ONES = 16
LOG2E = math.log2(math.e)
SAFE_BOUND = 60.0
F32 = jnp.float32
BF16 = jnp.bfloat16
NT = 4
VMEM_LIMIT = 16 * 2**20
SMALL_LIMIT = 10 * 2**20


def head_norms(x, heads):
    x = x.astype(F32)
    x = x * x
    rows = [jnp.sum(x[h * HD : (h + 1) * HD], axis=0, keepdims=True) for h in range(heads)]
    return jnp.max(jnp.concatenate(rows, axis=0), axis=1, keepdims=True)


def rel_rows(z_ref, k, group):
    return pl.ds(pl.multiple_of((z_ref[0] + k) % NT * group, group), group)


def stage_kernel(z_ref, *refs, count):
    x_refs, refs = refs[:count], refs[count:]
    add_refs, o_refs, scratch = refs[: -NT - 1], refs[-NT - 1 : -1], refs[-1]
    inner = scratch.shape[0]
    group = inner // NT
    for a, x_ref in enumerate(x_refs):
        for c in range(0, inner, LANES):
            scratch[c : c + LANES, :] = x_ref[:, c : c + LANES].T
        for k in range(NT):
            o_refs[k][a * group : (a + 1) * group, :] = scratch[rel_rows(z_ref, k, group), :]
    if add_refs:
        for k in range(NT):
            rows = slice(k * group, (k + 1) * group)
            both = add_refs[0][rows, :].astype(F32) + add_refs[1][rows, :].astype(F32)
            o_refs[k][count * group :, :] = both.astype(BF16)


def stage(z, arrays, addends=()):
    tok, inner = arrays[0].shape
    parts = len(arrays) + len(addends) // 2
    vm = pl.BlockSpec(memory_space=pltpu.VMEM)
    shape = jax.ShapeDtypeStruct((parts * inner // NT, tok), BF16)
    return pl.pallas_call(
        functools.partial(stage_kernel, count=len(arrays)),
        out_shape=(shape,) * NT,
        in_specs=[pl.BlockSpec(memory_space=pltpu.SMEM)] + [vm] * (len(arrays) + len(addends)),
        out_specs=(vm,) * NT,
        scratch_shapes=[pltpu.VMEM((inner, tok), BF16)],
        cost_estimate=pl.CostEstimate(
            flops=0, transcendentals=0, bytes_accessed=4 * parts * tok * inner
        ),
        compiler_params=pltpu.CompilerParams(vmem_limit_bytes=SMALL_LIMIT),
        name="stage",
    )(z[None], *arrays, *addends)


def caption_kernel(z_ref, c_ref, proj_ref, states_ref, keep_ref, send_ref, scratch):
    scratch[...] = lax.dot_general(
        proj_ref[...], states_ref[...], (((0,), (1,)), ((), ())), preferred_element_type=F32
    ).astype(BF16)
    inner = scratch.shape[0] // 2
    half = inner // (2 * NT)
    for o_ref, core in ((keep_ref, c_ref[0]), (send_ref, 1 - c_ref[0])):
        for k in range(NT):
            for a in range(2):
                start = a * inner + ((z_ref[0] + k) % NT * 2 + core) * half
                at = (2 * k + a) * half
                o_ref[at : at + half, :] = scratch[pl.ds(pl.multiple_of(start, half), half), :]


def caption_partial(z, c, proj, states):
    features, width = proj.shape
    cap = states.shape[0]
    vm = pl.BlockSpec(memory_space=pltpu.VMEM)
    smem = pl.BlockSpec(memory_space=pltpu.SMEM)
    shape = jax.ShapeDtypeStruct((width // 2, cap), BF16)
    return pl.pallas_call(
        caption_kernel,
        out_shape=(shape, shape),
        in_specs=[smem, smem, vm, vm],
        out_specs=(vm, vm),
        scratch_shapes=[pltpu.VMEM((width, cap), BF16)],
        cost_estimate=pl.CostEstimate(
            flops=2 * width * cap * features, transcendentals=0, bytes_accessed=4 * width * cap
        ),
        compiler_params=pltpu.CompilerParams(vmem_limit_bytes=SMALL_LIMIT),
        name="caption_partial",
    )(z[None], c[None], proj, states)


def pack_kernel(*refs, rows, count):
    o_ref, total = refs[count], None
    for i, ref in enumerate(refs[:count]):
        o_ref[i * rows : (i + 1) * rows, :] = ref[0:rows, :]
        if ref.shape[0] > rows:
            more = ref[rows:, :].astype(F32)
            total = more if total is None else total + more
    if total is not None:
        refs[count + 1][...] = total.astype(BF16)


def pack(chunks, rows):
    tok = chunks[0].shape[1]
    added = chunks[0].shape[0] - rows
    vm = pl.BlockSpec(memory_space=pltpu.VMEM)
    shapes = [jax.ShapeDtypeStruct((len(chunks) * rows, tok), BF16)]
    if added:
        shapes.append(jax.ShapeDtypeStruct((added, tok), BF16))
    return pl.pallas_call(
        functools.partial(pack_kernel, rows=rows, count=len(chunks)),
        out_shape=tuple(shapes),
        in_specs=[vm] * len(chunks),
        out_specs=(vm,) * len(shapes),
        compiler_params=pltpu.CompilerParams(vmem_limit_bytes=SMALL_LIMIT),
        name="pack",
    )(*chunks)


def halves_kernel(x_ref, y_ref, upper_ref, lower_ref):
    half = upper_ref.shape[0]
    upper_ref[...] = x_ref[0:half, :]
    lower_ref[...] = y_ref[half:, :]


def halves(x, y):
    rows, cols = x.shape
    vm = pl.BlockSpec(memory_space=pltpu.VMEM)
    shape = jax.ShapeDtypeStruct((rows // 2, cols), x.dtype)
    return pl.pallas_call(
        halves_kernel,
        out_shape=(shape, shape),
        in_specs=[vm, vm],
        out_specs=(vm, vm),
        compiler_params=pltpu.CompilerParams(vmem_limit_bytes=6 * 2**20),
        name="halves",
    )(x, y)


def unstage_kernel(z_ref, *refs):
    x_refs, o_ref, scratch = refs[:NT], refs[NT], refs[NT + 1]
    group = x_refs[0].shape[0]
    for k in range(NT):
        start = pl.multiple_of((z_ref[0] + k) % NT * group, group)
        scratch[pl.ds(start, group), :] = x_refs[k][...]
    for c in range(0, NT * group, LANES):
        o_ref[:, c : c + LANES] = scratch[c : c + LANES, :].T


def unstage(z, pieces):
    group, tok = pieces[0].shape
    vm = pl.BlockSpec(memory_space=pltpu.VMEM)
    return pl.pallas_call(
        unstage_kernel,
        out_shape=jax.ShapeDtypeStruct((tok, NT * group), BF16),
        in_specs=[pl.BlockSpec(memory_space=pltpu.SMEM)] + [vm] * NT,
        out_specs=vm,
        scratch_shapes=[pltpu.VMEM((NT * group, tok), BF16)],
        compiler_params=pltpu.CompilerParams(vmem_limit_bytes=VMEM_LIMIT),
        name="unstage",
    )(z[None], *pieces)


def attention_kernel(len_ref, core_ref, q_ref, *refs, tiles, sources, first, last, block_q, block_k):
    kv_refs, refs = refs[:sources], refs[sources:]
    old_ref = None
    if not first:
        old_ref, refs = refs[0], refs[1:]
    if last:
        piece_refs, cap_ref, refs = refs[:2], refs[-3], refs[2:-3] + refs[-2:]
        half = cap_ref.shape[0] // 4
        for flip in range(2):
            one = slice(2 * flip * half, 2 * (flip + 1) * half)
            rows = piece_refs[0][one, :].astype(F32) + piece_refs[1][one, :].astype(F32)
            rows = rows.astype(BF16)
            for a in range(2):
                start = pl.multiple_of((2 * a + (core_ref[0] ^ flip)) * half, half)
                cap_ref[pl.ds(start, half), :] = rows[a * half : (a + 1) * half]
    o_refs, (keys, vals) = refs[:-2], refs[-2:]
    inner, tok = q_ref.shape[0] // tiles, q_ref.shape[1]
    heads = inner // HD
    total = keys.shape[1]
    cap = cap_ref.shape[1] if last else 0
    length = len_ref[0]
    pairs = [
        (ref[r : r + inner, :], ref[r + inner : r + 2 * inner, :])
        for ref in kv_refs
        for r in range(0, ref.shape[0] // (2 * inner) * 2 * inner, 2 * inner)
    ]

    def place(col, k, v, kept):
        n = k.shape[1]
        for h in range(heads):
            keys[h, col : col + n, :] = k[h * HD : (h + 1) * HD].T
            vh = v[h * HD : (h + 1) * HD]
            one = jnp.ones((ONES, n), BF16)
            if kept is not None:
                vh = jnp.where(kept, vh, BF16(0))
                one = jnp.where(kept, one, BF16(0))
            vals[h, 0:HD, col : col + n] = vh
            vals[h, HD : HD + ONES, col : col + n] = one

    kmax = None
    for b, (k, v) in enumerate(pairs):
        place(b * tok, k, v, None)
        norms = head_norms(k, heads)
        kmax = norms if kmax is None else jnp.maximum(kmax, norms)
    if last:
        kept = lax.broadcasted_iota(jnp.int32, (1, cap), 1) < length
        ck = cap_ref[0:inner, :]
        place(len(pairs) * tok, ck, cap_ref[inner : 2 * inner, :], kept)
        kmax = jnp.maximum(kmax, head_norms(ck, heads))
    qmax = None
    for i in range(tiles):
        norms = head_norms(q_ref[i * inner : (i + 1) * inner, :], heads)
        qmax = norms if qmax is None else jnp.maximum(qmax, norms)
    small = jnp.max(qmax * kmax) < HD * SAFE_BOUND * SAFE_BOUND
    if not first:
        offset = jnp.max(jnp.abs(old_ref[0, HD + ONES :, :]))
        for h in range(1, heads):
            offset = jnp.maximum(offset, jnp.max(jnp.abs(old_ref[h, HD + ONES :, :])))
        small = jnp.logical_and(small, offset == 0.0)

    per = block_q // tok

    def block(h, start, safe):
        rows = pl.ds(pl.multiple_of(h * HD, HD), HD)
        cols = slice(start * tok, start * tok + block_q)
        at = [pl.multiple_of((start + b) * inner + h * HD, HD) for b in range(per)]
        qt = jnp.concatenate([q_ref[pl.ds(i, HD), :] for i in at], axis=1)
        qt = qt * BF16(0.125)
        acc = None if first else old_ref[h, 0 : HD + ONES, cols]
        m = jnp.zeros((8, block_q), F32)
        if safe:
            n = tok

            def score(c):
                s0 = pl.multiple_of(c * n, n)
                s = jnp.dot(keys[h, pl.ds(s0, n), :], qt, preferred_element_type=F32)
                if not last:
                    return s
                key = lax.broadcasted_iota(jnp.int32, (n, 1), 0) + s0
                return jnp.where(key < total - cap + length, s, -1e30)

            def peak(c, m):
                return jnp.maximum(m, jnp.max(score(c), axis=0, keepdims=True))

            old = jnp.full((1, block_q), -1e30, F32)
            if not first:
                old = old_ref[h, HD + ONES : HD + ONES + 1, cols]
            m = lax.fori_loop(0, total // n, peak, old)
            if first:
                acc = jnp.zeros((HD + ONES, block_q), F32)
            else:
                acc = acc * jnp.exp2((old - m) * LOG2E)

            def step(c, acc):
                p = jnp.exp2((score(c) - m) * LOG2E).astype(BF16)
                v = vals[h, :, pl.ds(pl.multiple_of(c * n, n), n)]
                return acc + jnp.dot(v, p, preferred_element_type=F32)

            acc = lax.fori_loop(0, total // n, step, acc)
        else:
            for c in range(0, total, block_k):
                n = min(block_k, total - c)
                s = jnp.dot(keys[h, c : c + n, :], qt, preferred_element_type=F32)
                p = jnp.exp2(s * LOG2E).astype(BF16)
                t = jnp.dot(vals[h, :, c : c + n], p, preferred_element_type=F32)
                acc = t if acc is None else acc + t
        if last:
            out = (acc[0:HD] / acc[HD : HD + 1]).astype(BF16)
            for b in range(per):
                o_refs[start + b][rows, :] = out[:, b * tok : (b + 1) * tok]
        else:
            o_refs[0][h, 0 : HD + ONES, cols] = acc
            o_refs[0][h, HD + ONES :, cols] = jnp.broadcast_to(m, (8, block_q))

    def run(safe):
        for start in range(0, tiles, per):
            lax.fori_loop(0, heads, lambda h, _: (block(h, start, safe), 0)[1], 0)

    @pl.when(small)
    def _():
        run(False)

    @pl.when(jnp.logical_not(small))
    def _():
        run(True)


def attention(length, core, queries, kvs, state=None, caption=(), block_q=512):
    inner, tok = queries.shape[0] // NT, queries.shape[1]
    heads = inner // HD
    tiles = NT
    first, last = state is None, bool(caption)
    blocks = sum(x.shape[0] // (2 * inner) for x in kvs)
    total = blocks * tok + (caption[0].shape[1] if last else 0)
    smem = pl.BlockSpec(memory_space=pltpu.SMEM)
    vm = pl.BlockSpec(memory_space=pltpu.VMEM)
    operands = (queries, *kvs, *(() if first else (state,)), *caption)
    if last:
        out_shape = (jax.ShapeDtypeStruct((inner, tok), BF16),) * tiles
    else:
        out_shape = (jax.ShapeDtypeStruct((heads, HD + ONES + 8, tiles * tok), F32),)
    return pl.pallas_call(
        functools.partial(
            attention_kernel,
            tiles=tiles,
            sources=len(kvs),
            first=first,
            last=last,
            block_q=block_q,
            block_k=total // 2,
        ),
        out_shape=out_shape,
        in_specs=[smem, smem]
        + [vm] * len(operands),
        out_specs=(vm,) * len(out_shape),
        scratch_shapes=([pltpu.VMEM((2 * inner, tok), BF16)] if last else [])
        + [
            pltpu.VMEM((heads, total, HD), BF16),
            pltpu.VMEM((heads, HD + ONES, total), BF16),
        ],
        cost_estimate=pl.CostEstimate(flops=0, transcendentals=0, bytes_accessed=0),
        compiler_params=pltpu.CompilerParams(vmem_limit_bytes=VMEM_LIMIT),
        name="attention",
    )(length, core[None], *operands)


def grad_kernel(t_ref, core_ref, *refs, tiles, part, step, flip):
    o_refs, cot_refs, g_ref = refs[:tiles], refs[tiles:-1], refs[-1]
    width = cot_refs[0].shape[1]
    dp, pairs, chunk, _ = g_ref.shape
    rows = [
        pl.ds(pl.multiple_of((2 * s + (core_ref[0] ^ flip)) * part, 16), part) for s in range(pairs)
    ]
    left = jnp.concatenate(
        [jnp.concatenate([ref[r, :] for ref in o_refs], axis=1) for r in rows], axis=0
    )
    time = jnp.full((1, step), t_ref[0], jnp.int32).astype(F32)
    weight = 1.0 + 3.0 * (time + 0.5) / 1000.0
    for c in range(0, width, step):
        n = min(step, width - c)
        right = jnp.concatenate([ref[:, c : c + n] for ref in cot_refs], axis=0)
        g = (jnp.dot(left, right, preferred_element_type=F32) * weight[:, :n]).astype(BF16)
        for t in range(n // LANES):
            cols = slice(t * LANES, (t + 1) * LANES)
            for s in range(pairs):
                done = 0
                while done < part:
                    flat = (c // LANES + t) * part + done
                    count = min(part - done, chunk - flat % chunk)
                    g_ref[flat // chunk, s, flat % chunk : flat % chunk + count, :] = g[
                        s * part + done : s * part + done + count, cols
                    ]
                    done += count
    used = width // LANES * part - (dp - 1) * chunk
    if used < chunk:
        for s in range(pairs):
            g_ref[dp - 1, s, used:, :] = jnp.zeros((chunk - used, LANES), BF16)


def local_grad(timestep, core, flip, attended, cots, part, dp):
    inner, tok = attended[0].shape
    width = cots[0].shape[1]
    pairs = inner // (2 * part)
    chunk = -(-(width // LANES * part) // (dp * 16)) * 16
    vm = pl.BlockSpec(memory_space=pltpu.VMEM)
    smem = pl.BlockSpec(memory_space=pltpu.SMEM)
    tiles = len(attended)
    step = 2 * LANES
    return pl.pallas_call(
        functools.partial(grad_kernel, tiles=tiles, part=part, step=step, flip=flip),
        out_shape=jax.ShapeDtypeStruct((dp, pairs, chunk, LANES), BF16),
        in_specs=[smem, smem] + [vm] * (tiles + len(cots)),
        out_specs=vm,
        cost_estimate=pl.CostEstimate(
            flops=tiles * tok * inner * width,
            transcendentals=0,
            bytes_accessed=2 * tiles * tok * (inner + width) + inner * width,
        ),
        compiler_params=pltpu.CompilerParams(vmem_limit_bytes=16 * 2**20),
        name="local_grad",
    )(timestep, core[None], *attended, *cots)


def add_two_kernel(x_ref, y_ref, o_ref):
    o_ref[...] = (x_ref[...].astype(F32) + y_ref[...].astype(F32)).astype(BF16)


def add_two(x, y):
    vm = pl.BlockSpec(memory_space=pltpu.VMEM)
    return pl.pallas_call(
        add_two_kernel,
        out_shape=jax.ShapeDtypeStruct(x.shape, BF16),
        in_specs=[vm, vm],
        out_specs=vm,
        compiler_params=pltpu.CompilerParams(vmem_limit_bytes=SMALL_LIMIT),
        name="add_two",
    )(x, y)


def add_pieces_kernel(x_ref, o_ref, s_ref):
    total = x_ref[0].astype(F32)
    for i in range(1, x_ref.shape[0]):
        total = total + x_ref[i].astype(F32)
    total = total.astype(BF16)
    o_ref[...] = total
    x = total.astype(F32)
    rows = jnp.sum(x * x, axis=0, keepdims=True)
    s_ref[...] = jnp.broadcast_to(jnp.sum(rows, axis=1, keepdims=True), s_ref.shape)


def add_pieces(x, peers):
    vm = pl.BlockSpec(memory_space=pltpu.VMEM)
    return pl.pallas_call(
        add_pieces_kernel,
        out_shape=(
            jax.ShapeDtypeStruct(x.shape[1:], BF16),
            jax.ShapeDtypeStruct((peers, LANES), F32),
        ),
        in_specs=[vm],
        out_specs=(vm, vm),
        compiler_params=pltpu.CompilerParams(vmem_limit_bytes=SMALL_LIMIT),
        name="add_pieces",
    )(x)


def adam_kernel(at_ref, s_ref, *refs):
    g_refs, refs, g_ref = refs[:4], refs[4:-1], refs[-1]
    chunk = g_refs[0].shape[1]
    for k, ref in enumerate(g_refs):
        for i in range(2):
            at = (at_ref[0] ^ i) * 4 + (at_ref[1] + 4 - k) % 4
            rows = pl.ds(pl.multiple_of(at * chunk, chunk), chunk)
            g_ref[rows, :] = ref[i]
    adam_rows(s_ref, g_ref, *refs)


def adam_rows(s_ref, g_ref, w_ref, mv_ref, ms_ref, vv_ref, vs_ref, nw, nmv, nms, nvv, nvs):
    rows, width = w_ref.shape
    squares = jnp.sum(s_ref[...], axis=0, keepdims=True)
    factor = 256.0 / jnp.sqrt(squares + 1e-06)
    diagonal = lax.broadcasted_iota(jnp.int32, (rows, rows), 0) == lax.broadcasted_iota(
        jnp.int32, (rows, rows), 1
    )

    def down(row):
        return jnp.sum(jnp.where(diagonal, row, 0.0), axis=1, keepdims=True)

    def across(column):
        return jnp.sum(jnp.where(diagonal, column, 0.0), axis=0, keepdims=True)

    for t in range(width // LANES):
        cols = slice(t * LANES, (t + 1) * LANES)
        one = slice(t, t + 1)
        g = g_ref[t * rows : (t + 1) * rows, :].astype(F32) * factor
        first = mv_ref[:, cols].astype(F32) * down(ms_ref[one, :])
        second = vv_ref[:, cols].astype(F32) * down(vs_ref[one, :])
        first = 0.9 * first + 0.1 * g
        second = 0.999 * second + 0.001 * g * g
        update = first / (1.0 - 0.9**10) / (jnp.sqrt(second / (1.0 - 0.999**10)) + 1e-08)
        nw[:, cols] = (w_ref[:, cols].astype(F32) - 0.02 * update).astype(BF16)
        fs = jnp.max(jnp.abs(first), axis=1, keepdims=True) + 1e-06
        ss = jnp.max(jnp.abs(second), axis=1, keepdims=True) + 1e-06
        nms[one, :] = across(fs)
        nvs[one, :] = across(ss)
        nmv[:, cols] = (first / fs).astype(BF16)
        nvv[:, cols] = (second / ss).astype(BF16)


def adam(at, squares, grads, out_weight, mom_val, mom_scale, var_val, var_scale):
    vm = pl.BlockSpec(memory_space=pltpu.VMEM)
    like = lambda a: jax.ShapeDtypeStruct(a.shape, a.dtype)
    mom_scale, var_scale = mom_scale.T, var_scale.T
    new_weight, first_val, first_scale, second_val, second_scale = pl.pallas_call(
        adam_kernel,
        out_shape=(like(out_weight), like(mom_val), like(mom_scale), like(var_val), like(var_scale)),
        in_specs=[pl.BlockSpec(memory_space=pltpu.SMEM)] + [vm] * 10,
        out_specs=(vm,) * 5,
        scratch_shapes=[pltpu.VMEM((8 * grads[0].shape[1], LANES), BF16)],
        compiler_params=pltpu.CompilerParams(vmem_limit_bytes=SMALL_LIMIT),
        name="adam",
    )(at, squares, *grads, out_weight, mom_val, mom_scale, var_val, var_scale)
    return new_weight, first_val, first_scale.T, second_val, second_scale.T


def swap(x, axis):
    return lax.ppermute(x, axis, [(0, 1), (1, 0)])


def shift(x, k):
    return lax.ppermute(x, "z", [(i, (i + k) % NT) for i in range(NT)])


def body(
    latent_q,
    latent_k,
    latent_v,
    caption_states,
    caption_proj,
    caption_len,
    timestep,
    out_cot,
    out_weight,
    mom_val,
    mom_scale,
    var_val,
    var_scale,
):
    tok, inner = latent_q.shape[1:]
    cap = caption_states.shape[1]
    xh, z, c = lax.axis_index("xh"), lax.axis_index("z"), lax.axis_index("c")

    keep, send = caption_partial(z, c, caption_proj, caption_states[0])
    other = swap(send, "c")

    group = inner // NT
    staged = stage(z, (latent_k[0], latent_v[0]))
    kvs = [staged[0]] + [shift(staged[k], k) for k in range(1, NT)]
    staged = stage(z, (latent_q[0],), (keep, other))
    queries = [staged[0]] + [shift(staged[k], k) for k in range(1, NT)]
    far_own, far_next = swap(kvs[0], "xh"), swap(kvs[1], "xh")
    held = lax.optimization_barrier((*kvs, *queries, far_own, far_next))
    kvs, queries, far_own, far_next = held[:NT], held[NT : 2 * NT], held[-2], held[-1]

    (ring,), (rest,) = pack(kvs, 2 * group), pack(kvs[2:], 2 * group)
    near, far = swap(ring, "c"), swap(rest, "xh")
    queries, here = pack(queries, group)
    (here,) = pack((here, swap(here, "c")), group)

    cot, queries = lax.optimization_barrier((out_cot[0], queries))
    before, after = shift(cot, 1), shift(cot, -1)
    there, last_own, last_next = swap(here, "xh"), swap(far_own, "c"), swap(far_next, "c")

    (state,) = attention(caption_len, c, queries, [ring, near])
    held = lax.optimization_barrier((state, far, last_own, last_next))
    state, far, last_own, last_next = held
    last = swap(far, "c")
    (state,) = attention(caption_len, c, queries, [far_own, far_next, far], state, block_q=NT * tok)
    state, before, after, there = lax.optimization_barrier((state, before, after, there))
    upper, lower = halves(before, after)
    cots = [cot, before, shift(upper, 1), shift(lower, -1), after]
    kvs = [last_own, last_next, last]
    attended = attention(caption_len, c, queries, kvs, state, (here, there), NT * tok)
    back = [attended[0]] + [shift(attended[k], -k) for k in range(1, NT)]

    rows = out_weight.shape[0]
    dp = lax.axis_size("xl") * lax.axis_size("y")
    other = swap(local_grad(timestep, c, 1, attended, cots, rows, dp), "c")
    grad = local_grad(timestep, c, 0, attended, cots, rows, dp)
    chunk = grad.shape[2]
    grad = add_two(grad, other)
    grad = lax.all_to_all(
        grad.reshape(2 * dp, chunk, LANES), ("xl", "y", "xh"), 0, 0, tiled=True
    )
    grad, *back = lax.optimization_barrier((grad, *back))
    everyone = ("xl", "y", "xh", "z", "c")
    grad, squares = add_pieces(grad, lax.axis_size(everyone))
    pair = []
    for flip in range(2):
        perm = []
        for i in range(4 * NT):
            xl, s, t = i // (2 * NT), i // NT % 2, i % NT
            perm.append((i, (xl ^ flip) * 2 * NT + t // 2 * NT + t % 2 * 2 + s))
        pair.append(lax.ppermute(grad, ("xl", "xh", "z"), perm))
    pair = jnp.stack(pair)
    squares = lax.all_to_all(squares, everyone, 0, 0, tiled=True)
    grads = [pair] + [
        lax.ppermute(pair, "y", [(i, (i + k) % 4) for i in range(4)]) for k in range(1, 4)
    ]
    at = jnp.stack([lax.axis_index("xl"), lax.axis_index("y")])
    attn_out = unstage(z, back)[None]
    updated = adam(at, squares, grads, out_weight, mom_val, mom_scale, var_val, var_scale)
    return (attn_out, *updated)


def solution(mesh):
    fine = Mesh(mesh.devices.reshape(2, 4, 2, NT, 2), ("xl", "y", "xh", "z", "c"))
    dp = ("xl", "y")
    ctx = ("xh", "z", "c")
    tokens = P(dp, ctx, None)
    rows = P(ctx, None)
    return jax.shard_map(
        body,
        mesh=fine,
        in_specs=(
            tokens,
            tokens,
            tokens,
            P(dp, None, ctx),
            rows,
            P(dp),
            P(dp),
            tokens,
            rows,
            rows,
            rows,
            rows,
            rows,
        ),
        out_specs=(tokens, rows, rows, rows, rows, rows),
        check_vma=False,
    )
```

```python
import functools
import math

import jax
import jax.numpy as jnp
from jax import lax
from jax.experimental import pallas as pl
from jax.experimental.pallas import tpu as pltpu
from jax.sharding import Mesh, PartitionSpec as P

HD = 64
LANES = 128
ONES = 16
LOG2E = math.log2(math.e)
SAFE_BOUND = 60.0
F32 = jnp.float32
BF16 = jnp.bfloat16
NT = 4
VMEM_LIMIT = 16 * 2**20
SMALL_LIMIT = 10 * 2**20


def head_norms(x, heads):
    x = x.astype(F32)
    x = x * x
    rows = [jnp.sum(x[h * HD : (h + 1) * HD], axis=0, keepdims=True) for h in range(heads)]
    return jnp.max(jnp.concatenate(rows, axis=0), axis=1, keepdims=True)


def rel_rows(z_ref, k, group):
    return pl.ds(pl.multiple_of((z_ref[0] + k) % NT * group, group), group)


def stage_kernel(z_ref, *refs, count):
    x_refs, refs = refs[:count], refs[count:]
    add_refs, o_refs, scratch = refs[: -NT - 1], refs[-NT - 1 : -1], refs[-1]
    inner = scratch.shape[0]
    group = inner // NT
    for a, x_ref in enumerate(x_refs):
        for c in range(0, inner, LANES):
            scratch[c : c + LANES, :] = x_ref[:, c : c + LANES].T
        for k in range(NT):
            o_refs[k][a * group : (a + 1) * group, :] = scratch[rel_rows(z_ref, k, group), :]
    if add_refs:
        for k in range(NT):
            rows = slice(k * group, (k + 1) * group)
            both = add_refs[0][rows, :].astype(F32) + add_refs[1][rows, :].astype(F32)
            o_refs[k][count * group :, :] = both.astype(BF16)


def stage(z, arrays, addends=()):
    tok, inner = arrays[0].shape
    parts = len(arrays) + len(addends) // 2
    vm = pl.BlockSpec(memory_space=pltpu.VMEM)
    shape = jax.ShapeDtypeStruct((parts * inner // NT, tok), BF16)
    return pl.pallas_call(
        functools.partial(stage_kernel, count=len(arrays)),
        out_shape=(shape,) * NT,
        in_specs=[pl.BlockSpec(memory_space=pltpu.SMEM)] + [vm] * (len(arrays) + len(addends)),
        out_specs=(vm,) * NT,
        scratch_shapes=[pltpu.VMEM((inner, tok), BF16)],
        cost_estimate=pl.CostEstimate(
            flops=0, transcendentals=0, bytes_accessed=4 * parts * tok * inner
        ),
        compiler_params=pltpu.CompilerParams(vmem_limit_bytes=SMALL_LIMIT),
        name="stage",
    )(z[None], *arrays, *addends)


def caption_kernel(z_ref, c_ref, proj_ref, states_ref, keep_ref, send_ref, scratch):
    scratch[...] = lax.dot_general(
        proj_ref[...], states_ref[...], (((0,), (1,)), ((), ())), preferred_element_type=F32
    ).astype(BF16)
    inner = scratch.shape[0] // 2
    half = inner // (2 * NT)
    for o_ref, core in ((keep_ref, c_ref[0]), (send_ref, 1 - c_ref[0])):
        for k in range(NT):
            for a in range(2):
                start = a * inner + ((z_ref[0] + k) % NT * 2 + core) * half
                at = (2 * k + a) * half
                o_ref[at : at + half, :] = scratch[pl.ds(pl.multiple_of(start, half), half), :]


def caption_partial(z, c, proj, states):
    features, width = proj.shape
    cap = states.shape[0]
    vm = pl.BlockSpec(memory_space=pltpu.VMEM)
    smem = pl.BlockSpec(memory_space=pltpu.SMEM)
    shape = jax.ShapeDtypeStruct((width // 2, cap), BF16)
    return pl.pallas_call(
        caption_kernel,
        out_shape=(shape, shape),
        in_specs=[smem, smem, vm, vm],
        out_specs=(vm, vm),
        scratch_shapes=[pltpu.VMEM((width, cap), BF16)],
        cost_estimate=pl.CostEstimate(
            flops=2 * width * cap * features, transcendentals=0, bytes_accessed=4 * width * cap
        ),
        compiler_params=pltpu.CompilerParams(vmem_limit_bytes=SMALL_LIMIT),
        name="caption_partial",
    )(z[None], c[None], proj, states)


def pack_kernel(*refs, rows, count):
    o_ref, total = refs[count], None
    for i, ref in enumerate(refs[:count]):
        o_ref[i * rows : (i + 1) * rows, :] = ref[0:rows, :]
        if ref.shape[0] > rows:
            more = ref[rows:, :].astype(F32)
            total = more if total is None else total + more
    if total is not None:
        refs[count + 1][...] = total.astype(BF16)


def pack(chunks, rows):
    tok = chunks[0].shape[1]
    added = chunks[0].shape[0] - rows
    vm = pl.BlockSpec(memory_space=pltpu.VMEM)
    shapes = [jax.ShapeDtypeStruct((len(chunks) * rows, tok), BF16)]
    if added:
        shapes.append(jax.ShapeDtypeStruct((added, tok), BF16))
    return pl.pallas_call(
        functools.partial(pack_kernel, rows=rows, count=len(chunks)),
        out_shape=tuple(shapes),
        in_specs=[vm] * len(chunks),
        out_specs=(vm,) * len(shapes),
        compiler_params=pltpu.CompilerParams(vmem_limit_bytes=SMALL_LIMIT),
        name="pack",
    )(*chunks)


def halves_kernel(x_ref, y_ref, upper_ref, lower_ref):
    half = upper_ref.shape[0]
    upper_ref[...] = x_ref[0:half, :]
    lower_ref[...] = y_ref[half:, :]


def halves(x, y):
    rows, cols = x.shape
    vm = pl.BlockSpec(memory_space=pltpu.VMEM)
    shape = jax.ShapeDtypeStruct((rows // 2, cols), x.dtype)
    return pl.pallas_call(
        halves_kernel,
        out_shape=(shape, shape),
        in_specs=[vm, vm],
        out_specs=(vm, vm),
        compiler_params=pltpu.CompilerParams(vmem_limit_bytes=6 * 2**20),
        name="halves",
    )(x, y)


def unstage_kernel(z_ref, *refs):
    x_refs, o_ref, scratch = refs[:NT], refs[NT], refs[NT + 1]
    group = x_refs[0].shape[0]
    for k in range(NT):
        start = pl.multiple_of((z_ref[0] + k) % NT * group, group)
        scratch[pl.ds(start, group), :] = x_refs[k][...]
    for c in range(0, NT * group, LANES):
        o_ref[:, c : c + LANES] = scratch[c : c + LANES, :].T


def unstage(z, pieces):
    group, tok = pieces[0].shape
    vm = pl.BlockSpec(memory_space=pltpu.VMEM)
    return pl.pallas_call(
        unstage_kernel,
        out_shape=jax.ShapeDtypeStruct((tok, NT * group), BF16),
        in_specs=[pl.BlockSpec(memory_space=pltpu.SMEM)] + [vm] * NT,
        out_specs=vm,
        scratch_shapes=[pltpu.VMEM((NT * group, tok), BF16)],
        compiler_params=pltpu.CompilerParams(vmem_limit_bytes=VMEM_LIMIT),
        name="unstage",
    )(z[None], *pieces)


def attention_kernel(len_ref, core_ref, q_ref, *refs, tiles, sources, first, last, block_q, block_k):
    kv_refs, refs = refs[:sources], refs[sources:]
    old_ref = None
    if not first:
        old_ref, refs = refs[0], refs[1:]
    if last:
        piece_refs, cap_ref, refs = refs[:2], refs[-3], refs[2:-3] + refs[-2:]
        half = cap_ref.shape[0] // 4
        for flip in range(2):
            one = slice(2 * flip * half, 2 * (flip + 1) * half)
            rows = piece_refs[0][one, :].astype(F32) + piece_refs[1][one, :].astype(F32)
            rows = rows.astype(BF16)
            for a in range(2):
                start = pl.multiple_of((2 * a + (core_ref[0] ^ flip)) * half, half)
                cap_ref[pl.ds(start, half), :] = rows[a * half : (a + 1) * half]
    o_refs, (keys, vals) = refs[:-2], refs[-2:]
    inner, tok = q_ref.shape[0] // tiles, q_ref.shape[1]
    heads = inner // HD
    total = keys.shape[1]
    cap = cap_ref.shape[1] if last else 0
    length = len_ref[0]
    pairs = [
        (ref[r : r + inner, :], ref[r + inner : r + 2 * inner, :])
        for ref in kv_refs
        for r in range(0, ref.shape[0] // (2 * inner) * 2 * inner, 2 * inner)
    ]

    def place(col, k, v, kept):
        n = k.shape[1]
        for h in range(heads):
            keys[h, col : col + n, :] = k[h * HD : (h + 1) * HD].T
            vh = v[h * HD : (h + 1) * HD]
            one = jnp.ones((ONES, n), BF16)
            if kept is not None:
                vh = jnp.where(kept, vh, BF16(0))
                one = jnp.where(kept, one, BF16(0))
            vals[h, 0:HD, col : col + n] = vh
            vals[h, HD : HD + ONES, col : col + n] = one

    kmax = None
    for b, (k, v) in enumerate(pairs):
        place(b * tok, k, v, None)
        norms = head_norms(k, heads)
        kmax = norms if kmax is None else jnp.maximum(kmax, norms)
    if last:
        kept = lax.broadcasted_iota(jnp.int32, (1, cap), 1) < length
        ck = cap_ref[0:inner, :]
        place(len(pairs) * tok, ck, cap_ref[inner : 2 * inner, :], kept)
        kmax = jnp.maximum(kmax, head_norms(ck, heads))
    qmax = None
    for i in range(tiles):
        norms = head_norms(q_ref[i * inner : (i + 1) * inner, :], heads)
        qmax = norms if qmax is None else jnp.maximum(qmax, norms)
    small = jnp.max(qmax * kmax) < HD * SAFE_BOUND * SAFE_BOUND
    if not first:
        offset = jnp.max(jnp.abs(old_ref[0, HD + ONES :, :]))
        for h in range(1, heads):
            offset = jnp.maximum(offset, jnp.max(jnp.abs(old_ref[h, HD + ONES :, :])))
        small = jnp.logical_and(small, offset == 0.0)

    per = block_q // tok

    def block(h, start, safe):
        rows = pl.ds(pl.multiple_of(h * HD, HD), HD)
        cols = slice(start * tok, start * tok + block_q)
        at = [pl.multiple_of((start + b) * inner + h * HD, HD) for b in range(per)]
        qt = jnp.concatenate([q_ref[pl.ds(i, HD), :] for i in at], axis=1)
        qt = qt * BF16(0.125)
        acc = None if first else old_ref[h, 0 : HD + ONES, cols]
        m = jnp.zeros((8, block_q), F32)
        if safe:
            n = tok

            def score(c):
                s0 = pl.multiple_of(c * n, n)
                s = jnp.dot(keys[h, pl.ds(s0, n), :], qt, preferred_element_type=F32)
                if not last:
                    return s
                key = lax.broadcasted_iota(jnp.int32, (n, 1), 0) + s0
                return jnp.where(key < total - cap + length, s, -1e30)

            def peak(c, m):
                return jnp.maximum(m, jnp.max(score(c), axis=0, keepdims=True))

            old = jnp.full((1, block_q), -1e30, F32)
            if not first:
                old = old_ref[h, HD + ONES : HD + ONES + 1, cols]
            m = lax.fori_loop(0, total // n, peak, old)
            if first:
                acc = jnp.zeros((HD + ONES, block_q), F32)
            else:
                acc = acc * jnp.exp2((old - m) * LOG2E)

            def step(c, acc):
                p = jnp.exp2((score(c) - m) * LOG2E).astype(BF16)
                v = vals[h, :, pl.ds(pl.multiple_of(c * n, n), n)]
                return acc + jnp.dot(v, p, preferred_element_type=F32)

            acc = lax.fori_loop(0, total // n, step, acc)
        else:
            for c in range(0, total, block_k):
                n = min(block_k, total - c)
                s = jnp.dot(keys[h, c : c + n, :], qt, preferred_element_type=F32)
                p = jnp.exp2(s * LOG2E).astype(BF16)
                t = jnp.dot(vals[h, :, c : c + n], p, preferred_element_type=F32)
                acc = t if acc is None else acc + t
        if last:
            out = (acc[0:HD] / acc[HD : HD + 1]).astype(BF16)
            for b in range(per):
                o_refs[start + b][rows, :] = out[:, b * tok : (b + 1) * tok]
        else:
            o_refs[0][h, 0 : HD + ONES, cols] = acc
            o_refs[0][h, HD + ONES :, cols] = jnp.broadcast_to(m, (8, block_q))

    def run(safe):
        for start in range(0, tiles, per):
            lax.fori_loop(0, heads, lambda h, _: (block(h, start, safe), 0)[1], 0)

    @pl.when(small)
    def _():
        run(False)

    @pl.when(jnp.logical_not(small))
    def _():
        run(True)


def attention(length, core, queries, kvs, state=None, caption=(), block_q=512):
    inner, tok = queries.shape[0] // NT, queries.shape[1]
    heads = inner // HD
    tiles = NT
    first, last = state is None, bool(caption)
    blocks = sum(x.shape[0] // (2 * inner) for x in kvs)
    total = blocks * tok + (caption[0].shape[1] if last else 0)
    smem = pl.BlockSpec(memory_space=pltpu.SMEM)
    vm = pl.BlockSpec(memory_space=pltpu.VMEM)
    operands = (queries, *kvs, *(() if first else (state,)), *caption)
    if last:
        out_shape = (jax.ShapeDtypeStruct((inner, tok), BF16),) * tiles
    else:
        out_shape = (jax.ShapeDtypeStruct((heads, HD + ONES + 8, tiles * tok), F32),)
    return pl.pallas_call(
        functools.partial(
            attention_kernel,
            tiles=tiles,
            sources=len(kvs),
            first=first,
            last=last,
            block_q=block_q,
            block_k=total // 2,
        ),
        out_shape=out_shape,
        in_specs=[smem, smem]
        + [vm] * len(operands),
        out_specs=(vm,) * len(out_shape),
        scratch_shapes=([pltpu.VMEM((2 * inner, tok), BF16)] if last else [])
        + [
            pltpu.VMEM((heads, total, HD), BF16),
            pltpu.VMEM((heads, HD + ONES, total), BF16),
        ],
        cost_estimate=pl.CostEstimate(flops=0, transcendentals=0, bytes_accessed=0),
        compiler_params=pltpu.CompilerParams(vmem_limit_bytes=VMEM_LIMIT),
        name="attention",
    )(length, core[None], *operands)


def grad_kernel(t_ref, core_ref, *refs, tiles, part, step, flip):
    o_refs, cot_refs, g_ref = refs[:tiles], refs[tiles:-1], refs[-1]
    width = cot_refs[0].shape[1]
    dp, pairs, chunk, _ = g_ref.shape
    rows = [
        pl.ds(pl.multiple_of((2 * s + (core_ref[0] ^ flip)) * part, 16), part) for s in range(pairs)
    ]
    left = jnp.concatenate(
        [jnp.concatenate([ref[r, :] for ref in o_refs], axis=1) for r in rows], axis=0
    )
    time = jnp.full((1, step), t_ref[0], jnp.int32).astype(F32)
    weight = 1.0 + 3.0 * (time + 0.5) / 1000.0
    for c in range(0, width, step):
        n = min(step, width - c)
        right = jnp.concatenate([ref[:, c : c + n] for ref in cot_refs], axis=0)
        g = (jnp.dot(left, right, preferred_element_type=F32) * weight[:, :n]).astype(BF16)
        for t in range(n // LANES):
            cols = slice(t * LANES, (t + 1) * LANES)
            for s in range(pairs):
                done = 0
                while done < part:
                    flat = (c // LANES + t) * part + done
                    count = min(part - done, chunk - flat % chunk)
                    g_ref[flat // chunk, s, flat % chunk : flat % chunk + count, :] = g[
                        s * part + done : s * part + done + count, cols
                    ]
                    done += count
    used = width // LANES * part - (dp - 1) * chunk
    if used < chunk:
        for s in range(pairs):
            g_ref[dp - 1, s, used:, :] = jnp.zeros((chunk - used, LANES), BF16)


def local_grad(timestep, core, flip, attended, cots, part, dp):
    inner, tok = attended[0].shape
    width = cots[0].shape[1]
    pairs = inner // (2 * part)
    chunk = -(-(width // LANES * part) // (dp * 16)) * 16
    vm = pl.BlockSpec(memory_space=pltpu.VMEM)
    smem = pl.BlockSpec(memory_space=pltpu.SMEM)
    tiles = len(attended)
    step = 2 * LANES
    return pl.pallas_call(
        functools.partial(grad_kernel, tiles=tiles, part=part, step=step, flip=flip),
        out_shape=jax.ShapeDtypeStruct((dp, pairs, chunk, LANES), BF16),
        in_specs=[smem, smem] + [vm] * (tiles + len(cots)),
        out_specs=vm,
        cost_estimate=pl.CostEstimate(
            flops=tiles * tok * inner * width,
            transcendentals=0,
            bytes_accessed=2 * tiles * tok * (inner + width) + inner * width,
        ),
        compiler_params=pltpu.CompilerParams(vmem_limit_bytes=16 * 2**20),
        name="local_grad",
    )(timestep, core[None], *attended, *cots)


def add_two_kernel(x_ref, y_ref, o_ref):
    o_ref[...] = (x_ref[...].astype(F32) + y_ref[...].astype(F32)).astype(BF16)


def add_two(x, y):
    vm = pl.BlockSpec(memory_space=pltpu.VMEM)
    return pl.pallas_call(
        add_two_kernel,
        out_shape=jax.ShapeDtypeStruct(x.shape, BF16),
        in_specs=[vm, vm],
        out_specs=vm,
        compiler_params=pltpu.CompilerParams(vmem_limit_bytes=SMALL_LIMIT),
        name="add_two",
    )(x, y)


def add_pieces_kernel(x_ref, o_ref, s_ref):
    total = x_ref[0].astype(F32)
    for i in range(1, x_ref.shape[0]):
        total = total + x_ref[i].astype(F32)
    total = total.astype(BF16)
    o_ref[...] = total
    x = total.astype(F32)
    rows = jnp.sum(x * x, axis=0, keepdims=True)
    s_ref[...] = jnp.broadcast_to(jnp.sum(rows, axis=1, keepdims=True), s_ref.shape)


def add_pieces(x, peers):
    vm = pl.BlockSpec(memory_space=pltpu.VMEM)
    return pl.pallas_call(
        add_pieces_kernel,
        out_shape=(
            jax.ShapeDtypeStruct(x.shape[1:], BF16),
            jax.ShapeDtypeStruct((peers, LANES), F32),
        ),
        in_specs=[vm],
        out_specs=(vm, vm),
        compiler_params=pltpu.CompilerParams(vmem_limit_bytes=SMALL_LIMIT),
        name="add_pieces",
    )(x)


def adam_kernel(at_ref, s_ref, *refs):
    g_refs, refs, g_ref = refs[:4], refs[4:-1], refs[-1]
    chunk = g_refs[0].shape[1]
    for k, ref in enumerate(g_refs):
        for i in range(2):
            at = (at_ref[0] ^ i) * 4 + (at_ref[1] + 4 - k) % 4
            rows = pl.ds(pl.multiple_of(at * chunk, chunk), chunk)
            g_ref[rows, :] = ref[i]
    adam_rows(s_ref, g_ref, *refs)


def adam_rows(s_ref, g_ref, w_ref, mv_ref, ms_ref, vv_ref, vs_ref, nw, nmv, nms, nvv, nvs):
    rows, width = w_ref.shape
    squares = jnp.sum(s_ref[...], axis=0, keepdims=True)
    factor = 256.0 / jnp.sqrt(squares + 1e-06)
    diagonal = lax.broadcasted_iota(jnp.int32, (rows, rows), 0) == lax.broadcasted_iota(
        jnp.int32, (rows, rows), 1
    )

    def down(row):
        return jnp.sum(jnp.where(diagonal, row, 0.0), axis=1, keepdims=True)

    def across(column):
        return jnp.sum(jnp.where(diagonal, column, 0.0), axis=0, keepdims=True)

    for t in range(width // LANES):
        cols = slice(t * LANES, (t + 1) * LANES)
        one = slice(t, t + 1)
        g = g_ref[t * rows : (t + 1) * rows, :].astype(F32) * factor
        first = mv_ref[:, cols].astype(F32) * down(ms_ref[one, :])
        second = vv_ref[:, cols].astype(F32) * down(vs_ref[one, :])
        first = 0.9 * first + 0.1 * g
        second = 0.999 * second + 0.001 * g * g
        update = first * (1.0 / (1.0 - 0.9**10)) / (jnp.sqrt(second * (1.0 / (1.0 - 0.999**10))) + 1e-08)
        nw[:, cols] = (w_ref[:, cols].astype(F32) - 0.02 * update).astype(BF16)
        fs = jnp.max(jnp.abs(first), axis=1, keepdims=True) + 1e-06
        ss = jnp.max(jnp.abs(second), axis=1, keepdims=True) + 1e-06
        nms[one, :] = across(fs)
        nvs[one, :] = across(ss)
        nmv[:, cols] = (first * (1.0 / fs)).astype(BF16)
        nvv[:, cols] = (second * (1.0 / ss)).astype(BF16)


def adam(at, squares, grads, out_weight, mom_val, mom_scale, var_val, var_scale):
    vm = pl.BlockSpec(memory_space=pltpu.VMEM)
    like = lambda a: jax.ShapeDtypeStruct(a.shape, a.dtype)
    mom_scale, var_scale = mom_scale.T, var_scale.T
    new_weight, first_val, first_scale, second_val, second_scale = pl.pallas_call(
        adam_kernel,
        out_shape=(like(out_weight), like(mom_val), like(mom_scale), like(var_val), like(var_scale)),
        in_specs=[pl.BlockSpec(memory_space=pltpu.SMEM)] + [vm] * 10,
        out_specs=(vm,) * 5,
        scratch_shapes=[pltpu.VMEM((8 * grads[0].shape[1], LANES), BF16)],
        compiler_params=pltpu.CompilerParams(vmem_limit_bytes=SMALL_LIMIT),
        name="adam",
    )(at, squares, *grads, out_weight, mom_val, mom_scale, var_val, var_scale)
    return new_weight, first_val, first_scale.T, second_val, second_scale.T


def swap(x, axis):
    return lax.ppermute(x, axis, [(0, 1), (1, 0)])


def shift(x, k):
    return lax.ppermute(x, "z", [(i, (i + k) % NT) for i in range(NT)])


def body(
    latent_q,
    latent_k,
    latent_v,
    caption_states,
    caption_proj,
    caption_len,
    timestep,
    out_cot,
    out_weight,
    mom_val,
    mom_scale,
    var_val,
    var_scale,
):
    tok, inner = latent_q.shape[1:]
    cap = caption_states.shape[1]
    xh, z, c = lax.axis_index("xh"), lax.axis_index("z"), lax.axis_index("c")

    keep, send = caption_partial(z, c, caption_proj, caption_states[0])
    other = swap(send, "c")

    group = inner // NT
    staged = stage(z, (latent_k[0], latent_v[0]))
    kvs = [staged[0]] + [shift(staged[k], k) for k in range(1, NT)]
    staged = stage(z, (latent_q[0],), (keep, other))
    queries = [staged[0]] + [shift(staged[k], k) for k in range(1, NT)]
    far_own, far_next = swap(kvs[0], "xh"), swap(kvs[1], "xh")
    held = lax.optimization_barrier((*kvs, *queries, far_own, far_next))
    kvs, queries, far_own, far_next = held[:NT], held[NT : 2 * NT], held[-2], held[-1]

    (ring,), (rest,) = pack(kvs, 2 * group), pack(kvs[2:], 2 * group)
    near, far = swap(ring, "c"), swap(rest, "xh")
    queries, here = pack(queries, group)
    (here,) = pack((here, swap(here, "c")), group)

    cot, queries = lax.optimization_barrier((out_cot[0], queries))
    before, after = shift(cot, 1), shift(cot, -1)
    there, last_own, last_next = swap(here, "xh"), swap(far_own, "c"), swap(far_next, "c")

    (state,) = attention(caption_len, c, queries, [ring, near])
    held = lax.optimization_barrier((state, far, last_own, last_next))
    state, far, last_own, last_next = held
    last = swap(far, "c")
    (state,) = attention(caption_len, c, queries, [far_own, far_next, far], state, block_q=NT * tok)
    state, before, after, there = lax.optimization_barrier((state, before, after, there))
    upper, lower = halves(before, after)
    cots = [cot, before, shift(upper, 1), shift(lower, -1), after]
    kvs = [last_own, last_next, last]
    attended = attention(caption_len, c, queries, kvs, state, (here, there), NT * tok)
    back = [attended[0]] + [shift(attended[k], -k) for k in range(1, NT)]

    rows = out_weight.shape[0]
    dp = lax.axis_size("xl") * lax.axis_size("y")
    other = swap(local_grad(timestep, c, 1, attended, cots, rows, dp), "c")
    grad = local_grad(timestep, c, 0, attended, cots, rows, dp)
    chunk = grad.shape[2]
    grad = add_two(grad, other)
    grad = lax.all_to_all(
        grad.reshape(2 * dp, chunk, LANES), ("xl", "y", "xh"), 0, 0, tiled=True
    )
    grad, *back = lax.optimization_barrier((grad, *back))
    everyone = ("xl", "y", "xh", "z", "c")
    grad, squares = add_pieces(grad, lax.axis_size(everyone))
    pair = []
    for flip in range(2):
        perm = []
        for i in range(4 * NT):
            xl, s, t = i // (2 * NT), i // NT % 2, i % NT
            perm.append((i, (xl ^ flip) * 2 * NT + t // 2 * NT + t % 2 * 2 + s))
        pair.append(lax.ppermute(grad, ("xl", "xh", "z"), perm))
    pair = jnp.stack(pair)
    squares = lax.all_to_all(squares, everyone, 0, 0, tiled=True)
    grads = [pair] + [
        lax.ppermute(pair, "y", [(i, (i + k) % 4) for i in range(4)]) for k in range(1, 4)
    ]
    at = jnp.stack([lax.axis_index("xl"), lax.axis_index("y")])
    attn_out = unstage(z, back)[None]
    updated = adam(at, squares, grads, out_weight, mom_val, mom_scale, var_val, var_scale)
    return (attn_out, *updated)


def solution(mesh):
    fine = Mesh(mesh.devices.reshape(2, 4, 2, NT, 2), ("xl", "y", "xh", "z", "c"))
    dp = ("xl", "y")
    ctx = ("xh", "z", "c")
    tokens = P(dp, ctx, None)
    rows = P(ctx, None)
    return jax.shard_map(
        body,
        mesh=fine,
        in_specs=(
            tokens,
            tokens,
            tokens,
            P(dp, None, ctx),
            rows,
            P(dp),
            P(dp),
            tokens,
            rows,
            rows,
            rows,
            rows,
            rows,
        ),
        out_specs=(tokens, rows, rows, rows, rows, rows),
        check_vma=False,
    )
```
